128 devices in a mesh: img: 16 (over z, y), txt: 8 (over x, core).
Axes of the slice: x: 4, y: 4, z: 4, core: 2. Of those that a mesh axis runs over, the one named last changes fastest.
Arguments:
- image_emb: float32 [16384, 1280], P(('img', 'txt')), may hold values from -8 to 8
- text_emb: float32 [16384, 1280], P(('txt', 'img')), may hold values from -8 to 8
- logit_scale: float32 [], replicated, may hold values from 8 to 12
Outputs:
- loss: float32 [], replicated
- image_grad: float32 [16384, 1280], P(('img', 'txt'))
- text_grad: float32 [16384, 1280], P(('txt', 'img'))
The draws below stay inside these ranges and needn't reach their ends.
All inputs are finite; a program needn't handle non-finite values.
Results may differ from the reference program's by a relative error of at most 0.0003.
Values sent between devices are 32-bit elements; how exact they have to be, the bound alone decides.
A program may use at most 128 MiB of HBM per device.

```python
import math
import jax
import jax.numpy as jnp
from jax import lax

E = 1280
BATCH = 16384


def shared_pair(key):
    first, second = jax.random.split(key, 2)
    positions = jnp.arange(BATCH, dtype=jnp.float32)
    rising = jnp.exp(jnp.log(3.0) * positions / BATCH)[:, None]
    image_base = 0.06 * jax.random.truncated_normal(first, -4.0, 4.0, (BATCH, E), jnp.float32) * rising
    text_base = 0.06 * jax.random.truncated_normal(second, -4.0, 4.0, (BATCH, E), jnp.float32) * rising
    return (image_base, text_base)


def draw_image_emb(key, part):
    image_base, text_base = shared_pair(key)
    return image_base


def draw_text_emb(key, part):
    image_base, text_base = shared_pair(key)
    return text_base


def setup_inputs(seed: int = 0) -> dict:
    seeds = jax.random.split(jax.random.key(seed), 4)
    return {
        "image_emb": draw_image_emb(jax.random.fold_in(seeds[3], 71), 0),
        "text_emb": draw_text_emb(jax.random.fold_in(seeds[3], 71), 0),
        "logit_scale": jnp.clip(jax.random.uniform(seeds[2], (), jnp.float32, 8.0, 12.0), 8.0, 12.0),
    }


def tile_logits(row_block, text_emb, logit_scale):
    return logit_scale * lax.dot_general(row_block, text_emb, (((1,), (1,)), ((), ())), precision=lax.Precision.HIGHEST, preferred_element_type=jnp.float32)


def reference(image_emb, text_emb, logit_scale):
    batch_rows = image_emb.shape[0]
    block_rows = math.gcd(batch_rows, 512)
    block_count = batch_rows // block_rows
    image_blocks = image_emb.reshape(block_count, block_rows, E)

    def first_pass(carry, row_block):
        col_peak, col_total = carry
        block_logits = tile_logits(row_block, text_emb, logit_scale)
        row_peak = jnp.max(block_logits, axis=1)
        row_lse = row_peak + jnp.log(jnp.sum(jnp.exp(block_logits - row_peak[:, None]), axis=1))
        new_peak = jnp.maximum(col_peak, jnp.max(block_logits, axis=0))
        col_total = col_total * jnp.exp(col_peak - new_peak) + jnp.sum(jnp.exp(block_logits - new_peak[None, :]), axis=0)
        return (new_peak, col_total), row_lse

    start_peak = jnp.full((batch_rows,), -jnp.inf, jnp.float32)
    start_total = jnp.zeros((batch_rows,), jnp.float32)
    (col_peak, col_total), row_lse = lax.scan(first_pass, (start_peak, start_total), image_blocks)
    col_lse = col_peak + jnp.log(col_total)
    row_lse = row_lse.reshape(batch_rows)
    diagonal = logit_scale * jnp.sum(image_emb * text_emb, axis=1)
    loss = (jnp.sum(row_lse) + jnp.sum(col_lse) - 2.0 * jnp.sum(diagonal)) / (2.0 * batch_rows)
    columns = jnp.arange(batch_rows, dtype=jnp.int32)

    def second_pass(text_acc, inputs):
        row_block, block_lse, block_index = inputs
        block_logits = tile_logits(row_block, text_emb, logit_scale)
        rows_global = block_index * block_rows + jnp.arange(block_rows, dtype=jnp.int32)
        diagonal_mask = (rows_global[:, None] == columns[None, :]).astype(jnp.float32)
        logit_grad = 0.5 * (jnp.exp(block_logits - block_lse[:, None]) + jnp.exp(block_logits - col_lse[None, :])) - diagonal_mask
        image_part = logit_scale * jnp.dot(logit_grad, text_emb, precision=lax.Precision.HIGHEST, preferred_element_type=jnp.float32)
        text_part = logit_scale * lax.dot_general(logit_grad, row_block, (((0,), (0,)), ((), ())), precision=lax.Precision.HIGHEST, preferred_element_type=jnp.float32)
        return text_acc + text_part, image_part

    block_ids = jnp.arange(block_count, dtype=jnp.int32)
    text_grad, image_parts = lax.scan(second_pass, jnp.zeros((batch_rows, E), jnp.float32), (image_blocks, row_lse.reshape(block_count, block_rows), block_ids))
    image_grad = image_parts.reshape(batch_rows, E)
    return loss, image_grad, text_grad
```

```python
import functools

import jax
import jax.numpy as jnp
from jax import lax
from jax.experimental import pallas as pl
from jax.experimental.pallas import tpu as pltpu
from jax.sharding import PartitionSpec as P

MESH = pl.DeviceIdType.MESH
BF16, F32 = jnp.bfloat16, jnp.float32
LOG2E = 1.4426950408889634
LN2 = 0.6931471805599453

STEP = (0, 1, 3, 2)
ROWS = 128
HALF = ROWS // 2
E = 1280
IMG, TXT = 1024, 2048


def step_of(q):
    return q + q // 2 - 2 * (q // 3)


def dot(a, b, ca, cb):
    return lax.dot_general(a, b, (((ca,), (cb,)), ((), ())), preferred_element_type=F32)


def dot3(ah, al, bh, bl, ca, cb):
    return dot(ah, bh, ca, cb) + (dot(ah, bl, ca, cb) + dot(al, bh, ca, cb))


class Wires:
    def __init__(self, send_sem, recv_sem):
        self.send_sem, self.recv_sem = send_sem, recv_sem
        self.sent, self.n_recv, self.arrivals = [], 0, {}

    def open(self, key, ref, *index):
        self.arrivals[key] = (ref, index, self.n_recv)
        self.n_recv += 1

    def send(self, src, key, dev):
        dst, index, n = self.arrivals[key]
        dst = dst.at[index]
        s = len(self.sent)
        cp = pltpu.make_async_remote_copy(
            src_ref=src,
            dst_ref=dst,
            send_sem=self.send_sem.at[s],
            recv_sem=self.recv_sem.at[n],
            device_id=dev,
            device_id_type=MESH,
        )
        cp.start()
        self.sent.append(dst.shape)

    def wait(self, key):
        dst, index, n = self.arrivals.pop(key)
        dst = dst.at[index]
        pltpu.make_async_copy(dst, dst, self.recv_sem.at[n]).wait()
        return dst

    def flush(self, like):
        for s, shape in enumerate(self.sent):
            ref = like(shape)
            pltpu.make_async_copy(ref, ref, self.send_sem.at[s]).wait()
        self.sent = []


def merge(parts):
    top = functools.reduce(jnp.maximum, [m for m, _ in parts])
    total = sum(s * jnp.exp2(m - top) for m, s in parts)
    return top, total


def kernel(
    scale_ref, img_ref, txt_ref,
    loss_ref, img_out, txt_out,
    Ib, Tb, Ih, Il, Th, Tl, L, Ph, Pl,
    row_m, row_s, rst, cst, acc, lbuf,
    tland, iland, eye,
    send_sem, recv_sem, local_sem,
):
    i, t = lax.axis_index("img"), lax.axis_index("txt")
    x, k = t // 2, t % 2
    z, y = i // 4, i % 4

    def dev(dx=0, dy=0, dz=0, dk=0):
        return (((z + dz) % 4) * 4 + (y + dy) % 4, ((x + dx) % 4) * 2 + (k + dk) % 2)

    sib = dev(dk=1)
    xs = {1: dev(dx=1), -1: dev(dx=3), 2: dev(dx=2)}
    ys = {1: dev(dy=1), -1: dev(dy=3), 2: dev(dy=2)}
    zs = {1: dev(dz=1), -1: dev(dz=3), 2: dev(dz=2)}
    peers = [sib, *xs.values(), *ys.values(), *zs.values()]
    barrier = pltpu.get_barrier_semaphore()
    for peer in peers:
        pl.semaphore_signal(barrier, inc=1, device_id=peer, device_id_type=MESH)
    pl.semaphore_wait(barrier, len(peers))

    w = Wires(send_sem, recv_sem)

    def like(shape):
        if shape[-1] == E:
            return Ib.at[0, pl.ds(0, shape[0])]
        return {2: lbuf, 3: rst if shape[-2] == 8 else cst}[len(shape)].at[0]
    lo, hi = pl.ds(0, HALF), pl.ds(HALF, HALF)

    def T(qz, qy, part):
        return Tb.at[qz * 4 + qy, part]

    for qz in range(4):
        for qy in range(4):
            for name, part, split in (("A", lo, qz == 0 and qy == 3), ("B", hi, qz == 3 and qy == 0)):
                if (qz, qy) == (0, 0):
                    continue
                if split:
                    at = 0 if name == "A" else HALF
                    w.open((name, qz, qy, 0), Tb, qz * 4 + qy, pl.ds(at, 32))
                    w.open((name, qz, qy, 1), Tb, qz * 4 + qy, pl.ds(at + 32, 32))
                else:
                    w.open((name, qz, qy), Tb, qz * 4 + qy, part)
    for q in (1, 2):
        w.open(("I", q), Ib, 2 * q)
    w.open(("I", 3, 0), Ib, 6, lo)
    w.open(("I", 3, 1), Ib, 6, hi)
    for q in range(4):
        w.open(("S", q), Ib, 2 * q + 1)

    own_t = pltpu.make_async_copy(txt_ref, Tb.at[0], local_sem.at[0])
    own_i = pltpu.make_async_copy(img_ref, Ib.at[0], local_sem.at[1])
    w.send(txt_ref.at[lo], ("A", 0, 2), ys[1])
    w.send(txt_ref.at[lo], ("A", 0, 1), ys[-1])
    w.send(txt_ref.at[hi], ("B", 2, 0), zs[1])
    w.send(txt_ref.at[hi], ("B", 1, 0), zs[-1])
    w.send(img_ref, ("I", 2), xs[1])
    w.send(img_ref, ("I", 1), xs[-1])
    w.send(txt_ref.at[lo], ("A", 2, 0), zs[1])
    w.send(txt_ref.at[lo], ("A", 1, 0), zs[-1])
    w.send(txt_ref.at[hi], ("B", 0, 2), ys[1])
    w.send(txt_ref.at[hi], ("B", 0, 1), ys[-1])
    w.send(img_ref, ("S", 0), sib)
    own_t.start()
    own_i.start()

    for q, back in ((2, 1), (1, -1)):
        part = 0 if q == 2 else 1
        src = w.wait(("A", 0, q))
        w.send(T(0, q, pl.ds(32 * part, 32)), ("A", 0, 3, part), ys[back])
        w.send(src, ("A", 2, q), zs[1])
        w.send(src, ("A", 1, q), zs[-1])
        src = w.wait(("B", q, 0))
        w.send(T(q, 0, pl.ds(HALF + 32 * part, 32)), ("B", 3, 0, part), zs[back])
        w.send(src, ("B", q, 2), ys[1])
        w.send(src, ("B", q, 1), ys[-1])
    for q, back in ((2, 1), (1, -1)):
        src = w.wait(("I", q))
        part = 0 if q == 2 else 1
        w.send(Ib.at[2 * q, pl.ds(HALF * part, HALF)], ("I", 3, part), xs[back])
        w.send(src, ("S", q), sib)
    for name, where, a, b in (("A", (0, 3), 2, 1), ("B", (3, 0), 2, 1)):
        w.wait((name, *where, 0))
        w.wait((name, *where, 1))
        if name == "A":
            w.send(T(0, 3, lo), ("A", 2, 3), zs[1])
            w.send(T(0, 3, lo), ("A", 1, 3), zs[-1])
        else:
            w.send(T(3, 0, hi), ("B", 3, 2), ys[1])
            w.send(T(3, 0, hi), ("B", 3, 1), ys[-1])

    def second_ring(q):
        if q in (0, 3):
            w.send(w.wait(("A", 2, q)), ("A", 3, q), zs[1])
            w.send(w.wait(("B", q, 2)), ("B", q, 3), ys[1])
        else:
            w.send(w.wait(("A", 1, q)), ("A", 3, q), zs[-1])
            w.send(w.wait(("B", q, 1)), ("B", q, 3), ys[-1])

    second_ring(0)
    own_i.wait()
    own_t.wait()
    rows_iota = lax.broadcasted_iota(jnp.int32, (ROWS, ROWS), 0)
    cols_iota = lax.broadcasted_iota(jnp.int32, (ROWS, ROWS), 1)
    eye[...] = (rows_iota == cols_iota).astype(F32)
    row_m[...] = jnp.full((IMG, 128), -jnp.inf, F32)
    row_s[...] = jnp.zeros((IMG, 128), F32)

    def split_rows(src, n, high, low, at):
        def body(b, carry):
            r = pl.ds(pl.multiple_of(b * 32, 32), 32)
            o = pl.ds(pl.multiple_of(at + b * 32, 32), 32)
            v = src[n, r, :]
            h = v.astype(BF16)
            high[o, :] = h
            low[o, :] = (v - h.astype(F32)).astype(BF16)
            return carry

        lax.fori_loop(0, ROWS // 32, body, 0)

    w.wait(("S", 0))
    w.wait(("S", 1))
    w.wait(("S", 2))
    w.wait(("I", 3, 0))
    w.wait(("I", 3, 1))
    w.send(Ib.at[6], ("S", 3), sib)
    w.wait(("S", 3))

    def split_img(n, carry):
        split_rows(Ib, n, Ih, Il, n * ROWS)
        return carry

    lax.fori_loop(0, 8, split_img, 0)

    s2 = scale_ref[0] * LOG2E

    def block_of(qz, qy):
        return ((z + step_of(qz)) % 4) * 4 + (y + step_of(qy)) % 4

    def tile(n, carry):
        for m in range(8):

            @pl.when(n == m)
            def _():
                if m in (2, 3, 4):
                    second_ring((0, 0, 1, 2, 3)[m])
                qz, e = m // 2, m % 2
                for qy in (2 * e, 2 * e + 1):
                    for key in list(w.arrivals):
                        if key[0] in "AB" and key[1:3] == (qz, qy):
                            w.wait(key)

        cols = pl.ds(pl.multiple_of(n * 256, 256), 256)
        split_rows(Tb, 2 * n, Th, Tl, n * 256)
        split_rows(Tb, 2 * n + 1, Th, Tl, n * 256 + ROWS)
        L[:, cols] = s2 * dot3(Ih[...], Il[...], Th[cols, :], Tl[cols, :], 1, 1)

        def peak(b, top):
            r = pl.ds(pl.multiple_of(b * ROWS, ROWS), ROWS)
            v = L[r, cols]
            v0, v1 = v[:, :128], v[:, 128:]
            old = row_m[r, :]
            new = jnp.maximum(old, jnp.maximum(v0, v1))
            row_s[r, :] = row_s[r, :] * jnp.exp2(old - new) + (jnp.exp2(v0 - new) + jnp.exp2(v1 - new))
            row_m[r, :] = new
            return jnp.maximum(top, jnp.max(v.reshape(ROWS // 8, 8, 256), axis=0))

        top = lax.fori_loop(0, 8, peak, jnp.full((8, 256), -jnp.inf, F32))

        def total(b, s):
            r = pl.ds(pl.multiple_of(b * ROWS, ROWS), ROWS)
            v = L[r, cols].reshape(ROWS // 8, 8, 256)
            return s + jnp.sum(jnp.exp2(v - top[None]), axis=0)

        s8 = lax.fori_loop(0, 8, total, jnp.zeros((8, 256), F32))
        m1 = jnp.max(top, axis=0, keepdims=True)
        s1 = jnp.sum(s8 * jnp.exp2(top - m1), axis=0, keepdims=True)
        qz, e = n // 2, n % 2
        for j in range(2):
            at = pl.ds(block_of(qz, 2 * e + j), 1)
            cst[0, 0, at, :] = m1[:, 128 * j : 128 * j + 128]
            cst[0, 1, at, :] = s1[:, 128 * j : 128 * j + 128]
        return carry

    lax.fori_loop(0, 8, tile, 0)

    def img_block(s):
        return ((x + step_of(s // 2)) % 4) * 2 + (k + s % 2) % 2

    def fold_rows(s, carry):
        r = pl.ds(pl.multiple_of(s * ROWS, ROWS), ROWS)
        mt, st = row_m[r, :].T, row_s[r, :].T
        m1 = jnp.max(mt, axis=0, keepdims=True)
        s1 = jnp.sum(st * jnp.exp2(mt - m1), axis=0, keepdims=True)
        at = pl.ds(img_block(s), 1)
        rst[0, 0, at, :] = m1
        rst[0, 1, at, :] = s1
        return carry

    lax.fori_loop(0, 8, fold_rows, 0)
    w.flush(like)
    assert not w.arrivals

    w.open("r1", rst, 1)
    for n, d in enumerate((1, -1, 2)):
        w.open(("c1", d), cst, 1 + n)
        w.open(("r2", d), rst, 3 + n)
        w.open(("c2", d), cst, 5 + n)
    w.send(rst.at[0], "r1", sib)
    for d in (1, -1, 2):
        w.send(cst.at[0], ("c1", d), ys[d])
    w.wait("r1")
    m, s = merge([(rst[n, 0], rst[n, 1]) for n in (0, 1)])
    rst[2, 0], rst[2, 1] = m, s
    for d in (1, -1, 2):
        w.send(rst.at[2], ("r2", d), xs[d])
    for d in (1, -1, 2):
        w.wait(("c1", d))
    m, s = merge([(cst[n, 0], cst[n, 1]) for n in range(4)])
    cst[4, 0], cst[4, 1] = m, s
    for d in (1, -1, 2):
        w.send(cst.at[4], ("c2", d), zs[d])
    for d in (1, -1, 2):
        w.wait(("r2", d))
    m, s = merge([(rst[n, 0], rst[n, 1]) for n in range(2, 6)])
    row_lse = m + jnp.log2(s)
    for d in (1, -1, 2):
        w.wait(("c2", d))
    m, s = merge([(cst[n, 0], cst[n, 1]) for n in range(4, 8)])
    col_lse = m + jnp.log2(s)
    w.flush(like)
    rst[6, 0] = row_lse + 1.0
    cst[8, 0] = col_lse + 1.0
    acc[...] = jnp.full((8, 128), LN2 * (jnp.sum(row_lse) / 8 + jnp.sum(col_lse) / 16), F32)

    def spread(s, carry):
        r = pl.ds(pl.multiple_of(s * ROWS, ROWS), ROWS)
        v = rst[6, 0, pl.ds(img_block(s), 1), :]
        row_m[r, :] = jnp.broadcast_to(v, (ROWS, 128)).T
        return carry

    lax.fori_loop(0, 8, spread, 0)

    for q in range(4):
        w.open(("AP", q), tland, q)
        w.open(("BP", q), tland, 4 + q)
        for n, d in enumerate((1, -1)):
            w.open(("AD", q, d), Ib, q, pl.ds(HALF * n, HALF))
            w.open(("BD", q, d), Ib, 4 + q, pl.ds(HALF * n, HALF))
    for n, d in enumerate((1, -1)):
        w.open(("A2", d), tland, 8 + n)
        w.open(("B2", d), tland, 10 + n)
        w.open(("A2P", d), tland, 12, pl.ds(32 * n, 32))
        w.open(("B2P", d), tland, 13, pl.ds(32 * n, 32))
        w.open(("ID", d), iland, 4 + n)
        w.open(("IP", d), iland, 6, pl.ds(HALF * n, HALF))
    for q in range(4):
        w.open(("IS", q), iland, q)
    w.open("ls", lbuf, 1)
    for n, d in enumerate((1, -1, 2)):
        w.open(("lx", d), lbuf, 3 + n)
        w.open(("ly", d), lbuf, 7 + n)
        w.open(("lz", d), lbuf, 11 + n)

    def add(dst, srcs, rows, out=None, mul=None):
        step = 16

        def body(b, carry):
            r = pl.ds(pl.multiple_of(b * step, step), step)
            v = dst[r, :]
            for src in srcs:
                v = v + src[r, :]
            if out is None:
                dst[r, :] = v
            else:
                out[r, :] = mul * v
            return carry

        lax.fori_loop(0, rows // step, body, 0)

    def TA(qz, qy):
        return Tb.at[qz * 4 + qy, lo]

    def TB(qz, qy):
        return Tb.at[qz * 4 + qy, hi]

    def first_ring(name, q1, q2):
        nbr = zs if name == "A" else ys
        ref = TA(q1, q2) if name == "A" else TB(q2, q1)
        plus = q2 in (0, 3)
        if q1 == 3:
            if plus:
                w.send(ref, (name + "P", q2), nbr[-1])
            else:
                w.send(ref, (name + "P", q2), nbr[1])
        elif q1 == 2:
            if plus:
                add(ref, [w.wait((name + "P", q2))], HALF)
            w.send(ref, (name + "D", q2, 1), nbr[-1])
        elif q1 == 1:
            if not plus:
                add(ref, [w.wait((name + "P", q2))], HALF)
            w.send(ref, (name + "D", q2, -1), nbr[1])

    def second(name, q2):
        nbr = ys if name == "A" else zs
        ref = TA(0, q2) if name == "A" else TB(q2, 0)
        add(ref, [w.wait((name + "D", q2, 1)), w.wait((name + "D", q2, -1))], HALF)
        if q2 == 3:
            w.send(ref.at[pl.ds(0, 32)], (name + "2P", 1), nbr[-1])
            w.send(ref.at[pl.ds(32, 32)], (name + "2P", -1), nbr[1])
        elif q2 == 2:
            add(ref.at[pl.ds(0, 32)], [w.wait((name + "2P", 1))], 32)
            w.send(ref, (name + "2", 1), nbr[-1])
        elif q2 == 1:
            add(ref.at[pl.ds(32, 32)], [w.wait((name + "2P", -1))], 32)
            w.send(ref, (name + "2", -1), nbr[1])
        else:
            at = lo if name == "A" else hi
            srcs = [w.wait((name + "2", 1)), w.wait((name + "2", -1))]
            add(ref, srcs, HALF, txt_out.at[at], scale_ref[0])

    def text_events(n):
        if n == 1:
            for q in (3, 0, 1, 2):
                first_ring("A", 3, q)
            first_ring("B", 3, 3)
            first_ring("B", 1, 3)
        if n == 3:
            for q in (1, 2):
                first_ring("A", 2, q)
            first_ring("B", 3, 2)
            first_ring("B", 2, 2)
            first_ring("B", 2, 3)
        if n == 5:
            for q in (3, 0):
                first_ring("A", 1, q)
            first_ring("B", 3, 1)
            first_ring("B", 2, 1)
            first_ring("A", 2, 3)
            first_ring("A", 2, 0)
            first_ring("A", 1, 1)
            first_ring("A", 1, 2)
            first_ring("B", 1, 2)
        if n == 7:
            first_ring("B", 3, 0)
            first_ring("B", 1, 0)
            first_ring("B", 1, 1)
            second("B", 3)

    dsum = jnp.zeros((8, 128), F32)
    lbuf[0] = dsum

    def text_step(n, carry):
        p = 7 - n
        qz, e = p // 2, p % 2
        cols = pl.ds(pl.multiple_of(p * 256, 256), 256)
        blocks = [block_of(qz, 2 * e + j) for j in range(2)]
        cl = jnp.concatenate([cst[8, 0, pl.ds(b, 1), :] for b in blocks], axis=1)

        def soft(b, inner):
            r = pl.ds(pl.multiple_of(b * 64, 64), 64)
            v = L[r, cols]
            rl = row_m[r, :]
            g = jnp.exp2(v - jnp.concatenate([rl, rl], axis=1)) + jnp.exp2(v - cl)
            h = g.astype(BF16)
            Ph[r, cols] = h
            Pl[r, cols] = (g - h.astype(F32)).astype(BF16)
            return inner

        lax.fori_loop(0, IMG // 64, soft, 0)
        for j in range(2):
            there = t * 16 + blocks[j] - i * 8

            @pl.when((there >= 0) & (there < 8))
            def _():
                d = (there // 2 + 4 - x) % 4
                s = step_of(d) * 2 + (there % 2 + k) % 2
                r = pl.ds(pl.multiple_of(s * ROWS, ROWS), ROWS)
                c = pl.ds(pl.multiple_of(p * 256 + j * 128, 128), 128)
                v = L[r, c]
                g = jnp.exp2(v - row_m[r, :]) + jnp.exp2(v - cl[:, 128 * j : 128 * j + 128]) - eye[...]
                h = g.astype(BF16)
                Ph[r, c] = h
                Pl[r, c] = (g - h.astype(F32)).astype(BF16)
                lbuf[0] += jnp.sum((v * eye[...]).reshape(ROWS // 8, 8, 128), axis=0)

        res = dot3(Ph[:, cols], Pl[:, cols], Ih[...], Il[...], 0, 0)
        Tb[2 * p] = res[:ROWS]
        Tb[2 * p + 1] = res[ROWS:]
        for m in range(8):

            @pl.when(n == m)
            def _():
                text_events(m)

        return carry

    lax.fori_loop(0, 8, text_step, 0)
    total = jnp.sum(acc[...]) / 1024 - 2.0 * LN2 * jnp.sum(lbuf[0])
    lbuf[0] = jnp.full((8, 128), total, F32)
    w.send(lbuf.at[0], "ls", sib)

    def iref(s):
        return L.at[pl.ds(s * ROWS, ROWS), pl.ds(0, E)]

    def image_events(m):
        q = 3 - m
        w.send(iref(2 * q + 1), ("IS", q), sib)
        if m == 0:
            first_ring("B", 2, 0)
            second("B", 2)
            second("A", 3)
        if m == 1:
            second("B", 1)
            second("A", 2)
            second("A", 1)
        mine = iref(2 * q)
        add(mine, [w.wait(("IS", q))], ROWS)
        if m == 0:
            w.send(mine.at[lo], ("IP", 1), xs[-1])
            w.send(mine.at[hi], ("IP", -1), xs[1])
        elif m == 1:
            add(mine.at[lo], [w.wait(("IP", 1))], HALF)
            w.send(mine, ("ID", 1), xs[-1])
        elif m == 2:
            add(mine.at[hi], [w.wait(("IP", -1))], HALF)
            w.send(mine, ("ID", -1), xs[1])
        if m == 0:
            w.wait("ls")
            lbuf[2] = lbuf[0] + lbuf[1]
            for d in (1, -1, 2):
                w.send(lbuf.at[2], ("lx", d), xs[d])
        elif m < 3:
            a, b, nbr, base = (("lx", "ly", ys, 2), ("ly", "lz", zs, 6))[m - 1]
            for d in (1, -1, 2):
                w.wait((a, d))
            lbuf[base + 4] = (lbuf[base] + lbuf[base + 1]) + (lbuf[base + 2] + lbuf[base + 3])
            for d in (1, -1, 2):
                w.send(lbuf.at[base + 4], (b, d), nbr[d])

    def image_step(m, carry):
        r = pl.ds(pl.multiple_of((3 - m) * 256, 256), 256)
        L[r, 0:E] = dot3(Ph[r, :], Pl[r, :], Th[...], Tl[...], 1, 0)
        for n in range(4):

            @pl.when(m == n)
            def _():
                image_events(n)

        return carry

    lax.fori_loop(0, 4, image_step, 0)
    second("A", 0)
    second("B", 0)
    add(iref(0), [w.wait(("ID", 1)), w.wait(("ID", -1))], ROWS, img_out, scale_ref[0])
    for d in (1, -1, 2):
        w.wait(("lz", d))
    loss_ref[...] = ((lbuf[10] + lbuf[11]) + (lbuf[12] + lbuf[13])) / (2.0 * 16384)
    w.flush(like)
    assert not w.arrivals


def on_device(image_emb, text_emb, logit_scale):
    vm = pltpu.VMEM
    loss, image_grad, text_grad = pl.pallas_call(
        kernel,
        out_shape=(
            jax.ShapeDtypeStruct((8, 128), F32),
            jax.ShapeDtypeStruct((ROWS, E), F32),
            jax.ShapeDtypeStruct((ROWS, E), F32),
        ),
        in_specs=[
            pl.BlockSpec(memory_space=pltpu.SMEM),
            pl.BlockSpec(memory_space=pl.ANY),
            pl.BlockSpec(memory_space=pl.ANY),
        ],
        out_specs=[pl.BlockSpec(memory_space=vm)] * 3,
        scratch_shapes=[
            vm((8, ROWS, E), F32),
            vm((16, ROWS, E), F32),
            vm((IMG, E), BF16),
            vm((IMG, E), BF16),
            vm((TXT, E), BF16),
            vm((TXT, E), BF16),
            vm((IMG, TXT), F32),
            vm((IMG, TXT), BF16),
            vm((IMG, TXT), BF16),
            vm((IMG, 128), F32),
            vm((IMG, 128), F32),
            vm((7, 2, 8, 128), F32),
            vm((9, 2, 16, 128), F32),
            vm((8, 128), F32),
            vm((14, 8, 128), F32),
            vm((14, HALF, E), F32),
            vm((7, ROWS, E), F32),
            vm((ROWS, ROWS), F32),
            pltpu.SemaphoreType.DMA((56,)),
            pltpu.SemaphoreType.DMA((112,)),
            pltpu.SemaphoreType.DMA((2,)),
        ],
        compiler_params=pltpu.CompilerParams(
            collective_id=0, has_side_effects=True, vmem_limit_bytes=63 * 2**20
        ),
        name="contrastive",
    )(logit_scale.reshape(1), image_emb, text_emb)
    return loss[0, 0], image_grad, text_grad


def solution(mesh):
    in_specs = (P(("img", "txt"), None), P(("txt", "img"), None), P())
    out_specs = (P(), P(("img", "txt"), None), P(("txt", "img"), None))
    return jax.shard_map(
        on_device, mesh=mesh, in_specs=in_specs, out_specs=out_specs, check_vma=False
    )
```

```python
import functools

import jax
import jax.numpy as jnp
from jax import lax
from jax.experimental import pallas as pl
from jax.experimental.pallas import tpu as pltpu
from jax.sharding import PartitionSpec as P

MESH = pl.DeviceIdType.MESH
BF16, F32 = jnp.bfloat16, jnp.float32
LOG2E = 1.4426950408889634
LN2 = 0.6931471805599453

STEP = (0, 1, 3, 2)
ROWS = 128
HALF = ROWS // 2
E = 1280
IMG, TXT = 1024, 2048


PAIRS = (
    ((0, 1), (0, 2)), ((1, 0), (2, 0)), ((1, 2), (0, 0)), ((0, 3), (1, 1)),
    ((3, 0), (2, 3)), ((1, 3), (2, 1)), ((3, 2), (2, 2)), ((3, 3), (3, 1)),
)
SLOT = {where: 2 * n + j for n, pair in enumerate(PAIRS) for j, where in enumerate(pair)}

GATHER = (
    (("B", 1, 0), ("B", 2, 0), ("A", 0, 2), ("A", 0, 1), ("I", 1), ("I", 2), ("S", 0),
     ("A", 2, 0), ("B", 0, 2), ("B", 0, 1), ("A", 1, 0)),
    (("A", 1, 1), ("A", 0, 3, 1), ("B", 3, 0, 0), ("B", 1, 2), ("B", 2, 1), ("A", 2, 1), ("B", 3, 0, 1),
     ("A", 0, 3, 0), ("I", 3, 0), ("S", 1), ("S", 2), ("I", 3, 1), ("A", 3, 0), ("B", 0, 3), ("B", 1, 1), ("A", 1, 2)),
    (),
    (("S", 3), ("A", 1, 3), ("A", 2, 3), ("B", 3, 2), ("B", 2, 3)),
    (), (),
    (("B", 1, 3), ("A", 3, 2), ("B", 2, 2), ("A", 2, 2)),
    (),
    (("A", 3, 3), ("B", 3, 1), ("B", 3, 3), ("A", 3, 1)),
    (), (), (), (),
)

STEPS = (("t", 0), ("t", 1), ("t", 2), ("t", 3), ("t", 4), ("t", 5),
         ("i", 3), ("i", 2), ("i", 1), ("t", 6), ("t", 7), ("i", 0))
RETURN = (
    (("B", "P", 3), ("A", "P", 3), ("A", "P", 1), ("B", "D", 3, -1)),
    (("A", "P", 2), ("B", "D", 2, 1), ("A", "D", 2, 1)),
    (("B", "P", 1), ("B", "D", 3, 1), ("A", "D", 3, -1), ("A", "D", 1, 1)),
    (("B", "P", 2),),
    (),
    (("A", "D", 3, 1), ("B", "P", 0), ("A", "D", 2, -1)),
    (("IS", 3), ("B", "D", 1, 1), ("B", "D", 1, -1), ("A", "P", 0), ("A", "D", 1, -1)),
    (("IP", 1), ("IP", -1), ("IS", 2), ("B", "D", 2, -1)),
    (("IS", 1), ("B", "2P", 1), ("B", "2P", -1), ("A", "2P", 1), ("A", "2P", -1)),
    (("A", "D", 0, -1),),
    (("ID", 1), ("ID", -1), ("B", "D", 0, 1), ("B", "D", 0, -1), ("B", "2", 1), ("B", "2", -1),
     ("A", "2", 1), ("A", "D", 0, 1)),
    (("A", "2", -1), ("IS", 0), ("B", "F"), ("IF",), ("A", "F")),
)


def pick(n, values):
    return sum(jnp.where(n == j, v, 0) for j, v in enumerate(values))


def dot(a, b, ca, cb):
    return lax.dot_general(a, b, (((ca,), (cb,)), ((), ())), preferred_element_type=F32)


def dot3(ah, al, bh, bl, ca, cb):
    return dot(ah, bh, ca, cb) + (dot(ah, bl, ca, cb) + dot(al, bh, ca, cb))


class Wires:
    def __init__(self, send_sem, recv_sem):
        self.send_sem, self.recv_sem = send_sem, recv_sem
        self.sent, self.n_recv, self.arrivals = [], 0, {}

    def open(self, key, ref, *index):
        self.arrivals[key] = (ref, index, self.n_recv)
        self.n_recv += 1

    def send(self, src, key, dev):
        dst, index, n = self.arrivals[key]
        dst = dst.at[index]
        s = len(self.sent)
        cp = pltpu.make_async_remote_copy(
            src_ref=src,
            dst_ref=dst,
            send_sem=self.send_sem.at[s],
            recv_sem=self.recv_sem.at[n],
            device_id=dev,
            device_id_type=MESH,
        )
        cp.start()
        self.sent.append(dst.shape)

    def wait(self, key):
        dst, index, n = self.arrivals.pop(key)
        dst = dst.at[index]
        pltpu.make_async_copy(dst, dst, self.recv_sem.at[n]).wait()
        return dst

    def need(self, *keys):
        for key in keys:
            if key in self.arrivals:
                self.wait(key)

    def flush(self, like):
        for s, shape in enumerate(self.sent):
            ref = like(shape)
            pltpu.make_async_copy(ref, ref, self.send_sem.at[s]).wait()
        self.sent = []


def merge(parts):
    top = functools.reduce(jnp.maximum, [m for m, _ in parts])
    total = sum(s * jnp.exp2(m - top) for m, s in parts)
    return top, total


def kernel(
    scale_ref, img_ref, txt_ref,
    loss_ref, img_out, txt_out,
    Ib, Tb, Ih, Il, Th, Tl, L, Ph, Pl,
    row_m, row_s, rst, cst, acc, lbuf,
    tland, iland, eye,
    send_sem, recv_sem, local_sem,
):
    i, t = lax.axis_index("img"), lax.axis_index("txt")
    x, k = t // 2, t % 2
    z, y = i // 4, i % 4

    def dev(dx=0, dy=0, dz=0, dk=0):
        return (((z + dz) % 4) * 4 + (y + dy) % 4, ((x + dx) % 4) * 2 + (k + dk) % 2)

    sib = dev(dk=1)
    xs = {1: dev(dx=1), -1: dev(dx=3), 2: dev(dx=2)}
    ys = {1: dev(dy=1), -1: dev(dy=3), 2: dev(dy=2)}
    zs = {1: dev(dz=1), -1: dev(dz=3), 2: dev(dz=2)}
    peers = [sib, *xs.values(), *ys.values(), *zs.values()]
    barrier = pltpu.get_barrier_semaphore()
    for peer in peers:
        pl.semaphore_signal(barrier, inc=1, device_id=peer, device_id_type=MESH)
    pl.semaphore_wait(barrier, len(peers))

    w = Wires(send_sem, recv_sem)

    def like(shape):
        if shape[-1] == E:
            return Ib.at[0, pl.ds(0, shape[0])]
        return {2: lbuf, 3: rst if shape[-2] == 8 else cst}[len(shape)].at[0]
    lo, hi = pl.ds(0, HALF), pl.ds(HALF, HALF)

    def T(qz, qy, part):
        return Tb.at[SLOT[qz, qy], part]

    for qz in range(4):
        for qy in range(4):
            for name, part, split in (("A", lo, qz == 0 and qy == 3), ("B", hi, qz == 3 and qy == 0)):
                if (qz, qy) == (0, 0):
                    continue
                if split:
                    at = 0 if name == "A" else HALF
                    w.open((name, qz, qy, 0), Tb, SLOT[qz, qy], pl.ds(at, 32))
                    w.open((name, qz, qy, 1), Tb, SLOT[qz, qy], pl.ds(at + 32, 32))
                else:
                    w.open((name, qz, qy), Tb, SLOT[qz, qy], part)
    for q in (1, 2):
        w.open(("I", q), Ib, 2 * q)
    w.open(("I", 3, 0), Ib, 6, lo)
    w.open(("I", 3, 1), Ib, 6, hi)
    for q in range(4):
        w.open(("S", q), Ib, 2 * q + 1)

    def text_keys(qz, qy):
        return [(n, qz, qy, *h) for n in "AB" for h in ((), (0,), (1,))]

    def gather_send(key):
        name, first = key[0], key[1]
        if name == "S":
            q = first
            w.need(("I", q), ("I", 3, 0), ("I", 3, 1)) if q == 3 else w.need(("I", q))
            w.send(img_ref if q == 0 else Ib.at[2 * q], key, sib)
        elif name == "I":
            if len(key) == 2:
                w.send(img_ref, key, xs[1 if first == 2 else -1])
            else:
                q = 2 - key[2]
                w.need(("I", q))
                w.send(Ib.at[2 * q, (lo, hi)[key[2]]], key, xs[1 - 2 * key[2]])
        else:
            q1, q2 = (key[2], key[1]) if name == "A" else (key[1], key[2])
            ring1, ring2 = (ys, zs) if name == "A" else (zs, ys)
            at = 0 if name == "A" else HALF

            def where(a, b):
                return (b, a) if name == "A" else (a, b)

            if len(key) == 4:
                q = 2 - key[3]
                w.need((name, *where(q, 0)))
                w.send(T(*where(q, 0), pl.ds(at + 32 * key[3], 32)), key, ring1[1 - 2 * key[3]])
            elif q2 == 0:
                w.send(txt_ref.at[pl.ds(at, HALF)], key, ring1[1 if q1 == 2 else -1])
            else:
                if q2 == 3:
                    q, d = (2, 1) if q1 in (0, 3) else (1, -1)
                else:
                    q, d = 0, (1 if q2 == 2 else -1)
                source = where(q1, q)
                if source == (0, 0):
                    w.send(txt_ref.at[pl.ds(at, HALF)], key, ring2[d])
                else:
                    w.need(*[k for k in text_keys(*source) if k[0] == name])
                    w.send(T(*source, pl.ds(at, HALF)), key, ring2[d])

    own_t = pltpu.make_async_copy(txt_ref, Tb.at[SLOT[0, 0]], local_sem.at[0])
    own_i = pltpu.make_async_copy(img_ref, Ib.at[0], local_sem.at[1])
    for key in GATHER[0]:
        gather_send(key)
    own_t.start()
    own_i.start()

    rows_iota = lax.broadcasted_iota(jnp.int32, (ROWS, ROWS), 0)
    cols_iota = lax.broadcasted_iota(jnp.int32, (ROWS, ROWS), 1)
    eye[...] = (rows_iota == cols_iota).astype(F32)
    row_m[...] = jnp.full((IMG, 128), -jnp.inf, F32)
    row_s[...] = jnp.zeros((IMG, 128), F32)

    def split_rows(src, n, high, low, at):
        def body(b, carry):
            r = pl.ds(pl.multiple_of(b * 32, 32), 32)
            o = pl.ds(pl.multiple_of(at + b * 32, 32), 32)
            v = src[n, r, :]
            h = v.astype(BF16)
            high[o, :] = h
            low[o, :] = (v - h.astype(F32)).astype(BF16)
            return carry

        lax.fori_loop(0, ROWS // 32, body, 0)

    own_i.wait()
    for q in range(4):
        if q > 0:
            for key in GATHER[q]:
                gather_send(key)
        w.need(("I", q), ("S", q), *([("I", 3, 0), ("I", 3, 1)] if q == 3 else []))
        split_rows(Ib, 2 * q, Ih, Il, 2 * q * ROWS)
        split_rows(Ib, 2 * q + 1, Ih, Il, (2 * q + 1) * ROWS)
    own_t.wait()

    s2 = scale_ref[0] * LOG2E
    held = [((z + STEP[qz]) % 4) * 4 + (y + STEP[qy]) % 4 for pair in PAIRS for qz, qy in pair]

    def blocks_of(n):
        return [pick(n, held[j::2]) for j in range(2)]

    def tile(n, carry):
        for m in range(8):

            @pl.when(n == m)
            def _():
                for key in GATHER[4 + m]:
                    gather_send(key)
                for where in PAIRS[m]:
                    w.need(*text_keys(*where))

        cols = pl.ds(pl.multiple_of(n * 256, 256), 256)
        split_rows(Tb, 2 * n, Th, Tl, n * 256)
        split_rows(Tb, 2 * n + 1, Th, Tl, n * 256 + ROWS)
        L[:, cols] = s2 * dot3(Ih[...], Il[...], Th[cols, :], Tl[cols, :], 1, 1)

        def peak(b, top):
            r = pl.ds(pl.multiple_of(b * ROWS, ROWS), ROWS)
            v = L[r, cols]
            v0, v1 = v[:, :128], v[:, 128:]
            old = row_m[r, :]
            new = jnp.maximum(old, jnp.maximum(v0, v1))
            row_s[r, :] = row_s[r, :] * jnp.exp2(old - new) + (jnp.exp2(v0 - new) + jnp.exp2(v1 - new))
            row_m[r, :] = new
            return jnp.maximum(top, jnp.max(v.reshape(ROWS // 8, 8, 256), axis=0))

        top = lax.fori_loop(0, 8, peak, jnp.full((8, 256), -jnp.inf, F32))

        def total(b, s):
            r = pl.ds(pl.multiple_of(b * ROWS, ROWS), ROWS)
            v = L[r, cols].reshape(ROWS // 8, 8, 256)
            return s + jnp.sum(jnp.exp2(v - top[None]), axis=0)

        s8 = lax.fori_loop(0, 8, total, jnp.zeros((8, 256), F32))
        m1 = jnp.max(top, axis=0, keepdims=True)
        s1 = jnp.sum(s8 * jnp.exp2(top - m1), axis=0, keepdims=True)
        for j, block in enumerate(blocks_of(n)):
            at = pl.ds(block, 1)
            cst[0, 0, at, :] = m1[:, 128 * j : 128 * j + 128]
            cst[0, 1, at, :] = s1[:, 128 * j : 128 * j + 128]
        return carry

    lax.fori_loop(0, 8, tile, 0)

    def step_of(q):
        return q + q // 2 - 2 * (q // 3)

    def img_block(s):
        return ((x + step_of(s // 2)) % 4) * 2 + (k + s % 2) % 2

    def fold_rows(s, carry):
        r = pl.ds(pl.multiple_of(s * ROWS, ROWS), ROWS)
        mt, st = row_m[r, :].T, row_s[r, :].T
        m1 = jnp.max(mt, axis=0, keepdims=True)
        s1 = jnp.sum(st * jnp.exp2(mt - m1), axis=0, keepdims=True)
        at = pl.ds(img_block(s), 1)
        rst[0, 0, at, :] = m1
        rst[0, 1, at, :] = s1
        return carry

    lax.fori_loop(0, 8, fold_rows, 0)
    w.flush(like)
    assert not w.arrivals

    w.open("r1", rst, 1)
    for n, d in enumerate((1, -1, 2)):
        w.open(("c1", d), cst, 1 + n)
        w.open(("r2", d), rst, 3 + n)
        w.open(("c2", d), cst, 5 + n)
    w.send(rst.at[0], "r1", sib)
    for d in (1, -1, 2):
        w.send(cst.at[0], ("c1", d), ys[d])
    w.wait("r1")
    m, s = merge([(rst[n, 0], rst[n, 1]) for n in (0, 1)])
    rst[2, 0], rst[2, 1] = m, s
    for d in (1, -1, 2):
        w.send(rst.at[2], ("r2", d), xs[d])
    for d in (1, -1, 2):
        w.wait(("c1", d))
    m, s = merge([(cst[n, 0], cst[n, 1]) for n in range(4)])
    cst[4, 0], cst[4, 1] = m, s
    for d in (1, -1, 2):
        w.send(cst.at[4], ("c2", d), zs[d])
    for d in (1, -1, 2):
        w.wait(("r2", d))
    m, s = merge([(rst[n, 0], rst[n, 1]) for n in range(2, 6)])
    row_lse = m + jnp.log2(s)
    for d in (1, -1, 2):
        w.wait(("c2", d))
    m, s = merge([(cst[n, 0], cst[n, 1]) for n in range(4, 8)])
    col_lse = m + jnp.log2(s)
    w.flush(like)
    rst[6, 0] = row_lse + 1.0
    cst[8, 0] = col_lse + 1.0
    acc[...] = jnp.full((8, 128), LN2 * (jnp.sum(row_lse) / 8 + jnp.sum(col_lse) / 16), F32)

    def spread(s, carry):
        r = pl.ds(pl.multiple_of(s * ROWS, ROWS), ROWS)
        v = rst[6, 0, pl.ds(img_block(s), 1), :]
        row_m[r, :] = jnp.broadcast_to(v, (ROWS, 128)).T
        return carry

    lax.fori_loop(0, 8, spread, 0)

    for base, name in enumerate("AB"):
        for q in range(4):
            w.open((name, "P", q), tland, 4 * base + q)
            for n, d in enumerate((1, -1)):
                w.open((name, "D", q, d), Ib, 4 * base + q, pl.ds(HALF * n, HALF))
        for n, d in enumerate((1, -1)):
            w.open((name, "2", d), tland, 8 + 2 * base + n)
            w.open((name, "2P", d), tland, 12 + base, pl.ds(32 * n, 32))
    for n, d in enumerate((1, -1)):
        w.open(("ID", d), iland, 4 + n)
        w.open(("IP", d), iland, 6, pl.ds(HALF * n, HALF))
    for q in range(4):
        w.open(("IS", q), iland, q)
    w.open("ls", lbuf, 1)
    for n, d in enumerate((1, -1, 2)):
        w.open(("lx", d), lbuf, 3 + n)
        w.open(("ly", d), lbuf, 7 + n)
        w.open(("lz", d), lbuf, 11 + n)

    def add(dst, srcs, rows, out=None, mul=None):
        step = 16

        def body(b, carry):
            r = pl.ds(pl.multiple_of(b * step, step), step)
            v = dst[r, :]
            for src in srcs:
                v = v + src[r, :]
            if out is None:
                dst[r, :] = v
            else:
                out[r, :] = mul * v
            return carry

        lax.fori_loop(0, rows // step, body, 0)

    summed = set()

    def text_send(key):
        name, kind = key[0], key[1]
        ring1, ring2 = (zs, ys) if name == "A" else (ys, zs)
        part = lo if name == "A" else hi

        def ref(q1, q2, rows=None):
            qz, qy = (q1, q2) if name == "A" else (q2, q1)
            at = (0 if name == "A" else HALF) + (rows or 0)
            return Tb.at[SLOT[qz, qy], pl.ds(at, HALF if rows is None else 32)]

        def first_sum(q2):
            if (name, q2) not in summed:
                summed.add((name, q2))
                add(ref(0, q2), [w.wait((name, "D", q2, 1)), w.wait((name, "D", q2, -1))], HALF)

        if kind == "P":
            q2 = key[2]
            w.send(ref(3, q2), key, ring1[-1 if q2 in (0, 3) else 1])
        elif kind == "D":
            q2, d = key[2], key[3]
            mine = ref(2 if d == 1 else 1, q2)
            if (d == 1) == (q2 in (0, 3)):
                add(mine, [w.wait((name, "P", q2))], HALF)
            w.send(mine, key, ring1[-d])
        elif kind == "2P":
            d = key[2]
            first_sum(3)
            w.send(ref(0, 3, 0 if d == 1 else 32), key, ring2[-d])
        elif kind == "2":
            d = key[2]
            q2 = 2 if d == 1 else 1
            first_sum(q2)
            add(ref(0, q2, 0 if d == 1 else 32), [w.wait((name, "2P", d))], 32)
            w.send(ref(0, q2), key, ring2[-d])
        else:
            srcs = [w.wait((name, "D", 0, 1)), w.wait((name, "D", 0, -1)), w.wait((name, "2", 1)), w.wait((name, "2", -1))]
            add(ref(0, 0), srcs, HALF, txt_out.at[part], scale_ref[0])

    def iref(s):
        return L.at[pl.ds(s * ROWS, ROWS), pl.ds(0, E)]

    def image_send(key):
        kind = key[0]
        if kind == "IS":
            w.send(iref(2 * key[1] + 1), key, sib)
        elif kind == "IP":
            if "i3" not in summed:
                summed.add("i3")
                add(iref(6), [w.wait(("IS", 3))], ROWS)
            w.send(iref(6).at[lo if key[1] == 1 else hi], key, xs[-key[1]])
        elif kind == "ID":
            d = key[1]
            q = 2 if d == 1 else 1
            add(iref(2 * q), [w.wait(("IS", q))], ROWS)
            add(iref(2 * q).at[lo if d == 1 else hi], [w.wait(("IP", d))], HALF)
            w.send(iref(2 * q), key, xs[-d])
        else:
            add(iref(0), [w.wait(("IS", 0)), w.wait(("ID", 1)), w.wait(("ID", -1))], ROWS, img_out, scale_ref[0])

    lbuf[0] = jnp.zeros((8, 128), F32)

    def soften(n, carry):
        p = 7 - n
        cols = pl.ds(pl.multiple_of(p * 256, 256), 256)
        blocks = blocks_of(p)
        cl = jnp.concatenate([cst[8, 0, pl.ds(b, 1), :] for b in blocks], axis=1)

        def soft(b, inner):
            r = pl.ds(pl.multiple_of(b * ROWS, ROWS), ROWS)
            v = L[r, cols]
            rl = row_m[r, :]
            g = jnp.exp2(v - jnp.concatenate([rl, rl], axis=1)) + jnp.exp2(v - cl)
            h = g.astype(BF16)
            Ph[r, cols] = h
            Pl[r, cols] = (g - h.astype(F32)).astype(BF16)
            return inner

        lax.fori_loop(0, IMG // ROWS, soft, 0)
        for j in range(2):
            there = t * 16 + blocks[j] - i * 8

            @pl.when((there >= 0) & (there < 8))
            def _():
                d = (there // 2 + 4 - x) % 4
                s = step_of(d) * 2 + (there % 2 + k) % 2
                r = pl.ds(pl.multiple_of(s * ROWS, ROWS), ROWS)
                c = pl.ds(pl.multiple_of(p * 256 + j * 128, 128), 128)
                v = L[r, c]
                g = jnp.exp2(v - row_m[r, :]) + jnp.exp2(v - cl[:, 128 * j : 128 * j + 128]) - eye[...]
                h = g.astype(BF16)
                Ph[r, c] = h
                Pl[r, c] = (g - h.astype(F32)).astype(BF16)
                lbuf[0] += jnp.sum((v * eye[...]).reshape(ROWS // 8, 8, 128), axis=0)

        return carry

    def loss_send(m):
        if m == 1:
            total = jnp.sum(acc[...]) / 1024 - 2.0 * LN2 * jnp.sum(lbuf[0])
            lbuf[0] = jnp.full((8, 128), total, F32)
            w.send(lbuf.at[0], "ls", sib)
        if m == 3:
            w.wait("ls")
            lbuf[2] = lbuf[0] + lbuf[1]
            for d in (1, -1, 2):
                w.send(lbuf.at[2], ("lx", d), xs[d])
        if m in (5, 7):
            a, b, nbr, base = ("lx", "ly", ys, 2) if m == 5 else ("ly", "lz", zs, 6)
            for d in (1, -1, 2):
                w.wait((a, d))
            lbuf[base + 4] = (lbuf[base] + lbuf[base + 1]) + (lbuf[base + 2] + lbuf[base + 3])
            for d in (1, -1, 2):
                w.send(lbuf.at[base + 4], (b, d), nbr[d])

    def back_step(n, carry):
        is_text = pick(n, [int(kind == "t") for kind, _ in STEPS])
        arg = pick(n, [a for _, a in STEPS])
        lax.fori_loop(pick(n, [0, 1]), pick(n, [1, 8]), soften, 0)

        @pl.when(is_text == 1)
        def _():
            p = 7 - arg
            cols = pl.ds(pl.multiple_of(p * 256, 256), 256)
            res = dot3(Ph[:, cols], Pl[:, cols], Ih[...], Il[...], 0, 0)
            Tb[2 * p] = res[:ROWS]
            Tb[2 * p + 1] = res[ROWS:]

        @pl.when(is_text == 0)
        def _():
            r = pl.ds(pl.multiple_of(arg * 256, 256), 256)
            L[r, 0:E] = dot3(Ph[r, :], Pl[r, :], Th[...], Tl[...], 1, 0)

        for m in range(len(STEPS)):

            @pl.when(n == m)
            def _():
                for key in RETURN[m]:
                    (image_send if key[0][0] == "I" else text_send)(key)
                loss_send(m)

        return carry

    lax.fori_loop(0, len(STEPS), back_step, 0)
    for d in (1, -1, 2):
        w.wait(("lz", d))
    loss_ref[...] = ((lbuf[10] + lbuf[11]) + (lbuf[12] + lbuf[13])) / (2.0 * 16384)
    w.flush(like)
    assert not w.arrivals


def on_device(image_emb, text_emb, logit_scale):
    vm = pltpu.VMEM
    loss, image_grad, text_grad = pl.pallas_call(
        kernel,
        out_shape=(
            jax.ShapeDtypeStruct((8, 128), F32),
            jax.ShapeDtypeStruct((ROWS, E), F32),
            jax.ShapeDtypeStruct((ROWS, E), F32),
        ),
        in_specs=[
            pl.BlockSpec(memory_space=pltpu.SMEM),
            pl.BlockSpec(memory_space=pl.ANY),
            pl.BlockSpec(memory_space=pl.ANY),
        ],
        out_specs=[pl.BlockSpec(memory_space=vm)] * 3,
        scratch_shapes=[
            vm((8, ROWS, E), F32),
            vm((16, ROWS, E), F32),
            vm((IMG, E), BF16),
            vm((IMG, E), BF16),
            vm((TXT, E), BF16),
            vm((TXT, E), BF16),
            vm((IMG, TXT), F32),
            vm((IMG, TXT), BF16),
            vm((IMG, TXT), BF16),
            vm((IMG, 128), F32),
            vm((IMG, 128), F32),
            vm((7, 2, 8, 128), F32),
            vm((9, 2, 16, 128), F32),
            vm((8, 128), F32),
            vm((14, 8, 128), F32),
            vm((14, HALF, E), F32),
            vm((7, ROWS, E), F32),
            vm((ROWS, ROWS), F32),
            pltpu.SemaphoreType.DMA((56,)),
            pltpu.SemaphoreType.DMA((112,)),
            pltpu.SemaphoreType.DMA((2,)),
        ],
        compiler_params=pltpu.CompilerParams(
            collective_id=0, has_side_effects=True, vmem_limit_bytes=63 * 2**20
        ),
        name="contrastive",
    )(logit_scale.reshape(1), image_emb, text_emb)
    return loss[0, 0], image_grad, text_grad


def solution(mesh):
    in_specs = (P(("img", "txt"), None), P(("txt", "img"), None), P())
    out_specs = (P(), P(("img", "txt"), None), P(("txt", "img"), None))
    return jax.shard_map(
        on_device, mesh=mesh, in_specs=in_specs, out_specs=out_specs, check_vma=False
    )
```

```python
import functools

import jax
import jax.numpy as jnp
from jax import lax
from jax.experimental import pallas as pl
from jax.experimental.pallas import tpu as pltpu
from jax.sharding import PartitionSpec as P

MESH = pl.DeviceIdType.MESH
BF16, F32 = jnp.bfloat16, jnp.float32
LOG2E = 1.4426950408889634
LN2 = 0.6931471805599453

STEP = (0, 1, 3, 2)
ROWS = 128
HALF = ROWS // 2
E = 1280
IMG, TXT = 1024, 2048

TILES = ((0, 0), (1, 0), (0, 2), (1, 2), (2, 0), (2, 2), (0, 1), (1, 1), (2, 1), (3, 0), (3, 1), (3, 2), (0, 3), (1, 3), (2, 3), (3, 3))
GATHER = (
    (("TA", 0, 1), ("TB", 2, 0), ("IB", 2, 0), ("TB", 1, 0), ("IA", 0, 1), ("IB", 1, 0), ("S", 0, 0), ("TB", 0, 1),
     ("TA", 2, 0), ("IA", 2, 0), ("TA", 1, 0), ("IB", 0, 1), ("IA", 1, 0), ("TB", 2, 1), ("TA", 2, 1),
     ("IB", 3, 0, 0), ("TB", 3, 0, 1), ("IB", 1, 1), ("IA", 1, 1), ("TA", 1, 1), ("IA", 2, 1), ("S", 0, 1),
     ("S", 1, 0), ("S", 2, 0), ("TB", 3, 0, 0), ("TB", 1, 1), ("IB", 3, 0, 1), ("IB", 2, 1)),
    (("TA", 3, 0), ("IA", 3, 0), ("S", 2, 1), ("IA", 3, 1)),
    (("TB", 3, 1),),
    (("TA", 3, 1), ("IB", 3, 1)),
    (("S", 1, 1),),
    (),
    (("S", 3, 0),),
    (),
    (("S", 3, 1),),
    (),
    (),
    (),
    (),
    (),
    (),
    (),
    (),
)

STEPS = (("t", 4), ("t", 6), ("t", 7), ("i", 3), ("t", 3), ("t", 5), ("t", 2), ("i", 2), ("i", 1), ("t", 1), ("i", 0), ("t", 0))
RETURN = (
    (("S", 2, 0),),
    (("S", 3, 0),),
    (("S", 3, 1),),
    (("TA", "P", 0), ("IA", "P", 1), ("TA", "P", 1), ("IA", "P", 0), ("TB", "Y", 3), ("IB", "Y", 3)),
    (("S", 1, 1),),
    (("S", 2, 1),),
    (("TB", "Y", 1), ("S", 1, 0)),
    (("IB", "Y", 2), ("TA", "D", 0, 1), ("TA", "D", 1, -1), ("IB", "P", -1), ("IA", "D", 1, 1), ("TB", "Y", 2)),
    (("IA", "D", 1, -1), ("IB", "Y", 1), ("IA", "D", 0, 1), ("TB", "P", -1), ("TA", "D", 1, 1)),
    (("S", 0, 1),),
    (("IA", "D", 0, -1), ("IB", "Y", 0), ("TB", "Y", 0), ("TB", "D", -1), ("IB", "P", 1), ("TB", "P", 1)),
    (("S", 0, 0), ("IB", "D", -1), ("IA", "2"), ("TA", "2"), ("TA", "D", 0, -1), ("IB", "D", 1), ("TB", "D", 1),
     ("I", "F"), ("T", "F")),
)


def pick(n, values):
    return sum(jnp.where(n == j, v, 0) for j, v in enumerate(values))


def dot(a, b, ca, cb):
    return lax.dot_general(a, b, (((ca,), (cb,)), ((), ())), preferred_element_type=F32)


def dot3(ah, al, bh, bl, ca, cb):
    return dot(ah, bh, ca, cb) + (dot(ah, bl, ca, cb) + dot(al, bh, ca, cb))


class Wires:
    def __init__(self, send_sem, recv_sem):
        self.send_sem, self.recv_sem = send_sem, recv_sem
        self.sent, self.n_recv, self.arrivals = [], 0, {}

    def open(self, key, ref, *index):
        self.arrivals[key] = (ref, index, self.n_recv)
        self.n_recv += 1

    def send(self, src, key, dev):
        dst, index, n = self.arrivals[key]
        dst = dst.at[index]
        s = len(self.sent)
        cp = pltpu.make_async_remote_copy(
            src_ref=src,
            dst_ref=dst,
            send_sem=self.send_sem.at[s],
            recv_sem=self.recv_sem.at[n],
            device_id=dev,
            device_id_type=MESH,
        )
        cp.start()
        self.sent.append(dst.shape)

    def wait(self, key):
        dst, index, n = self.arrivals.pop(key)
        dst = dst.at[index]
        pltpu.make_async_copy(dst, dst, self.recv_sem.at[n]).wait()
        return dst

    def need(self, *keys):
        for key in keys:
            if key in self.arrivals:
                self.wait(key)

    def flush(self, like):
        for s, shape in enumerate(self.sent):
            ref = like(shape)
            pltpu.make_async_copy(ref, ref, self.send_sem.at[s]).wait()
        self.sent = []


def merge(parts):
    top = functools.reduce(jnp.maximum, [m for m, _ in parts])
    total = sum(s * jnp.exp2(m - top) for m, s in parts)
    return top, total


def kernel(
    scale_ref, img_ref, txt_ref,
    loss_ref, img_out, txt_out,
    Ib, Tb, Ih, Il, Th, Tl, L, Ph, Pl,
    row_m, row_s, col_m, col_s, rst, cst, acc, lbuf,
    iland, tland, eye,
    send_sem, recv_sem, local_sem,
):
    i, t = lax.axis_index("img"), lax.axis_index("txt")
    x, k = t // 2, t % 2
    z, y = i // 4, i % 4
    even = 1 - 2 * (y % 2)

    def dev(dx=0, dy=0, dz=0, dk=0):
        return (((z + dz) % 4) * 4 + (y + dy + 4) % 4, ((x + dx) % 4) * 2 + (k + dk) % 2)

    sib = dev(dk=1)
    xs = {1: dev(dx=1), -1: dev(dx=3), 2: dev(dx=2)}
    zs = {1: dev(dz=1), -1: dev(dz=3), 2: dev(dz=2)}
    yi, yt = dev(dy=even), dev(dy=-even)
    row_peers = [*xs.values(), yi, *(dev(dx=d, dy=even) for d in (1, 3, 2))]
    col_peers = [sib, yt, dev(dy=-even, dk=1)]
    peers = [*row_peers, *col_peers, *zs.values()]
    barrier = pltpu.get_barrier_semaphore()
    for peer in peers:
        pl.semaphore_signal(barrier, inc=1, device_id=peer, device_id_type=MESH)
    pl.semaphore_wait(barrier, len(peers))

    w = Wires(send_sem, recv_sem)

    def like(shape):
        if shape[-1] == E:
            return Ib.at[0, pl.ds(0, shape[0])]
        return {2: lbuf, 3: rst if shape[-2] == 8 else cst}[len(shape)].at[0]

    lo, hi = pl.ds(0, HALF), pl.ds(HALF, HALF)
    ring = {"I": xs, "T": zs}
    across = {"I": yi, "T": yt}
    own = {"I": img_ref, "T": txt_ref}

    def place(name, q, p):
        return (Ib, 2 * q + p) if name == "I" else (Tb, 4 * q + 2 * p)

    for name in "IT":
        for q in range(4):
            for p in range(2):
                if (q, p) == (0, 0):
                    continue
                w.open((name + "A", q, p), *place(name, q, p), lo)
                if (q, p) == (3, 0):
                    for n in range(2):
                        w.open((name + "B", 3, 0, n), *place(name, 3, 0), pl.ds(HALF + 32 * n, 32))
                else:
                    w.open((name + "B", q, p), *place(name, q, p), hi)
    for q in range(4):
        for p in range(2):
            w.open(("S", q, p), Tb, 4 * q + 2 * p + 1)

    def keys_of(name, q, p, parts="AB"):
        return [(name + part, q, p, *n) for part in parts for n in ((), (0,), (1,))]

    def block(name, q, p, rows):
        if (q, p) == (0, 0):
            return own[name].at[rows]
        ref, n = place(name, q, p)
        return ref.at[n, rows]

    def gather_send(key):
        if key[0] == "S":
            q, p = key[1:]
            w.need(*keys_of("T", q, p))
            w.send(block("T", q, p, pl.ds(0, ROWS)), key, sib)
            return
        name, part, q, p = key[0][0], key[0][1], key[1], key[2]
        rows = lo if part == "A" else hi
        if part == "A" and p == 1 and q == 0:
            source, dst = (0, 0), across[name]
        elif part == "B" and p == 1:
            source, dst = (q, 0), across[name]
        elif len(key) == 4:
            source, dst = (2 - key[3], 0), ring[name][1 - 2 * key[3]]
            rows = pl.ds(HALF + 32 * key[3], 32)
        elif q == 3:
            source, dst = (2 - p, p), ring[name][1 - 2 * p]
        else:
            source, dst = (0, p), ring[name][1 if q == 2 else -1]
        w.need(*keys_of(name, *source, part))
        w.send(block(name, *source, rows), key, dst)

    own_t = pltpu.make_async_copy(txt_ref, Tb.at[0], local_sem.at[0])
    own_i = pltpu.make_async_copy(img_ref, Ib.at[0], local_sem.at[1])
    for key in GATHER[0][:13]:
        gather_send(key)
    own_t.start()
    own_i.start()

    rows_iota = lax.broadcasted_iota(jnp.int32, (ROWS, ROWS), 0)
    cols_iota = lax.broadcasted_iota(jnp.int32, (ROWS, ROWS), 1)
    eye[...] = (rows_iota == cols_iota).astype(F32)
    row_m[...] = jnp.full((IMG, 128), -jnp.inf, F32)
    row_s[...] = jnp.zeros((IMG, 128), F32)
    col_m[...] = jnp.full((8, TXT), -jnp.inf, F32)
    col_s[...] = jnp.zeros((8, TXT), F32)

    def split_rows(src, first, count, high, low):
        def body(b, carry):
            n = first + b // 4
            o = pl.ds(pl.multiple_of(first * ROWS + b * 32, 32), 32)
            v = src[n, pl.ds(pl.multiple_of((b % 4) * 32, 32), 32), :]
            h = v.astype(BF16)
            high[o, :] = h
            low[o, :] = (v - h.astype(F32)).astype(BF16)
            return carry

        lax.fori_loop(0, 4 * count, body, 0)

    own_i.wait()
    own_t.wait()
    for key in GATHER[0][13:]:
        gather_send(key)

    s2 = scale_ref[0] * LOG2E
    seen_i = [int(qi not in [a for a, _ in TILES[:n]]) for n, (qi, _) in enumerate(TILES)]
    seen_t = [int(qt not in [b for _, b in TILES[:n]]) for n, (_, qt) in enumerate(TILES)]

    def tile(n, carry):
        for m, (qi, qt) in enumerate(TILES):

            @pl.when(n == m)
            def _():
                if m > 0:
                    for key in GATHER[m]:
                        gather_send(key)
                for p in range(2):
                    w.need(*keys_of("I", qi, p), *keys_of("T", qt, p), ("S", qt, p))

        a, b = pick(n, [qi for qi, _ in TILES]), pick(n, [qt for _, qt in TILES])

        @pl.when(pick(n, seen_i) == 1)
        def _():
            split_rows(Ib, 2 * a, 2, Ih, Il)

        @pl.when(pick(n, seen_t) == 1)
        def _():
            split_rows(Tb, 4 * b, 4, Th, Tl)

        rows = pl.ds(pl.multiple_of(a * 256, 256), 256)
        cols = pl.ds(pl.multiple_of(b * 512, 512), 512)
        L[rows, cols] = s2 * dot3(Ih[rows, :], Il[rows, :], Th[cols, :], Tl[cols, :], 1, 1)

        def peak(c, top):
            r = pl.ds(pl.multiple_of(a * 256 + c * ROWS, ROWS), ROWS)
            v = L[r, cols]
            vs = [v[:, 128 * j : 128 * j + 128] for j in range(4)]
            old = row_m[r, :]
            new = functools.reduce(jnp.maximum, vs, old)
            row_s[r, :] = row_s[r, :] * jnp.exp2(old - new) + sum(jnp.exp2(u - new) for u in vs)
            row_m[r, :] = new
            return jnp.maximum(top, jnp.max(v.reshape(ROWS // 8, 8, 512), axis=0))

        old = col_m[:, cols]
        top = lax.fori_loop(0, 2, peak, old)

        def total(c, s):
            r = pl.ds(pl.multiple_of(a * 256 + c * ROWS, ROWS), ROWS)
            v = L[r, cols].reshape(ROWS // 8, 8, 512)
            return s + jnp.sum(jnp.exp2(v - top[None]), axis=0)

        col_s[:, cols] = lax.fori_loop(0, 2, total, col_s[:, cols] * jnp.exp2(old - top))
        col_m[:, cols] = top
        return carry

    lax.fori_loop(0, len(TILES), tile, 0)

    def step_of(q):
        return q + q // 2 - 2 * (q // 3)

    def img_block(s):
        return ((x + step_of(s // 2)) % 4) * 2 + (y + s % 2) % 2

    def txt_block(s):
        return (((z + step_of(s // 4)) % 4) * 2 + (y + (s // 2) % 2) % 2) * 2 + (k + s % 2) % 2

    def fold_cols(s, carry):
        c = pl.ds(pl.multiple_of(s * ROWS, ROWS), ROWS)
        m8 = col_m[:, c]
        m1 = jnp.max(m8, axis=0, keepdims=True)
        at = pl.ds(txt_block(s), 1)
        cst[0, 0, at, :] = m1
        cst[0, 1, at, :] = jnp.sum(col_s[:, c] * jnp.exp2(m8 - m1), axis=0, keepdims=True)
        return carry

    def fold_rows(s, carry):
        r = pl.ds(pl.multiple_of(s * ROWS, ROWS), ROWS)
        mt, st = row_m[r, :].T, row_s[r, :].T
        m1 = jnp.max(mt, axis=0, keepdims=True)
        at = pl.ds(img_block(s), 1)
        rst[0, 0, at, :] = m1
        rst[0, 1, at, :] = jnp.sum(st * jnp.exp2(mt - m1), axis=0, keepdims=True)
        return carry

    lax.fori_loop(0, 16, fold_cols, 0)
    w.flush(like)
    assert not w.arrivals
    for n in range(7):
        w.open(("r", n), rst, 1 + n)
    for n in range(3):
        w.open(("c1", n), cst, 1 + n)
        w.open(("c2", n), cst, 5 + n)
    for n in range(3):
        w.send(cst.at[0], ("c1", n), col_peers[n])
    lax.fori_loop(0, 8, fold_rows, 0)
    for n in range(7):
        w.send(rst.at[0], ("r", n), row_peers[n])
    for n in range(3):
        w.wait(("c1", n))
    cst[4, 0], cst[4, 1] = merge([(cst[n, 0], cst[n, 1]) for n in range(4)])
    for n, d in enumerate((1, -1, 2)):
        w.send(cst.at[4], ("c2", n), zs[d])
    for n in range(7):
        w.wait(("r", n))
    m, s = merge([(rst[n, 0], rst[n, 1]) for n in range(8)])
    row_lse = m + jnp.log2(s)
    rst[8, 0] = row_lse + 1.0

    def spread(s, carry):
        r = pl.ds(pl.multiple_of(s * ROWS, ROWS), ROWS)
        v = rst[8, 0, pl.ds(img_block(s), 1), :]
        row_m[r, :] = jnp.broadcast_to(v, (ROWS, 128)).T
        return carry

    lax.fori_loop(0, 8, spread, 0)
    for n in range(3):
        w.wait(("c2", n))
    m, s = merge([(cst[n, 0], cst[n, 1]) for n in range(4, 8)])
    col_lse = m + jnp.log2(s)
    w.flush(like)
    cst[8, 0] = col_lse + 1.0
    acc[...] = jnp.full((8, 128), LN2 * (jnp.sum(row_lse) / 8 + jnp.sum(col_lse) / 16), F32)

    for name, land in (("I", iland), ("T", tland)):
        for p in range(2):
            w.open((name + "A", "P", p), land, p)
            for n, d in enumerate((1, -1)):
                w.open((name + "A", "D", p, d), land, 2 + 2 * p + n)
        w.open((name + "A", "2"), land, 6)
        for q in range(4):
            w.open((name + "B", "Y", q), land, 7 + q)
        for n, d in enumerate((1, -1)):
            w.open((name + "B", "P", d), land, 11, pl.ds(32 * n, 32))
            w.open((name + "B", "D", d), land, 12 + n)
    for q in range(4):
        for p in range(2):
            w.open(("S", q, p), Ib, 2 * q + p)
    for n in range(7):
        w.open(("l1", n), lbuf, 1 + n)
    for n in range(3):
        w.open(("l2", n), lbuf, 9 + n)
        w.open(("l3", n), lbuf, 13 + n)

    def add(dst, srcs, rows, out=None):
        step = 16

        def body(b, carry):
            r = pl.ds(pl.multiple_of(b * step, step), step)
            v = dst[r, :]
            for src in srcs:
                v = v + src[r, :]
            (dst if out is None else out)[r, :] = v
            return carry

        lax.fori_loop(0, rows // step, body, 0)

    summed = set()

    def sums(name, q, p, at, rows):
        if name == "I":
            return L.at[pl.ds((2 * q + p) * ROWS + at, rows), pl.ds(0, E)]
        if (q, p) not in summed:
            summed.add((q, p))
            add(Tb.at[4 * q + 2 * p], [w.wait(("S", q, p))], ROWS)
        return Tb.at[4 * q + 2 * p, pl.ds(at, rows)]

    def back_send(key):
        if key[0] == "S":
            q, p = key[1:]
            w.send(Tb.at[4 * q + 2 * p + 1], key, sib)
            return
        name, kind = key[0][0], key[1]
        way, part = ring[name], key[0]
        if part == name:
            out = img_out if name == "I" else txt_out
            A, B = name + "A", name + "B"
            srcs = [w.wait((A, "D", 0, 1)), w.wait((A, "D", 0, -1)), w.wait((A, "2"))]
            add(sums(name, 0, 0, 0, HALF), srcs, HALF, out.at[lo])
            srcs = [w.wait((B, "Y", 0)), w.wait((B, "D", 1)), w.wait((B, "D", -1))]
            add(sums(name, 0, 0, HALF, HALF), srcs, HALF, out.at[hi])
        elif part[1] == "A":
            if kind == "P":
                w.send(sums(name, 3, key[2], 0, HALF), key, way[2 * key[2] - 1])
            elif kind == "D":
                p, d = key[2:]
                mine = sums(name, 2 if d == 1 else 1, p, 0, HALF)
                if p == (1 - d) // 2:
                    add(mine, [w.wait((part, "P", p))], HALF)
                w.send(mine, key, way[-d])
            else:
                mine = sums(name, 0, 1, 0, HALF)
                add(mine, [w.wait((part, "D", 1, 1)), w.wait((part, "D", 1, -1))], HALF)
                w.send(mine, key, across[name])
        elif kind == "Y":
            w.send(sums(name, key[2], 1, HALF, HALF), key, across[name])
        elif kind == "P":
            d = key[2]
            if (name, "far") not in summed:
                summed.add((name, "far"))
                add(sums(name, 3, 0, HALF, HALF), [w.wait((part, "Y", 3))], HALF)
            w.send(sums(name, 3, 0, HALF if d == 1 else HALF + 32, 32), key, way[-d])
        else:
            d = key[2]
            q = 2 if d == 1 else 1
            mine = sums(name, q, 0, HALF, HALF)
            add(mine, [w.wait((part, "Y", q))], HALF)
            add(mine.at[pl.ds(0 if d == 1 else 32, 32)], [w.wait((part, "P", d))], 32)
            w.send(mine, key, way[-d])

    lbuf[0] = jnp.zeros((8, 128), F32)

    def soften(n, carry):
        first = STEPS[0][1]
        p = pick(n, [first] + [m for m in range(8) if m != first])
        cols = pl.ds(pl.multiple_of(p * 256, 256), 256)
        cl = jnp.concatenate([cst[8, 0, pl.ds(txt_block(2 * p + j), 1), :] for j in range(2)], axis=1)

        def soft(b, inner):
            r = pl.ds(pl.multiple_of(b * ROWS, ROWS), ROWS)
            v = L[r, cols]
            rl = row_m[r, :]
            g = jnp.exp2(v - jnp.concatenate([rl, rl], axis=1)) + jnp.exp2(v - cl)
            h = g.astype(BF16)
            Ph[r, cols] = h
            Pl[r, cols] = (g - h.astype(F32)).astype(BF16)
            return inner

        lax.fori_loop(0, IMG // ROWS, soft, 0)
        for j in range(2):
            s = 2 * p + j
            owner = (x * 2 + (k + j) % 2) * 16 + ((z + step_of(s // 4)) % 4) * 4
            owner = owner + (y + ((s // 2) % 2) * (4 - even)) % 4
            bi, bt = owner // 8, owner % 8

            @pl.when((bi // 4 == z) & ((bi % 4) // 2 == y // 2) & (bt % 2 == k))
            def _():
                u = step_of((bt // 2 + 4 - x) % 4) * 2 + (bi + y) % 2
                r = pl.ds(pl.multiple_of(u * ROWS, ROWS), ROWS)
                c = pl.ds(pl.multiple_of(s * ROWS, ROWS), ROWS)
                v = L[r, c]
                g = jnp.exp2(v - row_m[r, :]) + jnp.exp2(v - cl[:, 128 * j : 128 * j + 128]) - eye[...]
                h = g.astype(BF16)
                Ph[r, c] = h
                Pl[r, c] = (g - h.astype(F32)).astype(BF16)
                lbuf[0] += jnp.sum((v * eye[...]).reshape(ROWS // 8, 8, 128), axis=0)

        return carry

    def loss_send(m):
        if m == 1:
            total = jnp.sum(acc[...]) / 1024 - 2.0 * LN2 * jnp.sum(lbuf[0])
            lbuf[0] = jnp.full((8, 128), total, F32)
            for n in range(7):
                w.send(lbuf.at[0], ("l1", n), row_peers[n])
        if m == 4:
            for n in range(7):
                w.wait(("l1", n))
            lbuf[8] = sum(lbuf[n] for n in range(8))
            for n in range(3):
                w.send(lbuf.at[8], ("l2", n), col_peers[n])
        if m == 7:
            for n in range(3):
                w.wait(("l2", n))
            lbuf[12] = sum(lbuf[n] for n in range(8, 12))
            for n, d in enumerate((1, -1, 2)):
                w.send(lbuf.at[12], ("l3", n), zs[d])

    def back_step(n, carry):
        is_text = pick(n, [int(kind == "t") for kind, _ in STEPS])
        arg = pick(n, [a for _, a in STEPS])
        lax.fori_loop(pick(n, [0, 1]), pick(n, [1, 8]), soften, 0)

        @pl.when(is_text == 1)
        def _():
            cols = pl.ds(pl.multiple_of(arg * 256, 256), 256)
            res = dot3(Ph[:, cols], Pl[:, cols], Ih[...], Il[...], 0, 0)
            Tb[2 * arg] = res[:ROWS]
            Tb[2 * arg + 1] = res[ROWS:]

        @pl.when(is_text == 0)
        def _():
            r = pl.ds(pl.multiple_of(arg * 256, 256), 256)
            L[r, 0:E] = dot3(Ph[r, :], Pl[r, :], Th[...], Tl[...], 1, 0)

        for m in range(len(STEPS)):

            @pl.when(n == m)
            def _():
                for key in RETURN[m]:
                    back_send(key)
                loss_send(m)

        return carry

    lax.fori_loop(0, len(STEPS), back_step, 0)
    for n in range(3):
        w.wait(("l3", n))
    loss_ref[0] = jnp.sum(sum(lbuf[n] for n in range(12, 16))) / (1024 * 2.0 * 16384)
    w.flush(like)
    assert not w.arrivals


def on_device(image_emb, text_emb, logit_scale):
    vm = pltpu.VMEM
    loss, image_grad, text_grad = pl.pallas_call(
        kernel,
        out_shape=(
            jax.ShapeDtypeStruct((1,), F32),
            jax.ShapeDtypeStruct((ROWS, E), F32),
            jax.ShapeDtypeStruct((ROWS, E), F32),
        ),
        in_specs=[
            pl.BlockSpec(memory_space=pltpu.SMEM),
            pl.BlockSpec(memory_space=pl.ANY),
            pl.BlockSpec(memory_space=pl.ANY),
        ],
        out_specs=[pl.BlockSpec(memory_space=pltpu.SMEM)] + [pl.BlockSpec(memory_space=vm)] * 2,
        scratch_shapes=[
            vm((8, ROWS, E), F32),
            vm((16, ROWS, E), F32),
            vm((IMG, E), BF16),
            vm((IMG, E), BF16),
            vm((TXT, E), BF16),
            vm((TXT, E), BF16),
            vm((IMG, TXT), F32),
            vm((IMG, TXT), BF16),
            vm((IMG, TXT), BF16),
            vm((IMG, 128), F32),
            vm((IMG, 128), F32),
            vm((8, TXT), F32),
            vm((8, TXT), F32),
            vm((9, 2, 8, 128), F32),
            vm((9, 2, 16, 128), F32),
            vm((8, 128), F32),
            vm((16, 8, 128), F32),
            vm((14, HALF, E), F32),
            vm((14, HALF, E), F32),
            vm((ROWS, ROWS), F32),
            pltpu.SemaphoreType.DMA((56,)),
            pltpu.SemaphoreType.DMA((112,)),
            pltpu.SemaphoreType.DMA((2,)),
        ],
        compiler_params=pltpu.CompilerParams(
            collective_id=0, has_side_effects=True, vmem_limit_bytes=63 * 2**20
        ),
        name="contrastive",
    )(logit_scale.reshape(1), image_emb, text_emb)
    return loss.reshape(()), logit_scale * image_grad, logit_scale * text_grad


def solution(mesh):
    in_specs = (P(("img", "txt"), None), P(("txt", "img"), None), P())
    out_specs = (P(), P(("img", "txt"), None), P(("txt", "img"), None))
    return jax.shard_map(
        on_device, mesh=mesh, in_specs=in_specs, out_specs=out_specs, check_vma=False
    )
```

```python
import functools

import jax
import jax.numpy as jnp
from jax import lax
from jax.experimental import pallas as pl
from jax.experimental.pallas import tpu as pltpu
from jax.sharding import PartitionSpec as P

MESH = pl.DeviceIdType.MESH
BF16, F32 = jnp.bfloat16, jnp.float32
LOG2E = 1.4426950408889634
LN2 = 0.6931471805599453

STEP = (0, 1, 3, 2)
F8 = jnp.float8_e4m3fn
ROWS = 128
HALF = ROWS // 2
E = 1280
IMG, TXT = 1024, 2048

TILES = ((0, 0), (1, 0), (0, 2), (1, 2), (2, 0), (2, 2), (0, 1), (1, 1), (2, 1), (3, 0), (3, 1), (3, 2), (0, 3), (1, 3), (2, 3), (3, 3))
GATHER = (
    (("TA", 0, 1), ("TB", 2, 0), ("IB", 2, 0), ("TB", 1, 0), ("IA", 0, 1), ("IB", 1, 0), ("S", 0, 0), ("TB", 0, 1),
     ("TA", 2, 0), ("IA", 2, 0), ("TA", 1, 0), ("IB", 0, 1), ("IA", 1, 0), ("TB", 2, 1), ("TA", 2, 1),
     ("IB", 3, 0, 0), ("TB", 3, 0, 1), ("IB", 1, 1), ("IA", 1, 1), ("TA", 1, 1), ("IA", 2, 1), ("S", 0, 1),
     ("S", 1, 0), ("S", 2, 0), ("TB", 3, 0, 0), ("TB", 1, 1), ("IB", 3, 0, 1), ("IB", 2, 1)),
    (("TA", 3, 0), ("IA", 3, 0), ("S", 2, 1), ("IA", 3, 1)),
    (("TB", 3, 1),),
    (("TA", 3, 1), ("IB", 3, 1)),
    (("S", 1, 1),),
    (),
    (("S", 3, 0),),
    (),
    (("S", 3, 1),),
    (),
    (),
    (),
    (),
    (),
    (),
    (),
    (),
)

STEPS = (("t", 7), ("t", 6), ("i", 3), ("t", 5), ("t", 3), ("i", 2), ("t", 4), ("i", 1), ("t", 1), ("t", 2), ("i", 0), ("t", 0))
RETURN = (
    (("S", 3, 1),),
    (("S", 3, 0), ("TB", "Y", 3), ("TA", "P", 1)),
    (("IA", "P", 0), ("IA", "P", 1), ("IB", "Y", 3), ("TA", "P", 0)),
    (("S", 2, 1),),
    (("S", 1, 1),),
    (("IB", "Y", 2), ("IA", "D", 1, 1), ("TB", "P", -1), ("TA", "D", 1, 1), ("TB", "Y", 2), ("TA", "D", 1, -1)),
    (("IB", "P", -1), ("S", 2, 0)),
    (("IA", "D", 1, -1), ("IB", "Y", 1), ("IA", "D", 0, 1), ("TA", "D", 0, 1), ("TB", "Y", 1)),
    (("S", 0, 1),),
    (("S", 1, 0), ("IA", "D", 0, -1)),
    (("IB", "Y", 0), ("TB", "Y", 0), ("IB", "P", 1), ("TA", "D", 0, -1), ("TB", "P", 1)),
    (("S", 0, 0), ("IB", "D", -1), ("IA", "2"), ("TA", "2"), ("TB", "D", -1), ("IB", "D", 1), ("TB", "D", 1),
     ("I", "F"), ("T", "F")),
)


def pick(n, values):
    return sum(jnp.where(n == j, v, 0) for j, v in enumerate(values))


def dot(a, b, ca, cb):
    return lax.dot_general(a, b, (((ca,), (cb,)), ((), ())), preferred_element_type=F32)


def dot3(ah, al, bh, bl, ca, cb):
    return dot(ah, bh, ca, cb) + (dot(ah, bl, ca, cb) + dot(al, bh, ca, cb))


class Wires:
    def __init__(self, send_sem, recv_sem):
        self.send_sem, self.recv_sem = send_sem, recv_sem
        self.sent, self.n_recv, self.arrivals = [], 0, {}

    def open(self, key, ref, *index):
        self.arrivals[key] = (ref, index, self.n_recv)
        self.n_recv += 1

    def send(self, src, key, dev):
        dst, index, n = self.arrivals[key]
        dst = dst.at[index]
        s = len(self.sent)
        cp = pltpu.make_async_remote_copy(
            src_ref=src,
            dst_ref=dst,
            send_sem=self.send_sem.at[s],
            recv_sem=self.recv_sem.at[n],
            device_id=dev,
            device_id_type=MESH,
        )
        cp.start()
        self.sent.append(dst.shape)

    def wait(self, key):
        dst, index, n = self.arrivals.pop(key)
        dst = dst.at[index]
        pltpu.make_async_copy(dst, dst, self.recv_sem.at[n]).wait()
        return dst

    def need(self, *keys):
        for key in keys:
            if key in self.arrivals:
                self.wait(key)

    def flush(self, like):
        for s, shape in enumerate(self.sent):
            ref = like(shape)
            pltpu.make_async_copy(ref, ref, self.send_sem.at[s]).wait()
        self.sent = []


def merge(parts):
    top = functools.reduce(jnp.maximum, [m for m, _ in parts])
    total = sum(s * jnp.exp2(m - top) for m, s in parts)
    return top, total


def kernel(
    scale_ref, img_ref, txt_ref,
    loss_ref, img_out, txt_out,
    Ib, Tb, Ih, Il, Th, Tl, L,
    P8h, P8l, I8h, I8l, T8h, T8l,
    row_m, row_s, col_m, col_s, rst, cst, acc, lbuf,
    iland, tland, eye,
    send_sem, recv_sem, local_sem,
):
    i, t = lax.axis_index("img"), lax.axis_index("txt")
    x, k = t // 2, t % 2
    z, y = i // 4, i % 4
    even = 1 - 2 * (y % 2)

    def dev(dx=0, dy=0, dz=0, dk=0):
        return (((z + dz) % 4) * 4 + (y + dy + 4) % 4, ((x + dx) % 4) * 2 + (k + dk) % 2)

    sib = dev(dk=1)
    xs = {1: dev(dx=1), -1: dev(dx=3), 2: dev(dx=2)}
    zs = {1: dev(dz=1), -1: dev(dz=3), 2: dev(dz=2)}
    yi, yt = dev(dy=even), dev(dy=-even)
    row_peers = [*xs.values(), yi, *(dev(dx=d, dy=even) for d in (1, 3, 2))]
    col_peers = [sib, yt, dev(dy=-even, dk=1)]
    peers = [*row_peers, *col_peers, *zs.values()]
    barrier = pltpu.get_barrier_semaphore()
    for peer in peers:
        pl.semaphore_signal(barrier, inc=1, device_id=peer, device_id_type=MESH)
    pl.semaphore_wait(barrier, len(peers))

    w = Wires(send_sem, recv_sem)

    def like(shape):
        if shape[-1] == E:
            return Ib.at[0, pl.ds(0, shape[0])]
        return {2: lbuf, 3: rst if shape[-2] == 8 else cst}[len(shape)].at[0]

    lo, hi = pl.ds(0, HALF), pl.ds(HALF, HALF)
    ring = {"I": xs, "T": zs}
    across = {"I": yi, "T": yt}
    own = {"I": img_ref, "T": txt_ref}

    def place(name, q, p):
        return (Ib, 2 * q + p) if name == "I" else (Tb, 4 * q + 2 * p)

    for name in "IT":
        for q in range(4):
            for p in range(2):
                if (q, p) == (0, 0):
                    continue
                w.open((name + "A", q, p), *place(name, q, p), lo)
                if (q, p) == (3, 0):
                    for n in range(2):
                        w.open((name + "B", 3, 0, n), *place(name, 3, 0), pl.ds(HALF + 32 * n, 32))
                else:
                    w.open((name + "B", q, p), *place(name, q, p), hi)
    for q in range(4):
        for p in range(2):
            w.open(("S", q, p), Tb, 4 * q + 2 * p + 1)

    def keys_of(name, q, p, parts="AB"):
        return [(name + part, q, p, *n) for part in parts for n in ((), (0,), (1,))]

    def block(name, q, p, rows):
        if (q, p) == (0, 0):
            return own[name].at[rows]
        ref, n = place(name, q, p)
        return ref.at[n, rows]

    def gather_send(key):
        if key[0] == "S":
            q, p = key[1:]
            w.need(*keys_of("T", q, p))
            w.send(block("T", q, p, pl.ds(0, ROWS)), key, sib)
            return
        name, part, q, p = key[0][0], key[0][1], key[1], key[2]
        rows = lo if part == "A" else hi
        if part == "A" and p == 1 and q == 0:
            source, dst = (0, 0), across[name]
        elif part == "B" and p == 1:
            source, dst = (q, 0), across[name]
        elif len(key) == 4:
            source, dst = (2 - key[3], 0), ring[name][1 - 2 * key[3]]
            rows = pl.ds(HALF + 32 * key[3], 32)
        elif q == 3:
            source, dst = (2 - p, p), ring[name][1 - 2 * p]
        else:
            source, dst = (0, p), ring[name][1 if q == 2 else -1]
        w.need(*keys_of(name, *source, part))
        w.send(block(name, *source, rows), key, dst)

    own_t = pltpu.make_async_copy(txt_ref, Tb.at[0], local_sem.at[0])
    own_i = pltpu.make_async_copy(img_ref, Ib.at[0], local_sem.at[1])
    for key in GATHER[0][:13]:
        gather_send(key)
    own_t.start()
    own_i.start()

    rows_iota = lax.broadcasted_iota(jnp.int32, (ROWS, ROWS), 0)
    cols_iota = lax.broadcasted_iota(jnp.int32, (ROWS, ROWS), 1)
    eye[...] = (rows_iota == cols_iota).astype(F32)
    row_m[...] = jnp.full((IMG, 128), -jnp.inf, F32)
    row_s[...] = jnp.zeros((IMG, 128), F32)
    col_m[...] = jnp.full((8, TXT), -jnp.inf, F32)
    col_s[...] = jnp.zeros((8, TXT), F32)

    def split_rows(src, first, count, high, low):
        def body(b, carry):
            n = first + b // 4
            o = pl.ds(pl.multiple_of(first * ROWS + b * 32, 32), 32)
            v = src[n, pl.ds(pl.multiple_of((b % 4) * 32, 32), 32), :]
            h = v.astype(BF16)
            high[o, :] = h
            low[o, :] = (v - h.astype(F32)).astype(BF16)
            return carry

        lax.fori_loop(0, 4 * count, body, 0)

    own_i.wait()
    own_t.wait()
    for key in GATHER[0][13:]:
        gather_send(key)

    s2 = scale_ref[0] * LOG2E
    seen_i = [int(qi not in [a for a, _ in TILES[:n]]) for n, (qi, _) in enumerate(TILES)]
    seen_t = [int(qt not in [b for _, b in TILES[:n]]) for n, (_, qt) in enumerate(TILES)]

    def tile(n, carry):
        for m, (qi, qt) in enumerate(TILES):

            @pl.when(n == m)
            def _():
                if m > 0:
                    for key in GATHER[m]:
                        gather_send(key)
                for p in range(2):
                    w.need(*keys_of("I", qi, p), *keys_of("T", qt, p), ("S", qt, p))

        a, b = pick(n, [qi for qi, _ in TILES]), pick(n, [qt for _, qt in TILES])

        @pl.when(pick(n, seen_i) == 1)
        def _():
            split_rows(Ib, 2 * a, 2, Ih, Il)

        @pl.when(pick(n, seen_t) == 1)
        def _():
            split_rows(Tb, 4 * b, 4, Th, Tl)

        rows = pl.ds(pl.multiple_of(a * 256, 256), 256)
        cols = pl.ds(pl.multiple_of(b * 512, 512), 512)
        L[rows, cols] = s2 * dot3(Ih[rows, :], Il[rows, :], Th[cols, :], Tl[cols, :], 1, 1)

        def peak(c, top):
            r = pl.ds(pl.multiple_of(a * 256 + c * ROWS, ROWS), ROWS)
            v = L[r, cols]
            vs = [v[:, 128 * j : 128 * j + 128] for j in range(4)]
            old = row_m[r, :]
            new = functools.reduce(jnp.maximum, vs, old)
            row_s[r, :] = row_s[r, :] * jnp.exp2(old - new) + sum(jnp.exp2(u - new) for u in vs)
            row_m[r, :] = new
            return jnp.maximum(top, jnp.max(v.reshape(ROWS // 8, 8, 512), axis=0))

        old = col_m[:, cols]
        top = lax.fori_loop(0, 2, peak, old)

        def total(c, s):
            r = pl.ds(pl.multiple_of(a * 256 + c * ROWS, ROWS), ROWS)
            v = L[r, cols].reshape(ROWS // 8, 8, 512)
            return s + jnp.sum(jnp.exp2(v - top[None]), axis=0)

        col_s[:, cols] = lax.fori_loop(0, 2, total, col_s[:, cols] * jnp.exp2(old - top))
        col_m[:, cols] = top
        return carry

    lax.fori_loop(0, len(TILES), tile, 0)

    def step_of(q):
        return q + q // 2 - 2 * (q // 3)

    def img_block(s):
        return ((x + step_of(s // 2)) % 4) * 2 + (y + s % 2) % 2

    def txt_block(s):
        return (((z + step_of(s // 4)) % 4) * 2 + (y + (s // 2) % 2) % 2) * 2 + (k + s % 2) % 2

    def fold_cols(s, carry):
        c = pl.ds(pl.multiple_of(s * ROWS, ROWS), ROWS)
        m8 = col_m[:, c]
        m1 = jnp.max(m8, axis=0, keepdims=True)
        at = pl.ds(txt_block(s), 1)
        cst[0, 0, at, :] = m1
        cst[0, 1, at, :] = jnp.sum(col_s[:, c] * jnp.exp2(m8 - m1), axis=0, keepdims=True)
        return carry

    def fold_rows(s, carry):
        r = pl.ds(pl.multiple_of(s * ROWS, ROWS), ROWS)
        mt, st = row_m[r, :].T, row_s[r, :].T
        m1 = jnp.max(mt, axis=0, keepdims=True)
        at = pl.ds(img_block(s), 1)
        rst[0, 0, at, :] = m1
        rst[0, 1, at, :] = jnp.sum(st * jnp.exp2(mt - m1), axis=0, keepdims=True)
        return carry

    lax.fori_loop(0, 16, fold_cols, 0)
    w.flush(like)
    assert not w.arrivals
    for n in range(7):
        w.open(("r", n), rst, 1 + n)
    for n in range(3):
        w.open(("c1", n), cst, 1 + n)
        w.open(("c2", n), cst, 5 + n)
    for n in range(3):
        w.send(cst.at[0], ("c1", n), col_peers[n])
    lax.fori_loop(0, 8, fold_rows, 0)
    for n in range(7):
        w.send(rst.at[0], ("r", n), row_peers[n])
    def largest(src, count):
        def body(b, top):
            v = jnp.abs(src[pl.ds(pl.multiple_of(b * 64, 64), 64), :]).astype(F32)
            return jnp.maximum(top, jnp.max(v.reshape(8, 8, E), axis=0))

        return jnp.max(lax.fori_loop(0, count // 64, body, jnp.zeros((8, E), F32)))

    i_scale = 240.0 / jnp.maximum(largest(Ih, IMG), 1e-30)
    t_scale = 240.0 / jnp.maximum(largest(Th, TXT), 1e-30)

    def to_eight(high, low, count, scale, high8, low8):
        def body(b, carry):
            r = pl.ds(pl.multiple_of(b * 64, 64), 64)
            high8[r, :] = (high[r, :].astype(F32) * scale).astype(F8)
            low8[r, :] = (low[r, :].astype(F32) * (256.0 * scale)).astype(F8)
            return carry

        lax.fori_loop(0, count // 64, body, 0)

    for n in range(3):
        w.wait(("c1", n))
    cst[4, 0], cst[4, 1] = merge([(cst[n, 0], cst[n, 1]) for n in range(4)])
    for n, d in enumerate((1, -1, 2)):
        w.send(cst.at[4], ("c2", n), zs[d])
    to_eight(Ih, Il, IMG, i_scale, I8h, I8l)
    to_eight(Th, Tl, TXT, t_scale, T8h, T8l)
    for n in range(7):
        w.wait(("r", n))
    m, s = merge([(rst[n, 0], rst[n, 1]) for n in range(8)])
    row_lse = m + jnp.log2(s)
    rst[8, 0] = row_lse + 1.0

    def spread(s, carry):
        r = pl.ds(pl.multiple_of(s * ROWS, ROWS), ROWS)
        v = rst[8, 0, pl.ds(img_block(s), 1), :]
        row_m[r, :] = jnp.broadcast_to(v, (ROWS, 128)).T
        return carry

    lax.fori_loop(0, 8, spread, 0)
    for n in range(3):
        w.wait(("c2", n))
    m, s = merge([(cst[n, 0], cst[n, 1]) for n in range(4, 8)])
    col_lse = m + jnp.log2(s)
    w.flush(like)
    cst[8, 0] = col_lse + 1.0
    acc[...] = jnp.full((8, 128), LN2 * (jnp.sum(row_lse) / 8 + jnp.sum(col_lse) / 16), F32)

    for name, land in (("I", iland), ("T", tland)):
        for p in range(2):
            w.open((name + "A", "P", p), land, p)
            for n, d in enumerate((1, -1)):
                w.open((name + "A", "D", p, d), land, 2 + 2 * p + n)
        w.open((name + "A", "2"), land, 6)
        for q in range(4):
            w.open((name + "B", "Y", q), land, 7 + q)
        for n, d in enumerate((1, -1)):
            w.open((name + "B", "P", d), land, 11, pl.ds(32 * n, 32))
            w.open((name + "B", "D", d), land, 12 + n)
    for q in range(4):
        for p in range(2):
            w.open(("S", q, p), Ib, 2 * q + p)
    for n in range(7):
        w.open(("l1", n), lbuf, 1 + n)
    for n in range(3):
        w.open(("l2", n), lbuf, 9 + n)
        w.open(("l3", n), lbuf, 13 + n)

    def add(dst, srcs, rows, out=None):
        step = 16

        def body(b, carry):
            r = pl.ds(pl.multiple_of(b * step, step), step)
            v = dst[r, :]
            for src in srcs:
                v = v + src[r, :]
            (dst if out is None else out)[r, :] = v
            return carry

        lax.fori_loop(0, rows // step, body, 0)

    summed = set()

    def sums(name, q, p, at, rows):
        if name == "I":
            return L.at[pl.ds((2 * q + p) * ROWS + at, rows), pl.ds(0, E)]
        if (q, p) not in summed:
            summed.add((q, p))
            add(Tb.at[4 * q + 2 * p], [w.wait(("S", q, p))], ROWS)
        return Tb.at[4 * q + 2 * p, pl.ds(at, rows)]

    def back_send(key):
        if key[0] == "S":
            q, p = key[1:]
            w.send(Tb.at[4 * q + 2 * p + 1], key, sib)
            return
        name, kind = key[0][0], key[1]
        way, part = ring[name], key[0]
        if part == name:
            out = img_out if name == "I" else txt_out
            A, B = name + "A", name + "B"
            srcs = [w.wait((A, "D", 0, 1)), w.wait((A, "D", 0, -1)), w.wait((A, "2"))]
            add(sums(name, 0, 0, 0, HALF), srcs, HALF, out.at[lo])
            srcs = [w.wait((B, "Y", 0)), w.wait((B, "D", 1)), w.wait((B, "D", -1))]
            add(sums(name, 0, 0, HALF, HALF), srcs, HALF, out.at[hi])
        elif part[1] == "A":
            if kind == "P":
                w.send(sums(name, 3, key[2], 0, HALF), key, way[2 * key[2] - 1])
            elif kind == "D":
                p, d = key[2:]
                mine = sums(name, 2 if d == 1 else 1, p, 0, HALF)
                if p == (1 - d) // 2:
                    add(mine, [w.wait((part, "P", p))], HALF)
                w.send(mine, key, way[-d])
            else:
                mine = sums(name, 0, 1, 0, HALF)
                add(mine, [w.wait((part, "D", 1, 1)), w.wait((part, "D", 1, -1))], HALF)
                w.send(mine, key, across[name])
        elif kind == "Y":
            w.send(sums(name, key[2], 1, HALF, HALF), key, across[name])
        elif kind == "P":
            d = key[2]
            if (name, "far") not in summed:
                summed.add((name, "far"))
                add(sums(name, 3, 0, HALF, HALF), [w.wait((part, "Y", 3))], HALF)
            w.send(sums(name, 3, 0, HALF if d == 1 else HALF + 32, 32), key, way[-d])
        else:
            d = key[2]
            q = 2 if d == 1 else 1
            mine = sums(name, q, 0, HALF, HALF)
            add(mine, [w.wait((part, "Y", q))], HALF)
            add(mine.at[pl.ds(0 if d == 1 else 32, 32)], [w.wait((part, "P", d))], 32)
            w.send(mine, key, way[-d])

    lbuf[0] = jnp.zeros((8, 128), F32)

    def put_grad(g, r, c, width):
        first, size = r
        h = g.astype(BF16)
        rows = pl.ds(pl.multiple_of(first, ROWS), size)
        cols = pl.ds(pl.multiple_of(c, ROWS), width)
        below = pl.ds(pl.multiple_of(first + (c // IMG) * IMG, ROWS), size)
        Tl[below, pl.ds(pl.multiple_of(c % IMG, ROWS), width)] = h
        hf = h.astype(F32)
        P8h[rows, cols] = (hf * 256.0).astype(F8)
        P8l[rows, cols] = ((g - hf) * 65536.0).astype(F8)

    def soften(n, carry):
        first = STEPS[0][1]
        p = pick(n, [first] + [m for m in range(8) if m != first])
        cols = pl.ds(pl.multiple_of(p * 256, 256), 256)
        cl = jnp.concatenate([cst[8, 0, pl.ds(txt_block(2 * p + j), 1), :] for j in range(2)], axis=1)

        def soft(b, inner):
            r = pl.ds(pl.multiple_of(b * ROWS, ROWS), ROWS)
            v = L[r, cols]
            rl = row_m[r, :]
            g = jnp.exp2(v - jnp.concatenate([rl, rl], axis=1)) + jnp.exp2(v - cl)
            put_grad(g, (b * ROWS, ROWS), p * 256, 256)
            return inner

        lax.fori_loop(0, IMG // ROWS, soft, 0)
        for j in range(2):
            s = 2 * p + j
            owner = (x * 2 + (k + j) % 2) * 16 + ((z + step_of(s // 4)) % 4) * 4
            owner = owner + (y + ((s // 2) % 2) * (4 - even)) % 4
            bi, bt = owner // 8, owner % 8

            @pl.when((bi // 4 == z) & ((bi % 4) // 2 == y // 2) & (bt % 2 == k))
            def _():
                u = step_of((bt // 2 + 4 - x) % 4) * 2 + (bi + y) % 2
                r = pl.ds(pl.multiple_of(u * ROWS, ROWS), ROWS)
                c = pl.ds(pl.multiple_of(s * ROWS, ROWS), ROWS)
                v = L[r, c]
                g = jnp.exp2(v - row_m[r, :]) + jnp.exp2(v - cl[:, 128 * j : 128 * j + 128]) - eye[...]
                put_grad(g, (u * ROWS, ROWS), s * ROWS, ROWS)
                lbuf[0] += jnp.sum((v * eye[...]).reshape(ROWS // 8, 8, 128), axis=0)

        return carry

    def loss_send(m):
        if m == 1:
            total = jnp.sum(acc[...]) / 1024 - 2.0 * LN2 * jnp.sum(lbuf[0])
            lbuf[0] = jnp.full((8, 128), total, F32)
            for n in range(7):
                w.send(lbuf.at[0], ("l1", n), row_peers[n])
        if m == 4:
            for n in range(7):
                w.wait(("l1", n))
            lbuf[8] = sum(lbuf[n] for n in range(8))
            for n in range(3):
                w.send(lbuf.at[8], ("l2", n), col_peers[n])
        if m == 7:
            for n in range(3):
                w.wait(("l2", n))
            lbuf[12] = sum(lbuf[n] for n in range(8, 12))
            for n, d in enumerate((1, -1, 2)):
                w.send(lbuf.at[12], ("l3", n), zs[d])

    def back_step(n, carry):
        is_text = pick(n, [int(kind == "t") for kind, _ in STEPS])
        arg = pick(n, [a for _, a in STEPS])
        lax.fori_loop(pick(n, [0, 1]), pick(n, [1, 8]), soften, 0)

        @pl.when(is_text == 1)
        def _():
            cols = pl.ds(pl.multiple_of(arg * 256, 256), 256)
            below = pl.ds(pl.multiple_of((arg // 4) * IMG, IMG), IMG)
            high = dot(Tl[below, pl.ds(pl.multiple_of((arg % 4) * 256, 256), 256)], Ih[...], 0, 0)
            cross = dot(P8h[:, cols], I8l[...], 0, 0) + dot(P8l[:, cols], I8h[...], 0, 0)
            res = high + (1.0 / (65536.0 * i_scale)) * cross
            Tb[2 * arg] = res[:ROWS]
            Tb[2 * arg + 1] = res[ROWS:]

        @pl.when(is_text == 0)
        def _():
            r = pl.ds(pl.multiple_of(arg * 256, 256), 256)
            r2 = pl.ds(pl.multiple_of(IMG + arg * 256, 256), 256)
            high = dot(Tl[r, 0:IMG], Th[0:IMG, :], 1, 0) + dot(Tl[r2, 0:IMG], Th[IMG:TXT, :], 1, 0)
            cross = dot(P8h[r, :], T8l[...], 1, 0) + dot(P8l[r, :], T8h[...], 1, 0)
            L[r, 0:E] = high + (1.0 / (65536.0 * t_scale)) * cross

        for m in range(len(STEPS)):

            @pl.when(n == m)
            def _():
                for key in RETURN[m]:
                    back_send(key)
                loss_send(m)

        return carry

    lax.fori_loop(0, len(STEPS), back_step, 0)
    for n in range(3):
        w.wait(("l3", n))
    loss_ref[0] = jnp.sum(sum(lbuf[n] for n in range(12, 16))) / (1024 * 2.0 * 16384)
    w.flush(like)
    assert not w.arrivals


def on_device(image_emb, text_emb, logit_scale):
    vm = pltpu.VMEM
    loss, image_grad, text_grad = pl.pallas_call(
        kernel,
        out_shape=(
            jax.ShapeDtypeStruct((1,), F32),
            jax.ShapeDtypeStruct((ROWS, E), F32),
            jax.ShapeDtypeStruct((ROWS, E), F32),
        ),
        in_specs=[
            pl.BlockSpec(memory_space=pltpu.SMEM),
            pl.BlockSpec(memory_space=pl.ANY),
            pl.BlockSpec(memory_space=pl.ANY),
        ],
        out_specs=[pl.BlockSpec(memory_space=pltpu.SMEM)] + [pl.BlockSpec(memory_space=vm)] * 2,
        scratch_shapes=[
            vm((8, ROWS, E), F32),
            vm((16, ROWS, E), F32),
            vm((IMG, E), BF16),
            vm((IMG, E), BF16),
            vm((TXT, E), BF16),
            vm((TXT, E), BF16),
            vm((IMG, TXT), F32),
            vm((IMG, TXT), F8),
            vm((IMG, TXT), F8),
            vm((IMG, E), F8),
            vm((IMG, E), F8),
            vm((TXT, E), F8),
            vm((TXT, E), F8),
            vm((IMG, 128), F32),
            vm((IMG, 128), F32),
            vm((8, TXT), F32),
            vm((8, TXT), F32),
            vm((9, 2, 8, 128), F32),
            vm((9, 2, 16, 128), F32),
            vm((8, 128), F32),
            vm((16, 8, 128), F32),
            vm((14, HALF, E), F32),
            vm((14, HALF, E), F32),
            vm((ROWS, ROWS), F32),
            pltpu.SemaphoreType.DMA((56,)),
            pltpu.SemaphoreType.DMA((112,)),
            pltpu.SemaphoreType.DMA((2,)),
        ],
        compiler_params=pltpu.CompilerParams(
            collective_id=0, has_side_effects=True, vmem_limit_bytes=63 * 2**20
        ),
        name="contrastive",
    )(logit_scale.reshape(1), image_emb, text_emb)
    return loss.reshape(()), logit_scale * image_grad, logit_scale * text_grad


def solution(mesh):
    in_specs = (P(("img", "txt"), None), P(("txt", "img"), None), P())
    out_specs = (P(), P(("img", "txt"), None), P(("txt", "img"), None))
    return jax.shard_map(
        on_device, mesh=mesh, in_specs=in_specs, out_specs=out_specs, check_vma=False
    )
```

```python
import functools

import jax
import jax.numpy as jnp
from jax import lax
from jax.experimental import pallas as pl
from jax.experimental.pallas import tpu as pltpu
from jax.sharding import PartitionSpec as P

MESH = pl.DeviceIdType.MESH
BF16, F32 = jnp.bfloat16, jnp.float32
LOG2E = 1.4426950408889634
LN2 = 0.6931471805599453

STEP = (0, 1, 3, 2)
F8 = jnp.float8_e4m3fn
ROWS = 128
HALF = ROWS // 2
E = 1280
CHUNK = 64
IMG, TXT = 1024, 2048

TILES = ((0, 0), (1, 0), (0, 2), (1, 2), (2, 0), (2, 2), (0, 1), (1, 1), (2, 1), (3, 0), (3, 1), (3, 2), (0, 3), (1, 3), (2, 3), (3, 3))
GATHER = (
    (("TA", 0, 1), ("TB", 2, 0), ("IB", 2, 0), ("TB", 1, 0), ("IA", 0, 1), ("IB", 1, 0), ("S", 0, 0), ("TB", 0, 1),
     ("TA", 2, 0), ("IA", 2, 0), ("TA", 1, 0), ("IB", 0, 1), ("IA", 1, 0), ("TB", 2, 1), ("TA", 2, 1),
     ("IB", 3, 0, 0), ("TB", 3, 0, 1), ("IB", 1, 1), ("IA", 1, 1), ("TA", 1, 1), ("IA", 2, 1), ("S", 0, 1),
     ("S", 1, 0), ("S", 2, 0), ("TB", 3, 0, 0), ("TB", 1, 1), ("IB", 3, 0, 1), ("IB", 2, 1)),
    (("TA", 3, 0), ("IA", 3, 0), ("S", 2, 1), ("IA", 3, 1)),
    (("TB", 3, 1),),
    (("TA", 3, 1), ("IB", 3, 1)),
    (("S", 1, 1),),
    (),
    (("S", 3, 0),),
    (),
    (("S", 3, 1),),
    (),
    (),
    (),
    (),
    (),
    (),
    (),
    (),
)

STEPS = (("t", 7), ("t", 6), ("i", 7), ("t", 5), ("i", 5), ("t", 3), ("t", 4), ("i", 6), ("i", 3), ("t", 1), ("t", 2), ("i", 2), ("i", 1), ("i", 4), ("t", 0), ("i", 0))
RETURN = (
    (("S", 3, 1),),
    (("S", 3, 0),),
    (("TB", "Y", 3), ("IB", "Y", 3), ("TA", "P", 1), ("IA", "P", 1), ("TA", "P", 0)),
    (("S", 2, 1),),
    (("IA", "D", 1, 1),),
    (("S", 1, 1), ("TB", "Y", 2), ("IB", "Y", 2)),
    (("S", 2, 0), ("TA", "D", 1, 1)),
    (("IB", "P", -1), ("TA", "D", 1, -1), ("IA", "P", 0)),
    (),
    (("S", 0, 1), ("IA", "D", 1, -1), ("TB", "Y", 1), ("TA", "D", 0, 1), ("IB", "Y", 1)),
    (("S", 1, 0), ("TB", "P", -1)),
    (("IB", "P", 1),),
    (("IA", "D", 0, -1), ("TA", "2"), ("TA", "D", 0, -1), ("IB", "Y", 0)),
    (("IA", "D", 0, 1), ("TB", "P", 1)),
    (("S", 0, 0),),
    (("IB", "D", -1), ("TB", "D", -1), ("IA", "2"), ("TB", "Y", 0), ("TB", "D", 1), ("IB", "D", 1), ("T", "F"),
     ("I", "F")),
)


FIRST_IMAGE = [kind for kind, _ in STEPS].index("i")
SOFT = [n if n <= FIRST_IMAGE else 8 for n in range(len(STEPS) + 1)]


def pick(n, values):
    return sum(jnp.where(n == j, v, 0) for j, v in enumerate(values))


def dot(a, b, ca, cb):
    return lax.dot_general(a, b, (((ca,), (cb,)), ((), ())), preferred_element_type=F32)


def dot3(ah, al, bh, bl, ca, cb):
    return dot(ah, bh, ca, cb) + (dot(ah, bl, ca, cb) + dot(al, bh, ca, cb))


class Wires:
    def __init__(self, send_sem, recv_sem):
        self.send_sem, self.recv_sem = send_sem, recv_sem
        self.sent, self.n_recv, self.arrivals = [], 0, {}

    def open(self, key, ref, *index):
        self.arrivals[key] = (ref, index, self.n_recv)
        self.n_recv += 1

    def send(self, src, key, dev):
        dst, index, n = self.arrivals[key]
        dst = dst.at[index]
        s = len(self.sent)
        cp = pltpu.make_async_remote_copy(
            src_ref=src,
            dst_ref=dst,
            send_sem=self.send_sem.at[s],
            recv_sem=self.recv_sem.at[n],
            device_id=dev,
            device_id_type=MESH,
        )
        cp.start()
        self.sent.append(dst.shape)

    def wait(self, key):
        dst, index, n = self.arrivals.pop(key)
        dst = dst.at[index]
        pltpu.make_async_copy(dst, dst, self.recv_sem.at[n]).wait()
        return dst

    def need(self, *keys):
        for key in keys:
            if key in self.arrivals:
                self.wait(key)

    def flush(self, like):
        for s, shape in enumerate(self.sent):
            ref = like(shape)
            pltpu.make_async_copy(ref, ref, self.send_sem.at[s]).wait()
        self.sent = []


def merge(parts):
    top = functools.reduce(jnp.maximum, [m for m, _ in parts])
    total = sum(s * jnp.exp2(m - top) for m, s in parts)
    return top, total


def kernel(
    scale_ref, img_ref, txt_ref,
    loss_ref, img_out, txt_out,
    Ib, Tb, Ih, Il, Th, Tl, L,
    P8h, P8l, I8h, I8l, T8h, T8l,
    row_m, row_s, col_m, col_s, rst, cst, acc, lbuf,
    iland, tland, eye,
    send_sem, recv_sem, local_sem,
):
    i, t = lax.axis_index("img"), lax.axis_index("txt")
    x, k = t // 2, t % 2
    z, y = i // 4, i % 4
    even = 1 - 2 * (y % 2)

    def dev(dx=0, dy=0, dz=0, dk=0):
        return (((z + dz) % 4) * 4 + (y + dy + 4) % 4, ((x + dx) % 4) * 2 + (k + dk) % 2)

    sib = dev(dk=1)
    xs = {1: dev(dx=1), -1: dev(dx=3), 2: dev(dx=2)}
    zs = {1: dev(dz=1), -1: dev(dz=3), 2: dev(dz=2)}
    yi, yt = dev(dy=even), dev(dy=-even)
    row_peers = [*xs.values(), yi, *(dev(dx=d, dy=even) for d in (1, 3, 2))]
    col_peers = [sib, yt, dev(dy=-even, dk=1)]
    peers = [*row_peers, *col_peers, *zs.values()]
    barrier = pltpu.get_barrier_semaphore()
    for peer in peers:
        pl.semaphore_signal(barrier, inc=1, device_id=peer, device_id_type=MESH)
    pl.semaphore_wait(barrier, len(peers))

    w = Wires(send_sem, recv_sem)

    def like(shape):
        if shape[-1] == E:
            return Ib.at[0, pl.ds(0, shape[0])]
        return {2: lbuf, 3: rst if shape[-2] == 8 else cst}[len(shape)].at[0]

    lo, hi = pl.ds(0, HALF), pl.ds(HALF, HALF)
    ring = {"I": xs, "T": zs}
    across = {"I": yi, "T": yt}
    own = {"I": img_ref, "T": txt_ref}

    def place(name, q, p):
        return (Ib, 2 * q + p) if name == "I" else (Tb, 4 * q + 2 * p)

    for name in "IT":
        for q in range(4):
            for p in range(2):
                if (q, p) == (0, 0):
                    continue
                w.open((name + "A", q, p), *place(name, q, p), lo)
                if (q, p) == (3, 0):
                    for n in range(2):
                        w.open((name + "B", 3, 0, n), *place(name, 3, 0), pl.ds(HALF + 32 * n, 32))
                else:
                    w.open((name + "B", q, p), *place(name, q, p), hi)
    for q in range(4):
        for p in range(2):
            w.open(("S", q, p), Tb, 4 * q + 2 * p + 1)

    def keys_of(name, q, p, parts="AB"):
        return [(name + part, q, p, *n) for part in parts for n in ((), (0,), (1,))]

    def block(name, q, p, rows):
        if (q, p) == (0, 0):
            return own[name].at[rows]
        ref, n = place(name, q, p)
        return ref.at[n, rows]

    def gather_send(key):
        if key[0] == "S":
            q, p = key[1:]
            w.need(*keys_of("T", q, p))
            w.send(block("T", q, p, pl.ds(0, ROWS)), key, sib)
            return
        name, part, q, p = key[0][0], key[0][1], key[1], key[2]
        rows = lo if part == "A" else hi
        if part == "A" and p == 1 and q == 0:
            source, dst = (0, 0), across[name]
        elif part == "B" and p == 1:
            source, dst = (q, 0), across[name]
        elif len(key) == 4:
            source, dst = (2 - key[3], 0), ring[name][1 - 2 * key[3]]
            rows = pl.ds(HALF + 32 * key[3], 32)
        elif q == 3:
            source, dst = (2 - p, p), ring[name][1 - 2 * p]
        else:
            source, dst = (0, p), ring[name][1 if q == 2 else -1]
        w.need(*keys_of(name, *source, part))
        w.send(block(name, *source, rows), key, dst)

    own_t = pltpu.make_async_copy(txt_ref, Tb.at[0], local_sem.at[0])
    own_i = pltpu.make_async_copy(img_ref, Ib.at[0], local_sem.at[1])
    for key in GATHER[0][:13]:
        gather_send(key)
    own_t.start()
    own_i.start()

    rows_iota = lax.broadcasted_iota(jnp.int32, (ROWS, ROWS), 0)
    cols_iota = lax.broadcasted_iota(jnp.int32, (ROWS, ROWS), 1)
    eye[...] = (rows_iota == cols_iota).astype(F32)
    row_m[...] = jnp.full((IMG, 128), -jnp.inf, F32)
    row_s[...] = jnp.zeros((IMG, 128), F32)
    col_m[...] = jnp.full((8, TXT), -jnp.inf, F32)
    col_s[...] = jnp.zeros((8, TXT), F32)

    def split_rows(src, first, count, high, low):
        def body(b, carry):
            n = first + b // 4
            o = pl.ds(pl.multiple_of(first * ROWS + b * 32, 32), 32)
            v = src[n, pl.ds(pl.multiple_of((b % 4) * 32, 32), 32), :]
            h = v.astype(BF16)
            high[o, :] = h
            low[o, :] = (v - h.astype(F32)).astype(BF16)
            return carry

        lax.fori_loop(0, 4 * count, body, 0)

    own_i.wait()
    own_t.wait()
    for key in GATHER[0][13:]:
        gather_send(key)

    s2 = scale_ref[0] * LOG2E
    seen_i = [int(qi not in [a for a, _ in TILES[:n]]) for n, (qi, _) in enumerate(TILES)]
    seen_t = [int(qt not in [b for _, b in TILES[:n]]) for n, (_, qt) in enumerate(TILES)]

    def tile_at(n):
        return pick(n, [qi for qi, _ in TILES]), pick(n, [qt for _, qt in TILES])

    def logits(a, b):
        rows = pl.ds(pl.multiple_of(a * 256, 256), 256)
        cols = pl.ds(pl.multiple_of(b * 512, 512), 512)
        L[rows, cols] = s2 * dot3(Ih[rows, :], Il[rows, :], Th[cols, :], Tl[cols, :], 1, 1)

    def statistics(n):
        a, b = tile_at(n)
        cols = pl.ds(pl.multiple_of(b * 512, 512), 512)
        old = col_m[:, cols]
        top = old
        some = [pl.ds(pl.multiple_of(a * 256 + CHUNK * c, CHUNK), CHUNK) for c in range(256 // CHUNK)]
        for r in some:
            v = L[r, cols]
            vs = [v[:, 128 * j : 128 * j + 128] for j in range(4)]
            was = row_m[r, :]
            new = functools.reduce(jnp.maximum, vs, was)
            row_s[r, :] = row_s[r, :] * jnp.exp2(was - new) + sum(jnp.exp2(u - new) for u in vs)
            row_m[r, :] = new
            top = jnp.maximum(top, jnp.max(v.reshape(CHUNK // 8, 8, 512), axis=0))
        total = col_s[:, cols] * jnp.exp2(old - top)
        for r in some:
            v = L[r, cols].reshape(CHUNK // 8, 8, 512)
            total = total + jnp.sum(jnp.exp2(v - top[None]), axis=0)
        col_s[:, cols] = total
        col_m[:, cols] = top

    def tile(n, carry):
        for m, (qi, qt) in enumerate(TILES):

            @pl.when(n == m)
            def _():
                if m > 0:
                    for key in GATHER[m]:
                        gather_send(key)
                for p in range(2):
                    w.need(*keys_of("I", qi, p), *keys_of("T", qt, p), ("S", qt, p))

        a, b = tile_at(n)

        @pl.when(pick(n, seen_i) == 1)
        def _():
            split_rows(Ib, 2 * a, 2, Ih, Il)

        @pl.when(pick(n, seen_t) == 1)
        def _():
            split_rows(Tb, 4 * b, 4, Th, Tl)

        @pl.when(n > 0)
        def _():
            statistics(n - 1)
            logits(a, b)

        @pl.when(n == 0)
        def _():
            logits(a, b)

        return carry

    lax.fori_loop(0, len(TILES), tile, 0)
    statistics(len(TILES) - 1)

    def step_of(q):
        return q + q // 2 - 2 * (q // 3)

    def img_block(s):
        return ((x + step_of(s // 2)) % 4) * 2 + (y + s % 2) % 2

    def txt_block(s):
        return (((z + step_of(s // 4)) % 4) * 2 + (y + (s // 2) % 2) % 2) * 2 + (k + s % 2) % 2

    def fold_cols(s, carry):
        c = pl.ds(pl.multiple_of(s * ROWS, ROWS), ROWS)
        m8 = col_m[:, c]
        m1 = jnp.max(m8, axis=0, keepdims=True)
        at = pl.ds(txt_block(s), 1)
        cst[0, 0, at, :] = m1
        cst[0, 1, at, :] = jnp.sum(col_s[:, c] * jnp.exp2(m8 - m1), axis=0, keepdims=True)
        return carry

    def fold_rows(s, carry):
        r = pl.ds(pl.multiple_of(s * ROWS, ROWS), ROWS)
        mt, st = row_m[r, :].T, row_s[r, :].T
        m1 = jnp.max(mt, axis=0, keepdims=True)
        at = pl.ds(img_block(s), 1)
        rst[0, 0, at, :] = m1
        rst[0, 1, at, :] = jnp.sum(st * jnp.exp2(mt - m1), axis=0, keepdims=True)
        return carry

    lax.fori_loop(0, 16, fold_cols, 0)
    w.flush(like)
    assert not w.arrivals
    for n in range(7):
        w.open(("r", n), rst, 1 + n)
    for n in range(3):
        w.open(("c1", n), cst, 1 + n)
        w.open(("c2", n), cst, 5 + n)
    for n in range(3):
        w.send(cst.at[0], ("c1", n), col_peers[n])
    lax.fori_loop(0, 8, fold_rows, 0)
    for n in range(7):
        w.send(rst.at[0], ("r", n), row_peers[n])
    def largest(src, count):
        def body(b, top):
            v = jnp.abs(src[pl.ds(pl.multiple_of(b * 64, 64), 64), :]).astype(F32)
            return jnp.maximum(top, jnp.max(v.reshape(8, 8, E), axis=0))

        return jnp.max(lax.fori_loop(0, count // 64, body, jnp.zeros((8, E), F32)))

    i_scale = 240.0 / jnp.maximum(largest(Ih, IMG), 1e-30)
    t_scale = 240.0 / jnp.maximum(largest(Th, TXT), 1e-30)

    def to_eight(high, low, count, scale, high8, low8):
        def body(b, carry):
            r = pl.ds(pl.multiple_of(b * 64, 64), 64)
            high8[r, :] = (high[r, :].astype(F32) * scale).astype(F8)
            low8[r, :] = (low[r, :].astype(F32) * (256.0 * scale)).astype(F8)
            return carry

        lax.fori_loop(0, count // 64, body, 0)

    for n in range(3):
        w.wait(("c1", n))
    cst[4, 0], cst[4, 1] = merge([(cst[n, 0], cst[n, 1]) for n in range(4)])
    for n, d in enumerate((1, -1, 2)):
        w.send(cst.at[4], ("c2", n), zs[d])
    to_eight(Ih, Il, IMG, i_scale, I8h, I8l)
    to_eight(Th, Tl, TXT, t_scale, T8h, T8l)
    for n in range(7):
        w.wait(("r", n))
    m, s = merge([(rst[n, 0], rst[n, 1]) for n in range(8)])
    row_lse = m + jnp.log2(s)
    rst[8, 0] = row_lse + 1.0

    def spread(s, carry):
        r = pl.ds(pl.multiple_of(s * ROWS, ROWS), ROWS)
        v = rst[8, 0, pl.ds(img_block(s), 1), :]
        row_m[r, :] = jnp.broadcast_to(v, (ROWS, 128)).T
        return carry

    lax.fori_loop(0, 8, spread, 0)
    for n in range(3):
        w.wait(("c2", n))
    m, s = merge([(cst[n, 0], cst[n, 1]) for n in range(4, 8)])
    col_lse = m + jnp.log2(s)
    w.flush(like)
    cst[8, 0] = col_lse + 1.0
    acc[...] = jnp.full((8, 128), LN2 * (jnp.sum(row_lse) / 8 + jnp.sum(col_lse) / 16), F32)

    for name, land in (("I", iland), ("T", tland)):
        for p in range(2):
            w.open((name + "A", "P", p), land, p)
            for n, d in enumerate((1, -1)):
                w.open((name + "A", "D", p, d), land, 2 + 2 * p + n)
        w.open((name + "A", "2"), land, 6)
        for q in range(4):
            w.open((name + "B", "Y", q), land, 7 + q)
        for n, d in enumerate((1, -1)):
            w.open((name + "B", "P", d), land, 11, pl.ds(32 * n, 32))
            w.open((name + "B", "D", d), land, 12 + n)
    for q in range(4):
        for p in range(2):
            w.open(("S", q, p), Ib, 2 * q + p)
    for n in range(7):
        w.open(("l1", n), lbuf, 1 + n)
    for n in range(3):
        w.open(("l2", n), lbuf, 9 + n)
        w.open(("l3", n), lbuf, 13 + n)

    def add(dst, srcs, rows, out=None):
        step = 16

        def body(b, carry):
            r = pl.ds(pl.multiple_of(b * step, step), step)
            v = dst[r, :]
            for src in srcs:
                v = v + src[r, :]
            (dst if out is None else out)[r, :] = v
            return carry

        lax.fori_loop(0, rows // step, body, 0)

    summed = set()

    def sums(name, q, p, at, rows):
        if name == "I":
            return L.at[pl.ds((2 * q + p) * ROWS + at, rows), pl.ds(0, E)]
        if (q, p) not in summed:
            summed.add((q, p))
            add(Tb.at[4 * q + 2 * p], [w.wait(("S", q, p))], ROWS)
        return Tb.at[4 * q + 2 * p, pl.ds(at, rows)]

    def back_send(key):
        if key[0] == "S":
            q, p = key[1:]
            w.send(Tb.at[4 * q + 2 * p + 1], key, sib)
            return
        name, kind = key[0][0], key[1]
        way, part = ring[name], key[0]
        if part == name:
            out = img_out if name == "I" else txt_out
            A, B = name + "A", name + "B"
            srcs = [w.wait((A, "D", 0, 1)), w.wait((A, "D", 0, -1)), w.wait((A, "2"))]
            add(sums(name, 0, 0, 0, HALF), srcs, HALF, out.at[lo])
            srcs = [w.wait((B, "Y", 0)), w.wait((B, "D", 1)), w.wait((B, "D", -1))]
            add(sums(name, 0, 0, HALF, HALF), srcs, HALF, out.at[hi])
        elif part[1] == "A":
            if kind == "P":
                w.send(sums(name, 3, key[2], 0, HALF), key, way[2 * key[2] - 1])
            elif kind == "D":
                p, d = key[2:]
                mine = sums(name, 2 if d == 1 else 1, p, 0, HALF)
                if p == (1 - d) // 2:
                    add(mine, [w.wait((part, "P", p))], HALF)
                w.send(mine, key, way[-d])
            else:
                mine = sums(name, 0, 1, 0, HALF)
                add(mine, [w.wait((part, "D", 1, 1)), w.wait((part, "D", 1, -1))], HALF)
                w.send(mine, key, across[name])
        elif kind == "Y":
            w.send(sums(name, key[2], 1, HALF, HALF), key, across[name])
        elif kind == "P":
            d = key[2]
            if (name, "far") not in summed:
                summed.add((name, "far"))
                add(sums(name, 3, 0, HALF, HALF), [w.wait((part, "Y", 3))], HALF)
            w.send(sums(name, 3, 0, HALF if d == 1 else HALF + 32, 32), key, way[-d])
        else:
            d = key[2]
            q = 2 if d == 1 else 1
            mine = sums(name, q, 0, HALF, HALF)
            add(mine, [w.wait((part, "Y", q))], HALF)
            add(mine.at[pl.ds(0 if d == 1 else 32, 32)], [w.wait((part, "P", d))], 32)
            w.send(mine, key, way[-d])

    lbuf[0] = jnp.zeros((8, 128), F32)

    def put_grad(g, r, c, width):
        first, size = r
        h = g.astype(BF16)
        rows = pl.ds(pl.multiple_of(first, ROWS), size)
        cols = pl.ds(pl.multiple_of(c, ROWS), width)
        below = pl.ds(pl.multiple_of(first + (c // IMG) * IMG, ROWS), size)
        Tl[below, pl.ds(pl.multiple_of(c % IMG, ROWS), width)] = h
        hf = h.astype(F32)
        P8h[rows, cols] = (hf * 256.0).astype(F8)
        P8l[rows, cols] = ((g - hf) * 65536.0).astype(F8)

    def soften(n, carry):
        p = pick(n, [m for kind, m in STEPS if kind == "t"])
        cols = pl.ds(pl.multiple_of(p * 256, 256), 256)
        cl = jnp.concatenate([cst[8, 0, pl.ds(txt_block(2 * p + j), 1), :] for j in range(2)], axis=1)

        def soft(b, inner):
            r = pl.ds(pl.multiple_of(b * ROWS, ROWS), ROWS)
            v = L[r, cols]
            rl = row_m[r, :]
            g = jnp.exp2(v - jnp.concatenate([rl, rl], axis=1)) + jnp.exp2(v - cl)
            put_grad(g, (b * ROWS, ROWS), p * 256, 256)
            return inner

        lax.fori_loop(0, IMG // ROWS, soft, 0)
        for j in range(2):
            s = 2 * p + j
            owner = (x * 2 + (k + j) % 2) * 16 + ((z + step_of(s // 4)) % 4) * 4
            owner = owner + (y + ((s // 2) % 2) * (4 - even)) % 4
            bi, bt = owner // 8, owner % 8

            @pl.when((bi // 4 == z) & ((bi % 4) // 2 == y // 2) & (bt % 2 == k))
            def _():
                u = step_of((bt // 2 + 4 - x) % 4) * 2 + (bi + y) % 2
                r = pl.ds(pl.multiple_of(u * ROWS, ROWS), ROWS)
                c = pl.ds(pl.multiple_of(s * ROWS, ROWS), ROWS)
                v = L[r, c]
                g = jnp.exp2(v - row_m[r, :]) + jnp.exp2(v - cl[:, 128 * j : 128 * j + 128]) - eye[...]
                put_grad(g, (u * ROWS, ROWS), s * ROWS, ROWS)
                lbuf[0] += jnp.sum((v * eye[...]).reshape(ROWS // 8, 8, 128), axis=0)

        return carry

    def loss_send(m):
        if m == FIRST_IMAGE:
            total = jnp.sum(acc[...]) / 1024 - 2.0 * LN2 * jnp.sum(lbuf[0])
            lbuf[0] = jnp.full((8, 128), total, F32)
            for n in range(7):
                w.send(lbuf.at[0], ("l1", n), row_peers[n])
        if m == FIRST_IMAGE + 3:
            for n in range(7):
                w.wait(("l1", n))
            lbuf[8] = sum(lbuf[n] for n in range(8))
            for n in range(3):
                w.send(lbuf.at[8], ("l2", n), col_peers[n])
        if m == FIRST_IMAGE + 6:
            for n in range(3):
                w.wait(("l2", n))
            lbuf[12] = sum(lbuf[n] for n in range(8, 12))
            for n, d in enumerate((1, -1, 2)):
                w.send(lbuf.at[12], ("l3", n), zs[d])

    def back_step(n, carry):
        is_text = pick(n, [int(kind == "t") for kind, _ in STEPS])
        arg = pick(n, [a for _, a in STEPS])
        lax.fori_loop(pick(n, SOFT[:-1]), pick(n, SOFT[1:]), soften, 0)

        @pl.when(is_text == 1)
        def _():
            cols = pl.ds(pl.multiple_of(arg * 256, 256), 256)
            below = pl.ds(pl.multiple_of((arg // 4) * IMG, IMG), IMG)
            high = dot(Tl[below, pl.ds(pl.multiple_of((arg % 4) * 256, 256), 256)], Ih[...], 0, 0)
            cross = dot(P8h[:, cols], I8l[...], 0, 0) + dot(P8l[:, cols], I8h[...], 0, 0)
            res = high + (1.0 / (65536.0 * i_scale)) * cross
            Tb[2 * arg] = res[:ROWS]
            Tb[2 * arg + 1] = res[ROWS:]

        @pl.when(is_text == 0)
        def _():
            r = pl.ds(pl.multiple_of(arg * ROWS, ROWS), ROWS)
            r2 = pl.ds(pl.multiple_of(IMG + arg * ROWS, ROWS), ROWS)
            high = dot(Tl[r, 0:IMG], Th[0:IMG, :], 1, 0) + dot(Tl[r2, 0:IMG], Th[IMG:TXT, :], 1, 0)
            cross = dot(P8h[r, :], T8l[...], 1, 0) + dot(P8l[r, :], T8h[...], 1, 0)
            L[r, 0:E] = high + (1.0 / (65536.0 * t_scale)) * cross

        for m in range(len(STEPS)):

            @pl.when(n == m)
            def _():
                for key in RETURN[m]:
                    back_send(key)
                loss_send(m)

        return carry

    lax.fori_loop(0, len(STEPS), back_step, 0)
    for n in range(3):
        w.wait(("l3", n))
    loss_ref[0] = jnp.sum(sum(lbuf[n] for n in range(12, 16))) / (1024 * 2.0 * 16384)
    w.flush(like)
    assert not w.arrivals


def on_device(image_emb, text_emb, logit_scale):
    vm = pltpu.VMEM
    loss, image_grad, text_grad = pl.pallas_call(
        kernel,
        out_shape=(
            jax.ShapeDtypeStruct((1,), F32),
            jax.ShapeDtypeStruct((ROWS, E), F32),
            jax.ShapeDtypeStruct((ROWS, E), F32),
        ),
        in_specs=[
            pl.BlockSpec(memory_space=pltpu.SMEM),
            pl.BlockSpec(memory_space=pl.ANY),
            pl.BlockSpec(memory_space=pl.ANY),
        ],
        out_specs=[pl.BlockSpec(memory_space=pltpu.SMEM)] + [pl.BlockSpec(memory_space=vm)] * 2,
        scratch_shapes=[
            vm((8, ROWS, E), F32),
            vm((16, ROWS, E), F32),
            vm((IMG, E), BF16),
            vm((IMG, E), BF16),
            vm((TXT, E), BF16),
            vm((TXT, E), BF16),
            vm((IMG, TXT), F32),
            vm((IMG, TXT), F8),
            vm((IMG, TXT), F8),
            vm((IMG, E), F8),
            vm((IMG, E), F8),
            vm((TXT, E), F8),
            vm((TXT, E), F8),
            vm((IMG, 128), F32),
            vm((IMG, 128), F32),
            vm((8, TXT), F32),
            vm((8, TXT), F32),
            vm((9, 2, 8, 128), F32),
            vm((9, 2, 16, 128), F32),
            vm((8, 128), F32),
            vm((16, 8, 128), F32),
            vm((14, HALF, E), F32),
            vm((14, HALF, E), F32),
            vm((ROWS, ROWS), F32),
            pltpu.SemaphoreType.DMA((56,)),
            pltpu.SemaphoreType.DMA((112,)),
            pltpu.SemaphoreType.DMA((2,)),
        ],
        compiler_params=pltpu.CompilerParams(
            collective_id=0, has_side_effects=True, vmem_limit_bytes=63 * 2**20
        ),
        name="contrastive",
    )(logit_scale.reshape(1), image_emb, text_emb)
    return loss.reshape(()), logit_scale * image_grad, logit_scale * text_grad


def solution(mesh):
    in_specs = (P(("img", "txt"), None), P(("txt", "img"), None), P())
    out_specs = (P(), P(("img", "txt"), None), P(("txt", "img"), None))
    return jax.shard_map(
        on_device, mesh=mesh, in_specs=in_specs, out_specs=out_specs, check_vma=False
    )
```

```python
import functools

import jax
import jax.numpy as jnp
from jax import lax
from jax.experimental import pallas as pl
from jax.experimental.pallas import tpu as pltpu
from jax.sharding import PartitionSpec as P

MESH = pl.DeviceIdType.MESH
BF16, F32 = jnp.bfloat16, jnp.float32
LOG2E = 1.4426950408889634
LN2 = 0.6931471805599453

STEP = (0, 1, 3, 2)
F8 = jnp.float8_e4m3fn
ROWS = 128
HALF = ROWS // 2
E = 1280
CHUNK = 64
IMG, TXT = 1024, 2048

TILES = ((0, 0), (1, 0), (0, 2), (1, 2), (2, 0), (2, 2), (0, 1), (1, 1), (2, 1), (3, 0), (3, 1), (3, 2), (0, 3), (1, 3), (2, 3), (3, 3))
GATHER = (
    (("TA", 0, 1), ("TB", 2, 0), ("IB", 2, 0), ("TB", 1, 0), ("IA", 0, 1), ("IB", 1, 0), ("S", 0, 0), ("TB", 0, 1),
     ("TA", 2, 0), ("IA", 2, 0), ("TA", 1, 0), ("IB", 0, 1), ("IA", 1, 0), ("TB", 2, 1), ("TA", 2, 1),
     ("IB", 3, 0, 0), ("TB", 3, 0, 1), ("IB", 1, 1), ("IA", 1, 1), ("TA", 1, 1), ("IA", 2, 1), ("S", 0, 1),
     ("S", 1, 0), ("S", 2, 0), ("TB", 3, 0, 0), ("TB", 1, 1), ("IB", 3, 0, 1), ("IB", 2, 1)),
    (("TA", 3, 0), ("IA", 3, 0), ("S", 2, 1), ("IA", 3, 1)),
    (("TB", 3, 1),),
    (("TA", 3, 1), ("IB", 3, 1)),
    (("S", 1, 1),),
    (),
    (("S", 3, 0),),
    (),
    (("S", 3, 1),),
    (),
    (),
    (),
    (),
    (),
    (),
    (),
    (),
)

STEPS = (("t", 7), ("t", 6), ("i", 7), ("t", 5), ("i", 5), ("t", 3), ("t", 4), ("i", 6), ("i", 3), ("t", 1), ("t", 2), ("i", 2), ("i", 1), ("i", 4), ("t", 0), ("i", 0))
RETURN = (
    (("S", 3, 1),),
    (("S", 3, 0),),
    (("TB", "Y", 3), ("IB", "Y", 3), ("TA", "P", 1), ("IA", "P", 1), ("TA", "P", 0)),
    (("S", 2, 1),),
    (("IA", "D", 1, 1),),
    (("S", 1, 1), ("TB", "Y", 2), ("IB", "Y", 2)),
    (("S", 2, 0), ("TA", "D", 1, 1)),
    (("IB", "P", -1), ("TA", "D", 1, -1), ("IA", "P", 0)),
    (),
    (("S", 0, 1), ("IA", "D", 1, -1), ("TB", "Y", 1), ("TA", "D", 0, 1), ("IB", "Y", 1)),
    (("S", 1, 0), ("TB", "P", -1)),
    (("IB", "P", 1),),
    (("IA", "D", 0, -1), ("TA", "2"), ("TA", "D", 0, -1), ("IB", "Y", 0)),
    (("IA", "D", 0, 1), ("TB", "P", 1)),
    (("S", 0, 0),),
    (("IB", "D", -1), ("TB", "D", -1), ("IA", "2"), ("TB", "Y", 0), ("TB", "D", 1), ("IB", "D", 1), ("T", "F"),
     ("I", "F")),
)


FIRST_IMAGE = [kind for kind, _ in STEPS].index("i")
SOFT = [n if n <= FIRST_IMAGE else 8 for n in range(len(STEPS) + 1)]


def pick(n, values):
    return sum(jnp.where(n == j, v, 0) for j, v in enumerate(values))


def dot(a, b, ca, cb):
    return lax.dot_general(a, b, (((ca,), (cb,)), ((), ())), preferred_element_type=F32)


def dot3(ah, al, bh, bl, ca, cb):
    return dot(ah, bh, ca, cb) + (dot(ah, bl, ca, cb) + dot(al, bh, ca, cb))


class Wires:
    def __init__(self, send_sem, recv_sem):
        self.send_sem, self.recv_sem = send_sem, recv_sem
        self.sent, self.n_recv, self.arrivals = [], 0, {}

    def open(self, key, ref, *index):
        self.arrivals[key] = (ref, index, self.n_recv)
        self.n_recv += 1

    def send(self, src, key, dev):
        dst, index, n = self.arrivals[key]
        dst = dst.at[index]
        s = len(self.sent)
        cp = pltpu.make_async_remote_copy(
            src_ref=src,
            dst_ref=dst,
            send_sem=self.send_sem.at[s],
            recv_sem=self.recv_sem.at[n],
            device_id=dev,
            device_id_type=MESH,
        )
        cp.start()
        self.sent.append(dst.shape)

    def wait(self, key):
        dst, index, n = self.arrivals.pop(key)
        dst = dst.at[index]
        pltpu.make_async_copy(dst, dst, self.recv_sem.at[n]).wait()
        return dst

    def need(self, *keys):
        for key in keys:
            if key in self.arrivals:
                self.wait(key)

    def flush(self, like):
        for s, shape in enumerate(self.sent):
            ref = like(shape)
            pltpu.make_async_copy(ref, ref, self.send_sem.at[s]).wait()
        self.sent = []


def merge(parts):
    top = functools.reduce(jnp.maximum, [m for m, _ in parts])
    total = sum(s * jnp.exp2(m - top) for m, s in parts)
    return top, total


def kernel(
    scale_ref, img_ref, txt_ref,
    loss_ref, img_out, txt_out,
    Ib, Tb, Ih, Il, Th, Tl, L,
    P8h, P8l, I8h, I8l, T8h, T8l,
    row_m, row_s, col_m, col_s, rst, cst, lbuf,
    iland, tland, eye,
    send_sem, recv_sem, local_sem,
):
    i, t = lax.axis_index("img"), lax.axis_index("txt")
    x, k = t // 2, t % 2
    z, y = i // 4, i % 4
    even = 1 - 2 * (y % 2)

    def dev(dx=0, dy=0, dz=0, dk=0):
        return (((z + dz) % 4) * 4 + (y + dy + 4) % 4, ((x + dx) % 4) * 2 + (k + dk) % 2)

    sib = dev(dk=1)
    xs = {1: dev(dx=1), -1: dev(dx=3), 2: dev(dx=2)}
    zs = {1: dev(dz=1), -1: dev(dz=3), 2: dev(dz=2)}
    yi, yt = dev(dy=even), dev(dy=-even)
    row_peers = [*xs.values(), yi, *(dev(dx=d, dy=even) for d in (1, 3, 2))]
    col_peers = [sib, yt, dev(dy=-even, dk=1)]
    peers = [*row_peers, *col_peers, *zs.values()]
    barrier = pltpu.get_barrier_semaphore()
    for peer in peers:
        pl.semaphore_signal(barrier, inc=1, device_id=peer, device_id_type=MESH)
    pl.semaphore_wait(barrier, len(peers))

    w = Wires(send_sem, recv_sem)

    def like(shape):
        if shape[-1] == E:
            return Ib.at[0, pl.ds(0, shape[0])]
        return {2: lbuf, 3: rst if shape[-2] == 8 else cst}[len(shape)].at[0]

    lo, hi = pl.ds(0, HALF), pl.ds(HALF, HALF)
    ring = {"I": xs, "T": zs}
    across = {"I": yi, "T": yt}
    own = {"I": img_ref, "T": txt_ref}

    def place(name, q, p):
        return (Ib, 2 * q + p) if name == "I" else (Tb, 4 * q + 2 * p)

    for name in "IT":
        for q in range(4):
            for p in range(2):
                if (q, p) == (0, 0):
                    continue
                w.open((name + "A", q, p), *place(name, q, p), lo)
                if (q, p) == (3, 0):
                    for n in range(2):
                        w.open((name + "B", 3, 0, n), *place(name, 3, 0), pl.ds(HALF + 32 * n, 32))
                else:
                    w.open((name + "B", q, p), *place(name, q, p), hi)
    for q in range(4):
        for p in range(2):
            w.open(("S", q, p), Tb, 4 * q + 2 * p + 1)

    def keys_of(name, q, p, parts="AB"):
        return [(name + part, q, p, *n) for part in parts for n in ((), (0,), (1,))]

    def block(name, q, p, rows):
        if (q, p) == (0, 0):
            return own[name].at[rows]
        ref, n = place(name, q, p)
        return ref.at[n, rows]

    def gather_send(key):
        if key[0] == "S":
            q, p = key[1:]
            w.need(*keys_of("T", q, p))
            w.send(block("T", q, p, pl.ds(0, ROWS)), key, sib)
            return
        name, part, q, p = key[0][0], key[0][1], key[1], key[2]
        rows = lo if part == "A" else hi
        if part == "A" and p == 1 and q == 0:
            source, dst = (0, 0), across[name]
        elif part == "B" and p == 1:
            source, dst = (q, 0), across[name]
        elif len(key) == 4:
            source, dst = (2 - key[3], 0), ring[name][1 - 2 * key[3]]
            rows = pl.ds(HALF + 32 * key[3], 32)
        elif q == 3:
            source, dst = (2 - p, p), ring[name][1 - 2 * p]
        else:
            source, dst = (0, p), ring[name][1 if q == 2 else -1]
        w.need(*keys_of(name, *source, part))
        w.send(block(name, *source, rows), key, dst)

    own_t = pltpu.make_async_copy(txt_ref, Tb.at[0], local_sem.at[0])
    own_i = pltpu.make_async_copy(img_ref, Ib.at[0], local_sem.at[1])
    for key in GATHER[0][:13]:
        gather_send(key)
    own_t.start()
    own_i.start()

    rows_iota = lax.broadcasted_iota(jnp.int32, (ROWS, ROWS), 0)
    cols_iota = lax.broadcasted_iota(jnp.int32, (ROWS, ROWS), 1)
    eye[...] = (rows_iota == cols_iota).astype(F32)
    row_m[...] = jnp.full((IMG, 128), -jnp.inf, F32)
    row_s[...] = jnp.zeros((IMG, 128), F32)
    col_m[...] = jnp.full((8, TXT), -jnp.inf, F32)
    col_s[...] = jnp.zeros((8, TXT), F32)

    def split_rows(src, first, count, high, low):
        def body(b, carry):
            n = first + b // 4
            o = pl.ds(pl.multiple_of(first * ROWS + b * 32, 32), 32)
            v = src[n, pl.ds(pl.multiple_of((b % 4) * 32, 32), 32), :]
            h = v.astype(BF16)
            high[o, :] = h
            low[o, :] = (v - h.astype(F32)).astype(BF16)
            return carry

        lax.fori_loop(0, 4 * count, body, 0)

    own_i.wait()
    own_t.wait()
    for key in GATHER[0][13:]:
        gather_send(key)

    s2 = scale_ref[0] * LOG2E
    seen_i = [int(qi not in [a for a, _ in TILES[:n]]) for n, (qi, _) in enumerate(TILES)]
    seen_t = [int(qt not in [b for _, b in TILES[:n]]) for n, (_, qt) in enumerate(TILES)]

    def tile_at(n):
        return pick(n, [qi for qi, _ in TILES]), pick(n, [qt for _, qt in TILES])

    def logits(a, b):
        rows = pl.ds(pl.multiple_of(a * 256, 256), 256)
        cols = pl.ds(pl.multiple_of(b * 512, 512), 512)
        L[rows, cols] = s2 * dot3(Ih[rows, :], Il[rows, :], Th[cols, :], Tl[cols, :], 1, 1)

    def statistics(n):
        a, b = tile_at(n)
        cols = pl.ds(pl.multiple_of(b * 512, 512), 512)
        old = col_m[:, cols]
        top = old
        some = [pl.ds(pl.multiple_of(a * 256 + CHUNK * c, CHUNK), CHUNK) for c in range(256 // CHUNK)]
        for r in some:
            v = L[r, cols]
            vs = [v[:, 128 * j : 128 * j + 128] for j in range(4)]
            was = row_m[r, :]
            new = functools.reduce(jnp.maximum, vs, was)
            row_s[r, :] = row_s[r, :] * jnp.exp2(was - new) + sum(jnp.exp2(u - new) for u in vs)
            row_m[r, :] = new
            top = jnp.maximum(top, jnp.max(v.reshape(CHUNK // 8, 8, 512), axis=0))
        total = col_s[:, cols] * jnp.exp2(old - top)
        for r in some:
            v = L[r, cols].reshape(CHUNK // 8, 8, 512)
            total = total + jnp.sum(jnp.exp2(v - top[None]), axis=0)
        col_s[:, cols] = total
        col_m[:, cols] = top

    def tile(n, carry):
        for m, (qi, qt) in enumerate(TILES):

            @pl.when(n == m)
            def _():
                if m > 0:
                    for key in GATHER[m]:
                        gather_send(key)
                for p in range(2):
                    w.need(*keys_of("I", qi, p), *keys_of("T", qt, p), ("S", qt, p))

        a, b = tile_at(n)

        @pl.when(pick(n, seen_i) == 1)
        def _():
            split_rows(Ib, 2 * a, 2, Ih, Il)

        @pl.when(pick(n, seen_t) == 1)
        def _():
            split_rows(Tb, 4 * b, 4, Th, Tl)

        @pl.when(n > 0)
        def _():
            statistics(n - 1)
            logits(a, b)

        @pl.when(n == 0)
        def _():
            logits(a, b)

        return carry

    lax.fori_loop(0, len(TILES), tile, 0)
    statistics(len(TILES) - 1)

    def step_of(q):
        return q + q // 2 - 2 * (q // 3)

    def img_block(s):
        return ((x + step_of(s // 2)) % 4) * 2 + (y + s % 2) % 2

    def txt_block(s):
        return (((z + step_of(s // 4)) % 4) * 2 + (y + (s // 2) % 2) % 2) * 2 + (k + s % 2) % 2

    def on_diagonal(s):
        owner = (x * 2 + (k + s % 2) % 2) * 16 + ((z + step_of(s // 4)) % 4) * 4
        owner = owner + (y + ((s // 2) % 2) * (4 - even)) % 4
        bi, bt = owner // 8, owner % 8
        here = (bi // 4 == z) & ((bi % 4) // 2 == y // 2) & (bt % 2 == k)
        return here, step_of((bt // 2 + 4 - x) % 4) * 2 + (bi + y) % 2

    def sum_diagonal(s, carry):
        here, u = on_diagonal(s)

        @pl.when(here)
        def _():
            r = pl.ds(pl.multiple_of(u * ROWS, ROWS), ROWS)
            v = L[r, pl.ds(pl.multiple_of(s * ROWS, ROWS), ROWS)]
            lbuf[0] += jnp.sum((v * eye[...]).reshape(ROWS // 8, 8, 128), axis=0)

        return carry

    def fold_cols(s, carry):
        c = pl.ds(pl.multiple_of(s * ROWS, ROWS), ROWS)
        m8 = col_m[:, c]
        m1 = jnp.max(m8, axis=0, keepdims=True)
        at = pl.ds(txt_block(s), 1)
        cst[0, 0, at, :] = m1
        cst[0, 1, at, :] = jnp.sum(col_s[:, c] * jnp.exp2(m8 - m1), axis=0, keepdims=True)
        return carry

    def fold_rows(s, carry):
        r = pl.ds(pl.multiple_of(s * ROWS, ROWS), ROWS)
        mt, st = row_m[r, :].T, row_s[r, :].T
        m1 = jnp.max(mt, axis=0, keepdims=True)
        at = pl.ds(img_block(s), 1)
        rst[0, 0, at, :] = m1
        rst[0, 1, at, :] = jnp.sum(st * jnp.exp2(mt - m1), axis=0, keepdims=True)
        return carry

    lax.fori_loop(0, 16, fold_cols, 0)
    w.flush(like)
    assert not w.arrivals
    for n in range(7):
        w.open(("r", n), rst, 1 + n)
    for n in range(3):
        w.open(("c1", n), cst, 1 + n)
        w.open(("c2", n), cst, 5 + n)
    for n in range(3):
        w.send(cst.at[0], ("c1", n), col_peers[n])
    lax.fori_loop(0, 8, fold_rows, 0)
    for n in range(7):
        w.send(rst.at[0], ("r", n), row_peers[n])
    def largest(src, count):
        def body(b, top):
            v = jnp.abs(src[pl.ds(pl.multiple_of(b * 64, 64), 64), :]).astype(F32)
            return jnp.maximum(top, jnp.max(v.reshape(8, 8, E), axis=0))

        return jnp.max(lax.fori_loop(0, count // 64, body, jnp.zeros((8, E), F32)))

    i_scale = 240.0 / jnp.maximum(largest(Ih, IMG), 1e-30)
    t_scale = 240.0 / jnp.maximum(largest(Th, TXT), 1e-30)

    def to_eight(high, low, count, scale, high8, low8):
        def body(b, carry):
            r = pl.ds(pl.multiple_of(b * 64, 64), 64)
            high8[r, :] = (high[r, :].astype(F32) * scale).astype(F8)
            low8[r, :] = (low[r, :].astype(F32) * (256.0 * scale)).astype(F8)
            return carry

        lax.fori_loop(0, count // 64, body, 0)

    for n in range(3):
        w.wait(("c1", n))
    cst[4, 0], cst[4, 1] = merge([(cst[n, 0], cst[n, 1]) for n in range(4)])
    for n, d in enumerate((1, -1, 2)):
        w.send(cst.at[4], ("c2", n), zs[d])
    to_eight(Ih, Il, IMG, i_scale, I8h, I8l)
    to_eight(Th, Tl, TXT, t_scale, T8h, T8l)
    lbuf[0] = jnp.zeros((8, 128), F32)
    lax.fori_loop(0, 16, sum_diagonal, 0)
    for n in range(7):
        w.wait(("r", n))
    m, s = merge([(rst[n, 0], rst[n, 1]) for n in range(8)])
    row_lse = m + jnp.log2(s)
    rst[8, 0] = row_lse + 1.0

    def spread(s, carry):
        r = pl.ds(pl.multiple_of(s * ROWS, ROWS), ROWS)
        v = rst[8, 0, pl.ds(img_block(s), 1), :]
        row_m[r, :] = jnp.broadcast_to(v, (ROWS, 128)).T
        return carry

    lax.fori_loop(0, 8, spread, 0)
    for n in range(3):
        w.wait(("c2", n))
    m, s = merge([(cst[n, 0], cst[n, 1]) for n in range(4, 8)])
    col_lse = m + jnp.log2(s)
    w.flush(like)
    cst[8, 0] = col_lse + 1.0
    share = jnp.sum(row_lse) / 8 + jnp.sum(col_lse) / 16 - 2.0 * jnp.sum(lbuf[0])
    lbuf[0] = jnp.full((8, 128), LN2 * share, F32)
    for n in range(7):
        w.open(("l1", n), lbuf, 1 + n)
    for n in range(3):
        w.open(("l2", n), lbuf, 9 + n)
        w.open(("l3", n), lbuf, 13 + n)
    for n in range(7):
        w.send(lbuf.at[0], ("l1", n), row_peers[n])

    for name, land in (("I", iland), ("T", tland)):
        for p in range(2):
            w.open((name + "A", "P", p), land, p)
            for n, d in enumerate((1, -1)):
                w.open((name + "A", "D", p, d), land, 2 + 2 * p + n)
        w.open((name + "A", "2"), land, 6)
        for q in range(4):
            w.open((name + "B", "Y", q), land, 7 + q)
        for n, d in enumerate((1, -1)):
            w.open((name + "B", "P", d), land, 11, pl.ds(32 * n, 32))
            w.open((name + "B", "D", d), land, 12 + n)
    for q in range(4):
        for p in range(2):
            w.open(("S", q, p), Ib, 2 * q + p)
    def add(dst, srcs, rows, out=None):
        step = 16

        def body(b, carry):
            r = pl.ds(pl.multiple_of(b * step, step), step)
            v = dst[r, :]
            for src in srcs:
                v = v + src[r, :]
            (dst if out is None else out)[r, :] = v
            return carry

        lax.fori_loop(0, rows // step, body, 0)

    summed = set()

    def sums(name, q, p, at, rows):
        if name == "I":
            return L.at[pl.ds((2 * q + p) * ROWS + at, rows), pl.ds(0, E)]
        if (q, p) not in summed:
            summed.add((q, p))
            add(Tb.at[4 * q + 2 * p], [w.wait(("S", q, p))], ROWS)
        return Tb.at[4 * q + 2 * p, pl.ds(at, rows)]

    def back_send(key):
        if key[0] == "S":
            q, p = key[1:]
            w.send(Tb.at[4 * q + 2 * p + 1], key, sib)
            return
        name, kind = key[0][0], key[1]
        way, part = ring[name], key[0]
        if part == name:
            out = img_out if name == "I" else txt_out
            A, B = name + "A", name + "B"
            srcs = [w.wait((A, "D", 0, 1)), w.wait((A, "D", 0, -1)), w.wait((A, "2"))]
            add(sums(name, 0, 0, 0, HALF), srcs, HALF, out.at[lo])
            srcs = [w.wait((B, "Y", 0)), w.wait((B, "D", 1)), w.wait((B, "D", -1))]
            add(sums(name, 0, 0, HALF, HALF), srcs, HALF, out.at[hi])
        elif part[1] == "A":
            if kind == "P":
                w.send(sums(name, 3, key[2], 0, HALF), key, way[2 * key[2] - 1])
            elif kind == "D":
                p, d = key[2:]
                mine = sums(name, 2 if d == 1 else 1, p, 0, HALF)
                if p == (1 - d) // 2:
                    add(mine, [w.wait((part, "P", p))], HALF)
                w.send(mine, key, way[-d])
            else:
                mine = sums(name, 0, 1, 0, HALF)
                add(mine, [w.wait((part, "D", 1, 1)), w.wait((part, "D", 1, -1))], HALF)
                w.send(mine, key, across[name])
        elif kind == "Y":
            w.send(sums(name, key[2], 1, HALF, HALF), key, across[name])
        elif kind == "P":
            d = key[2]
            if (name, "far") not in summed:
                summed.add((name, "far"))
                add(sums(name, 3, 0, HALF, HALF), [w.wait((part, "Y", 3))], HALF)
            w.send(sums(name, 3, 0, HALF if d == 1 else HALF + 32, 32), key, way[-d])
        else:
            d = key[2]
            q = 2 if d == 1 else 1
            mine = sums(name, q, 0, HALF, HALF)
            add(mine, [w.wait((part, "Y", q))], HALF)
            add(mine.at[pl.ds(0 if d == 1 else 32, 32)], [w.wait((part, "P", d))], 32)
            w.send(mine, key, way[-d])

    def put_grad(g, r, c, width):
        first, size = r
        h = g.astype(BF16)
        rows = pl.ds(pl.multiple_of(first, ROWS), size)
        cols = pl.ds(pl.multiple_of(c, ROWS), width)
        below = pl.ds(pl.multiple_of(first + (c // IMG) * IMG, ROWS), size)
        Tl[below, pl.ds(pl.multiple_of(c % IMG, ROWS), width)] = h
        hf = h.astype(F32)
        P8h[rows, cols] = (hf * 256.0).astype(F8)
        P8l[rows, cols] = ((g - hf) * 65536.0).astype(F8)

    def soften(n, carry):
        p = pick(n, [m for kind, m in STEPS if kind == "t"])
        cols = pl.ds(pl.multiple_of(p * 256, 256), 256)
        cl = jnp.concatenate([cst[8, 0, pl.ds(txt_block(2 * p + j), 1), :] for j in range(2)], axis=1)

        def soft(b, inner):
            r = pl.ds(pl.multiple_of(b * ROWS, ROWS), ROWS)
            v = L[r, cols]
            rl = row_m[r, :]
            g = jnp.exp2(v - jnp.concatenate([rl, rl], axis=1)) + jnp.exp2(v - cl)
            put_grad(g, (b * ROWS, ROWS), p * 256, 256)
            return inner

        lax.fori_loop(0, IMG // ROWS, soft, 0)
        for j in range(2):
            s = 2 * p + j
            here, u = on_diagonal(s)

            @pl.when(here)
            def _():
                r = pl.ds(pl.multiple_of(u * ROWS, ROWS), ROWS)
                c = pl.ds(pl.multiple_of(s * ROWS, ROWS), ROWS)
                v = L[r, c]
                g = jnp.exp2(v - row_m[r, :]) + jnp.exp2(v - cl[:, 128 * j : 128 * j + 128]) - eye[...]
                put_grad(g, (u * ROWS, ROWS), s * ROWS, ROWS)

        return carry

    def loss_send(m):
        if m == 1:
            for n in range(7):
                w.wait(("l1", n))
            lbuf[8] = sum(lbuf[n] for n in range(8))
            for n in range(3):
                w.send(lbuf.at[8], ("l2", n), col_peers[n])
        if m == 3:
            for n in range(3):
                w.wait(("l2", n))
            lbuf[12] = sum(lbuf[n] for n in range(8, 12))
            for n, d in enumerate((1, -1, 2)):
                w.send(lbuf.at[12], ("l3", n), zs[d])

    def back_step(n, carry):
        is_text = pick(n, [int(kind == "t") for kind, _ in STEPS])
        arg = pick(n, [a for _, a in STEPS])
        lax.fori_loop(pick(n, SOFT[:-1]), pick(n, SOFT[1:]), soften, 0)

        @pl.when(is_text == 1)
        def _():
            cols = pl.ds(pl.multiple_of(arg * 256, 256), 256)
            below = pl.ds(pl.multiple_of((arg // 4) * IMG, IMG), IMG)
            high = dot(Tl[below, pl.ds(pl.multiple_of((arg % 4) * 256, 256), 256)], Ih[...], 0, 0)
            cross = dot(P8h[:, cols], I8l[...], 0, 0) + dot(P8l[:, cols], I8h[...], 0, 0)
            res = high + (1.0 / (65536.0 * i_scale)) * cross
            Tb[2 * arg] = res[:ROWS]
            Tb[2 * arg + 1] = res[ROWS:]

        @pl.when(is_text == 0)
        def _():
            r = pl.ds(pl.multiple_of(arg * ROWS, ROWS), ROWS)
            r2 = pl.ds(pl.multiple_of(IMG + arg * ROWS, ROWS), ROWS)
            high = dot(Tl[r, 0:IMG], Th[0:IMG, :], 1, 0) + dot(Tl[r2, 0:IMG], Th[IMG:TXT, :], 1, 0)
            cross = dot(P8h[r, :], T8l[...], 1, 0) + dot(P8l[r, :], T8h[...], 1, 0)
            L[r, 0:E] = high + (1.0 / (65536.0 * t_scale)) * cross

        for m in range(len(STEPS)):

            @pl.when(n == m)
            def _():
                for key in RETURN[m]:
                    back_send(key)
                loss_send(m)

        return carry

    lax.fori_loop(0, len(STEPS), back_step, 0)
    for n in range(3):
        w.wait(("l3", n))
    loss_ref[0] = jnp.sum(sum(lbuf[n] for n in range(12, 16))) / (1024 * 2.0 * 16384)
    w.flush(like)
    assert not w.arrivals


def on_device(image_emb, text_emb, logit_scale):
    vm = pltpu.VMEM
    loss, image_grad, text_grad = pl.pallas_call(
        kernel,
        out_shape=(
            jax.ShapeDtypeStruct((1,), F32),
            jax.ShapeDtypeStruct((ROWS, E), F32),
            jax.ShapeDtypeStruct((ROWS, E), F32),
        ),
        in_specs=[
            pl.BlockSpec(memory_space=pltpu.SMEM),
            pl.BlockSpec(memory_space=pl.ANY),
            pl.BlockSpec(memory_space=pl.ANY),
        ],
        out_specs=[pl.BlockSpec(memory_space=pltpu.SMEM)] + [pl.BlockSpec(memory_space=vm)] * 2,
        scratch_shapes=[
            vm((8, ROWS, E), F32),
            vm((16, ROWS, E), F32),
            vm((IMG, E), BF16),
            vm((IMG, E), BF16),
            vm((TXT, E), BF16),
            vm((TXT, E), BF16),
            vm((IMG, TXT), F32),
            vm((IMG, TXT), F8),
            vm((IMG, TXT), F8),
            vm((IMG, E), F8),
            vm((IMG, E), F8),
            vm((TXT, E), F8),
            vm((TXT, E), F8),
            vm((IMG, 128), F32),
            vm((IMG, 128), F32),
            vm((8, TXT), F32),
            vm((8, TXT), F32),
            vm((9, 2, 8, 128), F32),
            vm((9, 2, 16, 128), F32),
            vm((16, 8, 128), F32),
            vm((14, HALF, E), F32),
            vm((14, HALF, E), F32),
            vm((ROWS, ROWS), F32),
            pltpu.SemaphoreType.DMA((56,)),
            pltpu.SemaphoreType.DMA((112,)),
            pltpu.SemaphoreType.DMA((2,)),
        ],
        compiler_params=pltpu.CompilerParams(
            collective_id=0, has_side_effects=True, vmem_limit_bytes=63 * 2**20
        ),
        name="contrastive",
    )(logit_scale.reshape(1), image_emb, text_emb)
    return loss.reshape(()), logit_scale * image_grad, logit_scale * text_grad


def solution(mesh):
    in_specs = (P(("img", "txt"), None), P(("txt", "img"), None), P())
    out_specs = (P(), P(("img", "txt"), None), P(("txt", "img"), None))
    return jax.shard_map(
        on_device, mesh=mesh, in_specs=in_specs, out_specs=out_specs, check_vma=False
    )
```

```python
import functools

import jax
import jax.numpy as jnp
from jax import lax
from jax.experimental import pallas as pl
from jax.experimental.pallas import tpu as pltpu
from jax.sharding import PartitionSpec as P

MESH = pl.DeviceIdType.MESH
BF16, F32 = jnp.bfloat16, jnp.float32
LOG2E = 1.4426950408889634
LN2 = 0.6931471805599453

STEP = (0, 1, 3, 2)
F8 = jnp.float8_e4m3fn
ROWS = 128
CUT = 64
REST = ROWS - CUT
H = REST // 2
E = 1280
CHUNK = 64
IMG, TXT = 1024, 2048

OWN = 13
TILES = ((0, 0), (2, 0), (0, 1), (2, 1), (1, 0), (1, 1), (0, 2), (1, 2), (2, 2), (3, 0), (3, 1), (3, 2), (0, 3), (1, 3), (2, 3), (3, 3))
GATHER = (
    (("TA", 0, 1), ("IA", 0, 1), ("TB", 1, 0), ("IB", 2, 0), ("IA", 1, 0), ("TB", 2, 0), ("S", 0, 0), ("TB", 0, 1),
     ("IB", 0, 1), ("TA", 1, 0), ("IA", 2, 0), ("IB", 1, 0), ("TA", 2, 0), ("TB", 1, 1), ("IB", 2, 1),
     ("TA", 1, 1), ("IA", 2, 1), ("IA", 1, 1), ("TA", 2, 1), ("S", 0, 1), ("S", 1, 0), ("S", 2, 0),
     ("TB", 3, 0, 1), ("IB", 3, 0, 1), ("IB", 1, 1), ("TB", 3, 0, 0), ("TB", 2, 1), ("IB", 3, 0, 0)),
    (("S", 1, 1), ("TA", 3, 0), ("IA", 3, 1), ("TA", 3, 1), ("IA", 3, 0)),
    (),
    (("IB", 3, 1), ("TB", 3, 1)),
    (("S", 2, 1),),
    (),
    (("S", 3, 0),),
    (),
    (("S", 3, 1),),
    (),
    (),
    (),
    (),
    (),
    (),
    (),
    (),
)

STEPS = (("t", 7), ("t", 6), ("i", 7), ("t", 3), ("i", 6), ("i", 5), ("t", 2), ("t", 5), ("t", 1), ("i", 3), ("t", 4), ("i", 2), ("i", 1), ("i", 4), ("t", 0), ("i", 0))
RETURN = (
    (("S", 3, 1),),
    (("S", 3, 0),),
    (("TA", "P", 0), ("TA", "P", 1), ("TB", "Y", 3), ("IA", "P", 1), ("IB", "Y", 3)),
    (("S", 1, 1),),
    (("IA", "P", 0),),
    (("TB", "Y", 1), ("IB", "Y", 2)),
    (("S", 1, 0), ("IA", "D", 1, 1)),
    (("S", 2, 1), ("IB", "P", -1), ("TA", "D", 1, -1), ("TB", "P", 1)),
    (("S", 0, 1),),
    (("IB", "Y", 1), ("IA", "D", 1, -1), ("TB", "Y", 2), ("TB", "P", -1), ("TA", "D", 1, 1), ("IB", "P", 1)),
    (("S", 2, 0),),
    (("TA", "D", 0, -1), ("TB", "Y", 0), ("IA", "D", 0, -1)),
    (("TA", "D", 0, 1), ("IB", "Y", 0)),
    (("IA", "D", 0, 1),),
    (("TB", "D", -1), ("S", 0, 0)),
    (("TB", "D", 1), ("IB", "D", -1), ("TA", "2"), ("IB", "D", 1), ("IA", "2"), ("T", "F"), ("I", "F")),
)


FIRST_IMAGE = [kind for kind, _ in STEPS].index("i")
SOFT = [n if n <= FIRST_IMAGE else 8 for n in range(len(STEPS) + 1)]


def pick(n, values):
    return sum(jnp.where(n == j, v, 0) for j, v in enumerate(values))


def dot(a, b, ca, cb):
    return lax.dot_general(a, b, (((ca,), (cb,)), ((), ())), preferred_element_type=F32)


def dot3(ah, al, bh, bl, ca, cb):
    return dot(ah, bh, ca, cb) + (dot(ah, bl, ca, cb) + dot(al, bh, ca, cb))


class Wires:
    def __init__(self, send_sem, recv_sem):
        self.send_sem, self.recv_sem = send_sem, recv_sem
        self.sent, self.n_recv, self.arrivals = [], 0, {}

    def open(self, key, ref, *index):
        self.arrivals[key] = (ref, index, self.n_recv)
        self.n_recv += 1

    def send(self, src, key, dev):
        dst, index, n = self.arrivals[key]
        dst = dst.at[index]
        s = len(self.sent)
        cp = pltpu.make_async_remote_copy(
            src_ref=src,
            dst_ref=dst,
            send_sem=self.send_sem.at[s],
            recv_sem=self.recv_sem.at[n],
            device_id=dev,
            device_id_type=MESH,
        )
        cp.start()
        self.sent.append(dst.shape)

    def wait(self, key):
        dst, index, n = self.arrivals.pop(key)
        dst = dst.at[index]
        pltpu.make_async_copy(dst, dst, self.recv_sem.at[n]).wait()
        return dst

    def need(self, *keys):
        for key in keys:
            if key in self.arrivals:
                self.wait(key)

    def flush(self, like):
        for s, shape in enumerate(self.sent):
            ref = like(shape)
            pltpu.make_async_copy(ref, ref, self.send_sem.at[s]).wait()
        self.sent = []


def merge(parts):
    top = functools.reduce(jnp.maximum, [m for m, _ in parts])
    total = sum(s * jnp.exp2(m - top) for m, s in parts)
    return top, total


def kernel(
    scale_ref, img_ref, txt_ref,
    loss_ref, img_out, txt_out,
    Ib, Tb, Ih, Il, Th, Tl, L,
    P8h, P8l, I8h, I8l, T8h, T8l,
    row_m, row_s, col_m, col_s, rst, cst, lbuf,
    ialand, ibland, taland, tbland, eye,
    send_sem, recv_sem, local_sem,
):
    i, t = lax.axis_index("img"), lax.axis_index("txt")
    x, k = t // 2, t % 2
    z, y = i // 4, i % 4
    even = 1 - 2 * (y % 2)

    def dev(dx=0, dy=0, dz=0, dk=0):
        return (((z + dz) % 4) * 4 + (y + dy + 4) % 4, ((x + dx) % 4) * 2 + (k + dk) % 2)

    sib = dev(dk=1)
    xs = {1: dev(dx=1), -1: dev(dx=3), 2: dev(dx=2)}
    zs = {1: dev(dz=1), -1: dev(dz=3), 2: dev(dz=2)}
    yi, yt = dev(dy=even), dev(dy=-even)
    row_peers = [*xs.values(), yi, *(dev(dx=d, dy=even) for d in (1, 3, 2))]
    col_peers = [sib, yt, dev(dy=-even, dk=1)]
    peers = [*row_peers, *col_peers, *zs.values()]
    barrier = pltpu.get_barrier_semaphore()
    for peer in peers:
        pl.semaphore_signal(barrier, inc=1, device_id=peer, device_id_type=MESH)
    pl.semaphore_wait(barrier, len(peers))

    w = Wires(send_sem, recv_sem)

    def like(shape):
        if shape[-1] == E:
            return Ib.at[0, pl.ds(0, shape[0])]
        return {2: lbuf, 3: rst if shape[-2] == 8 else cst}[len(shape)].at[0]

    lo, hi = pl.ds(0, CUT), pl.ds(CUT, REST)
    ring = {"I": xs, "T": zs}
    across = {"I": yi, "T": yt}
    own = {"I": img_ref, "T": txt_ref}

    def place(name, q, p):
        return (Ib, 2 * q + p) if name == "I" else (Tb, 4 * q + 2 * p)

    for name in "IT":
        for q in range(4):
            for p in range(2):
                if (q, p) == (0, 0):
                    continue
                w.open((name + "A", q, p), *place(name, q, p), lo)
                if (q, p) == (3, 0):
                    for n in range(2):
                        w.open((name + "B", 3, 0, n), *place(name, 3, 0), pl.ds(CUT + H * n, H))
                else:
                    w.open((name + "B", q, p), *place(name, q, p), hi)
    for q in range(4):
        for p in range(2):
            w.open(("S", q, p), Tb, 4 * q + 2 * p + 1)

    def keys_of(name, q, p, parts="AB"):
        return [(name + part, q, p, *n) for part in parts for n in ((), (0,), (1,))]

    def block(name, q, p, rows):
        if (q, p) == (0, 0):
            return own[name].at[rows]
        ref, n = place(name, q, p)
        return ref.at[n, rows]

    def gather_send(key):
        if key[0] == "S":
            q, p = key[1:]
            w.need(*keys_of("T", q, p))
            w.send(block("T", q, p, pl.ds(0, ROWS)), key, sib)
            return
        name, part, q, p = key[0][0], key[0][1], key[1], key[2]
        rows = lo if part == "A" else hi
        if part == "A" and p == 1 and q == 0:
            source, dst = (0, 0), across[name]
        elif part == "B" and p == 1:
            source, dst = (q, 0), across[name]
        elif len(key) == 4:
            source, dst = (2 - key[3], 0), ring[name][1 - 2 * key[3]]
            rows = pl.ds(CUT + H * key[3], H)
        elif q == 3:
            source, dst = (2 - p, p), ring[name][1 - 2 * p]
        else:
            source, dst = (0, p), ring[name][1 if q == 2 else -1]
        w.need(*keys_of(name, *source, part))
        w.send(block(name, *source, rows), key, dst)

    own_t = pltpu.make_async_copy(txt_ref, Tb.at[0], local_sem.at[0])
    own_i = pltpu.make_async_copy(img_ref, Ib.at[0], local_sem.at[1])
    for key in GATHER[0][:OWN]:
        gather_send(key)
    own_t.start()
    own_i.start()

    rows_iota = lax.broadcasted_iota(jnp.int32, (ROWS, ROWS), 0)
    cols_iota = lax.broadcasted_iota(jnp.int32, (ROWS, ROWS), 1)
    eye[...] = (rows_iota == cols_iota).astype(F32)
    row_m[...] = jnp.full((IMG, 128), -jnp.inf, F32)
    row_s[...] = jnp.zeros((IMG, 128), F32)
    col_m[...] = jnp.full((8, TXT), -jnp.inf, F32)
    col_s[...] = jnp.zeros((8, TXT), F32)

    def split_rows(src, first, count, high, low):
        def body(b, carry):
            n = first + b // 4
            o = pl.ds(pl.multiple_of(first * ROWS + b * 32, 32), 32)
            v = src[n, pl.ds(pl.multiple_of((b % 4) * 32, 32), 32), :]
            h = v.astype(BF16)
            high[o, :] = h
            low[o, :] = (v - h.astype(F32)).astype(BF16)
            return carry

        lax.fori_loop(0, 4 * count, body, 0)

    own_i.wait()
    own_t.wait()
    done = set()

    def split_arrived():
        for q in range(4):
            for p in range(2):
                if not any(key in w.arrivals for key in keys_of("I", q, p)) and ("I", q, p) not in done:
                    done.add(("I", q, p))
                    split_rows(Ib, 2 * q + p, 1, Ih, Il)
                if not any(key in w.arrivals for key in keys_of("T", q, p)) and ("T", q, p) not in done:
                    done.add(("T", q, p))
                    split_rows(Tb, 4 * q + 2 * p, 1, Th, Tl)
                if ("S", q, p) not in w.arrivals and ("S", q, p) not in done:
                    done.add(("S", q, p))
                    split_rows(Tb, 4 * q + 2 * p + 1, 1, Th, Tl)

    for n, key in enumerate(GATHER[0][OWN:]):
        gather_send(key)
        if n == 5:
            w.need(("S", 0, 0))
            split_arrived()
    split_arrived()

    s2 = scale_ref[0] * LOG2E
    def tile_at(n):
        return pick(n, [qi for qi, _ in TILES]), pick(n, [qt for _, qt in TILES])

    def logits(a, b):
        rows = pl.ds(pl.multiple_of(a * 256, 256), 256)
        cols = pl.ds(pl.multiple_of(b * 512, 512), 512)
        L[rows, cols] = s2 * dot3(Ih[rows, :], Il[rows, :], Th[cols, :], Tl[cols, :], 1, 1)

    def statistics(n):
        a, b = tile_at(n)
        cols = pl.ds(pl.multiple_of(b * 512, 512), 512)
        old = col_m[:, cols]
        top = old
        some = [pl.ds(pl.multiple_of(a * 256 + CHUNK * c, CHUNK), CHUNK) for c in range(256 // CHUNK)]
        for r in some:
            v = L[r, cols]
            vs = [v[:, 128 * j : 128 * j + 128] for j in range(4)]
            was = row_m[r, :]
            new = functools.reduce(jnp.maximum, vs, was)
            row_s[r, :] = row_s[r, :] * jnp.exp2(was - new) + sum(jnp.exp2(u - new) for u in vs)
            row_m[r, :] = new
            top = jnp.maximum(top, jnp.max(v.reshape(CHUNK // 8, 8, 512), axis=0))
        total = col_s[:, cols] * jnp.exp2(old - top)
        for r in some:
            v = L[r, cols].reshape(CHUNK // 8, 8, 512)
            total = total + jnp.sum(jnp.exp2(v - top[None]), axis=0)
        col_s[:, cols] = total
        col_m[:, cols] = top

    def tile(n, carry):
        for m, (qi, qt) in enumerate(TILES):

            @pl.when(n == m)
            def _():
                if m > 0:
                    for key in GATHER[m]:
                        gather_send(key)
                for p in range(2):
                    w.need(*keys_of("I", qi, p), *keys_of("T", qt, p), ("S", qt, p))
                split_arrived()

        a, b = tile_at(n)

        @pl.when(n > 0)
        def _():
            statistics(n - 1)
            logits(a, b)

        @pl.when(n == 0)
        def _():
            logits(a, b)

        return carry

    lax.fori_loop(0, len(TILES), tile, 0)
    statistics(len(TILES) - 1)

    def step_of(q):
        return q + q // 2 - 2 * (q // 3)

    def img_block(s):
        return ((x + step_of(s // 2)) % 4) * 2 + (y + s % 2) % 2

    def txt_block(s):
        return (((z + step_of(s // 4)) % 4) * 2 + (y + (s // 2) % 2) % 2) * 2 + (k + s % 2) % 2

    def on_diagonal(s):
        owner = (x * 2 + (k + s % 2) % 2) * 16 + ((z + step_of(s // 4)) % 4) * 4
        owner = owner + (y + ((s // 2) % 2) * (4 - even)) % 4
        bi, bt = owner // 8, owner % 8
        here = (bi // 4 == z) & ((bi % 4) // 2 == y // 2) & (bt % 2 == k)
        return here, step_of((bt // 2 + 4 - x) % 4) * 2 + (bi + y) % 2

    def sum_diagonal(s, carry):
        here, u = on_diagonal(s)

        @pl.when(here)
        def _():
            r = pl.ds(pl.multiple_of(u * ROWS, ROWS), ROWS)
            v = L[r, pl.ds(pl.multiple_of(s * ROWS, ROWS), ROWS)]
            lbuf[0] += jnp.sum((v * eye[...]).reshape(ROWS // 8, 8, 128), axis=0)

        return carry

    def fold_cols(s, carry):
        c = pl.ds(pl.multiple_of(s * ROWS, ROWS), ROWS)
        m8 = col_m[:, c]
        m1 = jnp.max(m8, axis=0, keepdims=True)
        at = pl.ds(txt_block(s), 1)
        cst[0, 0, at, :] = m1
        cst[0, 1, at, :] = jnp.sum(col_s[:, c] * jnp.exp2(m8 - m1), axis=0, keepdims=True)
        return carry

    def fold_rows(s, carry):
        r = pl.ds(pl.multiple_of(s * ROWS, ROWS), ROWS)
        mt, st = row_m[r, :].T, row_s[r, :].T
        m1 = jnp.max(mt, axis=0, keepdims=True)
        at = pl.ds(img_block(s), 1)
        rst[0, 0, at, :] = m1
        rst[0, 1, at, :] = jnp.sum(st * jnp.exp2(mt - m1), axis=0, keepdims=True)
        return carry

    lax.fori_loop(0, 16, fold_cols, 0)
    w.flush(like)
    assert not w.arrivals
    for n in range(7):
        w.open(("r", n), rst, 1 + n)
    for n in range(3):
        w.open(("c1", n), cst, 1 + n)
        w.open(("c2", n), cst, 5 + n)
    for n in range(3):
        w.send(cst.at[0], ("c1", n), col_peers[n])
    lax.fori_loop(0, 8, fold_rows, 0)
    for n in range(7):
        w.send(rst.at[0], ("r", n), row_peers[n])
    def largest(src, count):
        def body(b, top):
            v = jnp.abs(src[pl.ds(pl.multiple_of(b * 64, 64), 64), :]).astype(F32)
            return jnp.maximum(top, jnp.max(v.reshape(8, 8, E), axis=0))

        return jnp.max(lax.fori_loop(0, count // 64, body, jnp.zeros((8, E), F32)))

    i_scale = 240.0 / jnp.maximum(largest(Ih, IMG), 1e-30)
    t_scale = 240.0 / jnp.maximum(largest(Th, TXT), 1e-30)

    def to_eight(high, low, count, scale, high8, low8):
        def body(b, carry):
            r = pl.ds(pl.multiple_of(b * 64, 64), 64)
            high8[r, :] = (high[r, :].astype(F32) * scale).astype(F8)
            low8[r, :] = (low[r, :].astype(F32) * (256.0 * scale)).astype(F8)
            return carry

        lax.fori_loop(0, count // 64, body, 0)

    for n in range(3):
        w.wait(("c1", n))
    cst[4, 0], cst[4, 1] = merge([(cst[n, 0], cst[n, 1]) for n in range(4)])
    for n, d in enumerate((1, -1, 2)):
        w.send(cst.at[4], ("c2", n), zs[d])
    to_eight(Ih, Il, IMG, i_scale, I8h, I8l)
    to_eight(Th, Tl, TXT, t_scale, T8h, T8l)
    lbuf[0] = jnp.zeros((8, 128), F32)
    lax.fori_loop(0, 16, sum_diagonal, 0)
    for n in range(7):
        w.wait(("r", n))
    m, s = merge([(rst[n, 0], rst[n, 1]) for n in range(8)])
    row_lse = m + jnp.log2(s)
    rst[8, 0] = row_lse + 1.0

    def spread(s, carry):
        r = pl.ds(pl.multiple_of(s * ROWS, ROWS), ROWS)
        v = rst[8, 0, pl.ds(img_block(s), 1), :]
        row_m[r, :] = jnp.broadcast_to(v, (ROWS, 128)).T
        return carry

    lax.fori_loop(0, 8, spread, 0)
    for n in range(3):
        w.wait(("c2", n))
    m, s = merge([(cst[n, 0], cst[n, 1]) for n in range(4, 8)])
    col_lse = m + jnp.log2(s)
    w.flush(like)
    cst[8, 0] = col_lse + 1.0
    share = jnp.sum(row_lse) / 8 + jnp.sum(col_lse) / 16 - 2.0 * jnp.sum(lbuf[0])
    lbuf[0] = jnp.full((8, 128), LN2 * share, F32)
    for n in range(7):
        w.open(("l1", n), lbuf, 1 + n)
    for n in range(3):
        w.open(("l2", n), lbuf, 9 + n)
        w.open(("l3", n), lbuf, 13 + n)
    for n in range(7):
        w.send(lbuf.at[0], ("l1", n), row_peers[n])

    for name, land_a, land_b in (("I", ialand, ibland), ("T", taland, tbland)):
        for p in range(2):
            w.open((name + "A", "P", p), land_a, p)
            for n, d in enumerate((1, -1)):
                w.open((name + "A", "D", p, d), land_a, 2 + 2 * p + n)
        w.open((name + "A", "2"), land_a, 6)
        for q in range(4):
            w.open((name + "B", "Y", q), land_b, q)
        for n, d in enumerate((1, -1)):
            w.open((name + "B", "P", d), land_b, 4, pl.ds(H * n, H))
            w.open((name + "B", "D", d), land_b, 5 + n)
    for q in range(4):
        for p in range(2):
            w.open(("S", q, p), Ib, 2 * q + p)
    def add(dst, srcs, rows, out=None):
        step = 16 if rows % 16 == 0 else 8

        def body(b, carry):
            r = pl.ds(pl.multiple_of(b * step, step), step)
            v = dst[r, :]
            for src in srcs:
                v = v + src[r, :]
            (dst if out is None else out)[r, :] = v
            return carry

        lax.fori_loop(0, rows // step, body, 0)

    summed = set()

    def sums(name, q, p, at, rows):
        if name == "I":
            return L.at[pl.ds((2 * q + p) * ROWS + at, rows), pl.ds(0, E)]
        if (q, p) not in summed:
            summed.add((q, p))
            add(Tb.at[4 * q + 2 * p], [w.wait(("S", q, p))], ROWS)
        return Tb.at[4 * q + 2 * p, pl.ds(at, rows)]

    def back_send(key):
        if key[0] == "S":
            q, p = key[1:]
            w.send(Tb.at[4 * q + 2 * p + 1], key, sib)
            return
        name, kind = key[0][0], key[1]
        way, part = ring[name], key[0]
        if part == name:
            out = img_out if name == "I" else txt_out
            A, B = name + "A", name + "B"
            srcs = [w.wait((A, "D", 0, 1)), w.wait((A, "D", 0, -1)), w.wait((A, "2"))]
            add(sums(name, 0, 0, 0, CUT), srcs, CUT, out.at[lo])
            srcs = [w.wait((B, "Y", 0)), w.wait((B, "D", 1)), w.wait((B, "D", -1))]
            add(sums(name, 0, 0, CUT, REST), srcs, REST, out.at[hi])
        elif part[1] == "A":
            if kind == "P":
                w.send(sums(name, 3, key[2], 0, CUT), key, way[2 * key[2] - 1])
            elif kind == "D":
                p, d = key[2:]
                mine = sums(name, 2 if d == 1 else 1, p, 0, CUT)
                if p == (1 - d) // 2:
                    add(mine, [w.wait((part, "P", p))], CUT)
                w.send(mine, key, way[-d])
            else:
                mine = sums(name, 0, 1, 0, CUT)
                add(mine, [w.wait((part, "D", 1, 1)), w.wait((part, "D", 1, -1))], CUT)
                w.send(mine, key, across[name])
        elif kind == "Y":
            w.send(sums(name, key[2], 1, CUT, REST), key, across[name])
        elif kind == "P":
            d = key[2]
            if (name, "far") not in summed:
                summed.add((name, "far"))
                add(sums(name, 3, 0, CUT, REST), [w.wait((part, "Y", 3))], REST)
            w.send(sums(name, 3, 0, CUT if d == 1 else CUT + H, H), key, way[-d])
        else:
            d = key[2]
            q = 2 if d == 1 else 1
            mine = sums(name, q, 0, CUT, REST)
            add(mine, [w.wait((part, "Y", q))], REST)
            add(mine.at[pl.ds(0 if d == 1 else H, H)], [w.wait((part, "P", d))], H)
            w.send(mine, key, way[-d])

    def put_grad(g, r, c, width):
        first, size = r
        h = g.astype(BF16)
        rows = pl.ds(pl.multiple_of(first, ROWS), size)
        cols = pl.ds(pl.multiple_of(c, ROWS), width)
        below = pl.ds(pl.multiple_of(first + (c // IMG) * IMG, ROWS), size)
        Tl[below, pl.ds(pl.multiple_of(c % IMG, ROWS), width)] = h
        hf = h.astype(F32)
        P8h[rows, cols] = (hf * 256.0).astype(F8)
        P8l[rows, cols] = ((g - hf) * 65536.0).astype(F8)

    def soften(n, carry):
        p = pick(n, [m for kind, m in STEPS if kind == "t"])
        cols = pl.ds(pl.multiple_of(p * 256, 256), 256)
        cl = jnp.concatenate([cst[8, 0, pl.ds(txt_block(2 * p + j), 1), :] for j in range(2)], axis=1)

        def soft(b, inner):
            r = pl.ds(pl.multiple_of(b * ROWS, ROWS), ROWS)
            v = L[r, cols]
            rl = row_m[r, :]
            g = jnp.exp2(v - jnp.concatenate([rl, rl], axis=1)) + jnp.exp2(v - cl)
            put_grad(g, (b * ROWS, ROWS), p * 256, 256)
            return inner

        lax.fori_loop(0, IMG // ROWS, soft, 0)
        for j in range(2):
            s = 2 * p + j
            here, u = on_diagonal(s)

            @pl.when(here)
            def _():
                r = pl.ds(pl.multiple_of(u * ROWS, ROWS), ROWS)
                c = pl.ds(pl.multiple_of(s * ROWS, ROWS), ROWS)
                v = L[r, c]
                g = jnp.exp2(v - row_m[r, :]) + jnp.exp2(v - cl[:, 128 * j : 128 * j + 128]) - eye[...]
                put_grad(g, (u * ROWS, ROWS), s * ROWS, ROWS)

        return carry

    def loss_send(m):
        if m == 1:
            for n in range(7):
                w.wait(("l1", n))
            lbuf[8] = sum(lbuf[n] for n in range(8))
            for n in range(3):
                w.send(lbuf.at[8], ("l2", n), col_peers[n])
        if m == 3:
            for n in range(3):
                w.wait(("l2", n))
            lbuf[12] = sum(lbuf[n] for n in range(8, 12))
            for n, d in enumerate((1, -1, 2)):
                w.send(lbuf.at[12], ("l3", n), zs[d])

    def back_step(n, carry):
        is_text = pick(n, [int(kind == "t") for kind, _ in STEPS])
        arg = pick(n, [a for _, a in STEPS])
        lax.fori_loop(pick(n, SOFT[:-1]), pick(n, SOFT[1:]), soften, 0)

        @pl.when(is_text == 1)
        def _():
            cols = pl.ds(pl.multiple_of(arg * 256, 256), 256)
            below = pl.ds(pl.multiple_of((arg // 4) * IMG, IMG), IMG)
            high = dot(Tl[below, pl.ds(pl.multiple_of((arg % 4) * 256, 256), 256)], Ih[...], 0, 0)
            cross = dot(P8h[:, cols], I8l[...], 0, 0) + dot(P8l[:, cols], I8h[...], 0, 0)
            res = high + (1.0 / (65536.0 * i_scale)) * cross
            Tb[2 * arg] = res[:ROWS]
            Tb[2 * arg + 1] = res[ROWS:]

        @pl.when(is_text == 0)
        def _():
            r = pl.ds(pl.multiple_of(arg * ROWS, ROWS), ROWS)
            r2 = pl.ds(pl.multiple_of(IMG + arg * ROWS, ROWS), ROWS)
            high = dot(Tl[r, 0:IMG], Th[0:IMG, :], 1, 0) + dot(Tl[r2, 0:IMG], Th[IMG:TXT, :], 1, 0)
            cross = dot(P8h[r, :], T8l[...], 1, 0) + dot(P8l[r, :], T8h[...], 1, 0)
            L[r, 0:E] = high + (1.0 / (65536.0 * t_scale)) * cross

        for m in range(len(STEPS)):

            @pl.when(n == m)
            def _():
                for key in RETURN[m]:
                    back_send(key)
                loss_send(m)

        return carry

    lax.fori_loop(0, len(STEPS), back_step, 0)
    for n in range(3):
        w.wait(("l3", n))
    loss_ref[0] = jnp.sum(sum(lbuf[n] for n in range(12, 16))) / (1024 * 2.0 * 16384)
    w.flush(like)
    assert not w.arrivals


def on_device(image_emb, text_emb, logit_scale):
    vm = pltpu.VMEM
    loss, image_grad, text_grad = pl.pallas_call(
        kernel,
        out_shape=(
            jax.ShapeDtypeStruct((1,), F32),
            jax.ShapeDtypeStruct((ROWS, E), F32),
            jax.ShapeDtypeStruct((ROWS, E), F32),
        ),
        in_specs=[
            pl.BlockSpec(memory_space=pltpu.SMEM),
            pl.BlockSpec(memory_space=pl.ANY),
            pl.BlockSpec(memory_space=pl.ANY),
        ],
        out_specs=[pl.BlockSpec(memory_space=pltpu.SMEM)] + [pl.BlockSpec(memory_space=vm)] * 2,
        scratch_shapes=[
            vm((8, ROWS, E), F32),
            vm((16, ROWS, E), F32),
            vm((IMG, E), BF16),
            vm((IMG, E), BF16),
            vm((TXT, E), BF16),
            vm((TXT, E), BF16),
            vm((IMG, TXT), F32),
            vm((IMG, TXT), F8),
            vm((IMG, TXT), F8),
            vm((IMG, E), F8),
            vm((IMG, E), F8),
            vm((TXT, E), F8),
            vm((TXT, E), F8),
            vm((IMG, 128), F32),
            vm((IMG, 128), F32),
            vm((8, TXT), F32),
            vm((8, TXT), F32),
            vm((9, 2, 8, 128), F32),
            vm((9, 2, 16, 128), F32),
            vm((16, 8, 128), F32),
            vm((7, CUT, E), F32),
            vm((7, REST, E), F32),
            vm((7, CUT, E), F32),
            vm((7, REST, E), F32),
            vm((ROWS, ROWS), F32),
            pltpu.SemaphoreType.DMA((56,)),
            pltpu.SemaphoreType.DMA((112,)),
            pltpu.SemaphoreType.DMA((2,)),
        ],
        compiler_params=pltpu.CompilerParams(
            collective_id=0, has_side_effects=True, vmem_limit_bytes=63 * 2**20
        ),
        name="contrastive",
    )(logit_scale.reshape(1), image_emb, text_emb)
    return loss.reshape(()), logit_scale * image_grad, logit_scale * text_grad


def solution(mesh):
    in_specs = (P(("img", "txt"), None), P(("txt", "img"), None), P())
    out_specs = (P(), P(("img", "txt"), None), P(("txt", "img"), None))
    return jax.shard_map(
        on_device, mesh=mesh, in_specs=in_specs, out_specs=out_specs, check_vma=False
    )
```

```python
import functools

import jax
import jax.numpy as jnp
from jax import lax
from jax.experimental import pallas as pl
from jax.experimental.pallas import tpu as pltpu
from jax.sharding import PartitionSpec as P

MESH = pl.DeviceIdType.MESH
BF16, F32 = jnp.bfloat16, jnp.float32
LOG2E = 1.4426950408889634
LN2 = 0.6931471805599453

STEP = (0, 1, 3, 2)
F8 = jnp.float8_e4m3fn
ROWS = 128
CUT = 64
REST = ROWS - CUT
H = REST // 2
E = 1280
CHUNK = 64
IMG, TXT = 1024, 2048

OWN = 13
TILES = ((0, 0), (2, 0), (0, 1), (2, 1), (1, 0), (1, 1), (0, 2), (1, 2), (2, 2), (3, 0), (3, 1), (3, 2), (0, 3), (1, 3), (2, 3), (3, 3))
GATHER = (
    (("TA", 0, 1), ("IA", 0, 1), ("TB", 1, 0), ("IB", 2, 0), ("IA", 1, 0), ("TB", 2, 0), ("S", 0, 0), ("TB", 0, 1),
     ("IB", 0, 1), ("TA", 1, 0), ("IA", 2, 0), ("IB", 1, 0), ("TA", 2, 0), ("TB", 1, 1), ("IB", 2, 1),
     ("TA", 1, 1), ("IA", 2, 1), ("IA", 1, 1), ("TA", 2, 1), ("S", 0, 1), ("S", 1, 0), ("S", 2, 0),
     ("TB", 3, 0, 1), ("IB", 3, 0, 1), ("IB", 1, 1), ("TB", 3, 0, 0), ("TB", 2, 1), ("IB", 3, 0, 0)),
    (("S", 1, 1), ("TA", 3, 0), ("IA", 3, 1), ("TA", 3, 1), ("IA", 3, 0)),
    (),
    (("IB", 3, 1), ("TB", 3, 1)),
    (("S", 2, 1),),
    (),
    (("S", 3, 0),),
    (),
    (("S", 3, 1),),
    (),
    (),
    (),
    (),
    (),
    (),
    (),
    (),
)

STEPS = (("t", 7), ("t", 6), ("i", 7), ("t", 3), ("i", 6), ("i", 5), ("t", 2), ("t", 5), ("t", 1), ("i", 3), ("t", 4), ("i", 2), ("i", 1), ("i", 4), ("t", 0), ("i", 0))
RETURN = (
    (("S", 3, 1),),
    (("S", 3, 0),),
    (("TA", "P", 0), ("TA", "P", 1), ("TB", "Y", 3), ("IA", "P", 1), ("IB", "Y", 3)),
    (("S", 1, 1),),
    (("IA", "P", 0),),
    (("TB", "Y", 1), ("IB", "Y", 2)),
    (("S", 1, 0), ("IA", "D", 1, 1)),
    (("S", 2, 1), ("IB", "P", -1), ("TA", "D", 1, -1), ("TB", "P", 1)),
    (("S", 0, 1),),
    (("IB", "Y", 1), ("IA", "D", 1, -1), ("TB", "Y", 2), ("TB", "P", -1), ("TA", "D", 1, 1), ("IB", "P", 1)),
    (("S", 2, 0),),
    (("TA", "D", 0, -1), ("TB", "Y", 0), ("IA", "D", 0, -1)),
    (("TA", "D", 0, 1), ("IB", "Y", 0)),
    (("IA", "D", 0, 1),),
    (("TB", "D", -1), ("S", 0, 0)),
    (("TB", "D", 1), ("IB", "D", -1), ("TA", "2"), ("IB", "D", 1), ("IA", "2"), ("T", "F"), ("I", "F")),
)


FIRST_IMAGE = [kind for kind, _ in STEPS].index("i")
SOFT = [n if n <= FIRST_IMAGE else 8 for n in range(len(STEPS) + 1)]


def pick(n, values):
    return sum(jnp.where(n == j, v, 0) for j, v in enumerate(values))


def dot(a, b, ca, cb):
    return lax.dot_general(a, b, (((ca,), (cb,)), ((), ())), preferred_element_type=F32)


def dot3(ah, al, bh, bl, ca, cb):
    return dot(ah, bh, ca, cb) + (dot(ah, bl, ca, cb) + dot(al, bh, ca, cb))


class Wires:
    def __init__(self, send_sem, recv_sem):
        self.send_sem, self.recv_sem = send_sem, recv_sem
        self.sent, self.n_recv, self.arrivals = [], 0, {}

    def open(self, key, ref, *index):
        self.arrivals[key] = (ref, index, self.n_recv)
        self.n_recv += 1

    def send(self, src, key, dev):
        dst, index, n = self.arrivals[key]
        dst = dst.at[index]
        s = len(self.sent)
        cp = pltpu.make_async_remote_copy(
            src_ref=src,
            dst_ref=dst,
            send_sem=self.send_sem.at[s],
            recv_sem=self.recv_sem.at[n],
            device_id=dev,
            device_id_type=MESH,
        )
        cp.start()
        self.sent.append(dst.shape)

    def wait(self, key):
        dst, index, n = self.arrivals.pop(key)
        dst = dst.at[index]
        pltpu.make_async_copy(dst, dst, self.recv_sem.at[n]).wait()
        return dst

    def need(self, *keys):
        for key in keys:
            if key in self.arrivals:
                self.wait(key)

    def flush(self, like):
        for s, shape in enumerate(self.sent):
            ref = like(shape)
            pltpu.make_async_copy(ref, ref, self.send_sem.at[s]).wait()
        self.sent = []


def merge(parts):
    top = functools.reduce(jnp.maximum, [m for m, _ in parts])
    total = sum(s * jnp.exp2(m - top) for m, s in parts)
    return top, total


def kernel(
    scale_ref, img_ref, txt_ref,
    loss_ref, img_out, txt_out,
    Ib, Tb, Ih, Il, Th, Tl, L,
    P8h, P8l, I8h, I8l, T8h, T8l,
    row_m, row_s, col_m, col_s, rst, cst, lbuf,
    ialand, ibland, taland, tbland, eye, span,
    send_sem, recv_sem, local_sem,
):
    i, t = lax.axis_index("img"), lax.axis_index("txt")
    x, k = t // 2, t % 2
    z, y = i // 4, i % 4
    even = 1 - 2 * (y % 2)

    def dev(dx=0, dy=0, dz=0, dk=0):
        return (((z + dz) % 4) * 4 + (y + dy + 4) % 4, ((x + dx) % 4) * 2 + (k + dk) % 2)

    sib = dev(dk=1)
    xs = {1: dev(dx=1), -1: dev(dx=3), 2: dev(dx=2)}
    zs = {1: dev(dz=1), -1: dev(dz=3), 2: dev(dz=2)}
    yi, yt = dev(dy=even), dev(dy=-even)
    row_peers = [*xs.values(), yi, *(dev(dx=d, dy=even) for d in (1, 3, 2))]
    col_peers = [sib, yt, dev(dy=-even, dk=1)]
    peers = [*row_peers, *col_peers, *zs.values()]
    barrier = pltpu.get_barrier_semaphore()
    for peer in peers:
        pl.semaphore_signal(barrier, inc=1, device_id=peer, device_id_type=MESH)
    pl.semaphore_wait(barrier, len(peers))

    w = Wires(send_sem, recv_sem)

    def like(shape):
        if shape[-1] == E:
            return Ib.at[0, pl.ds(0, shape[0])]
        return {2: lbuf, 3: rst if shape[-2] == 8 else cst}[len(shape)].at[0]

    lo, hi = pl.ds(0, CUT), pl.ds(CUT, REST)
    ring = {"I": xs, "T": zs}
    across = {"I": yi, "T": yt}
    own = {"I": img_ref, "T": txt_ref}

    def place(name, q, p):
        return (Ib, 2 * q + p) if name == "I" else (Tb, 4 * q + 2 * p)

    for name in "IT":
        for q in range(4):
            for p in range(2):
                if (q, p) == (0, 0):
                    continue
                w.open((name + "A", q, p), *place(name, q, p), lo)
                if (q, p) == (3, 0):
                    for n in range(2):
                        w.open((name + "B", 3, 0, n), *place(name, 3, 0), pl.ds(CUT + H * n, H))
                else:
                    w.open((name + "B", q, p), *place(name, q, p), hi)
    for q in range(4):
        for p in range(2):
            w.open(("S", q, p), Tb, 4 * q + 2 * p + 1)

    def keys_of(name, q, p, parts="AB"):
        return [(name + part, q, p, *n) for part in parts for n in ((), (0,), (1,))]

    def block(name, q, p, rows):
        if (q, p) == (0, 0):
            return own[name].at[rows]
        ref, n = place(name, q, p)
        return ref.at[n, rows]

    def gather_send(key):
        if key[0] == "S":
            q, p = key[1:]
            w.need(*keys_of("T", q, p))
            w.send(block("T", q, p, pl.ds(0, ROWS)), key, sib)
            return
        name, part, q, p = key[0][0], key[0][1], key[1], key[2]
        rows = lo if part == "A" else hi
        if part == "A" and p == 1 and q == 0:
            source, dst = (0, 0), across[name]
        elif part == "B" and p == 1:
            source, dst = (q, 0), across[name]
        elif len(key) == 4:
            source, dst = (2 - key[3], 0), ring[name][1 - 2 * key[3]]
            rows = pl.ds(CUT + H * key[3], H)
        elif q == 3:
            source, dst = (2 - p, p), ring[name][1 - 2 * p]
        else:
            source, dst = (0, p), ring[name][1 if q == 2 else -1]
        w.need(*keys_of(name, *source, part))
        w.send(block(name, *source, rows), key, dst)

    own_t = pltpu.make_async_copy(txt_ref, Tb.at[0], local_sem.at[0])
    own_i = pltpu.make_async_copy(img_ref, Ib.at[0], local_sem.at[1])
    for key in GATHER[0][:OWN]:
        gather_send(key)
    own_t.start()
    own_i.start()

    rows_iota = lax.broadcasted_iota(jnp.int32, (ROWS, ROWS), 0)
    cols_iota = lax.broadcasted_iota(jnp.int32, (ROWS, ROWS), 1)
    span[...] = jnp.zeros((2, 8, E), F32)
    eye[...] = (rows_iota == cols_iota).astype(F32)
    row_m[...] = jnp.full((IMG, 128), -jnp.inf, F32)
    row_s[...] = jnp.zeros((IMG, 128), F32)
    col_m[...] = jnp.full((8, TXT), -jnp.inf, F32)
    col_s[...] = jnp.zeros((8, TXT), F32)

    def split_rows(src, first, count, high, low):
        def body(b, carry):
            n = first + b // 4
            o = pl.ds(pl.multiple_of(first * ROWS + b * 32, 32), 32)
            v = src[n, pl.ds(pl.multiple_of((b % 4) * 32, 32), 32), :]
            at = 0 if high is Ih else 1
            span[at] = jnp.maximum(span[at], jnp.max(jnp.abs(v).reshape(4, 8, E), axis=0))
            h = v.astype(BF16)
            high[o, :] = h
            low[o, :] = (v - h.astype(F32)).astype(BF16)
            return carry

        lax.fori_loop(0, 4 * count, body, 0)

    own_i.wait()
    own_t.wait()
    done = set()

    def split_arrived():
        for q in range(4):
            for p in range(2):
                if not any(key in w.arrivals for key in keys_of("I", q, p)) and ("I", q, p) not in done:
                    done.add(("I", q, p))
                    split_rows(Ib, 2 * q + p, 1, Ih, Il)
                if not any(key in w.arrivals for key in keys_of("T", q, p)) and ("T", q, p) not in done:
                    done.add(("T", q, p))
                    split_rows(Tb, 4 * q + 2 * p, 1, Th, Tl)
                if ("S", q, p) not in w.arrivals and ("S", q, p) not in done:
                    done.add(("S", q, p))
                    split_rows(Tb, 4 * q + 2 * p + 1, 1, Th, Tl)

    for n, key in enumerate(GATHER[0][OWN:]):
        gather_send(key)
        if n == 5:
            w.need(("S", 0, 0))
            split_arrived()
    split_arrived()

    s2 = scale_ref[0] * LOG2E
    def tile_at(n):
        return pick(n, [qi for qi, _ in TILES]), pick(n, [qt for _, qt in TILES])

    def logits(a, b):
        rows = pl.ds(pl.multiple_of(a * 256, 256), 256)
        cols = pl.ds(pl.multiple_of(b * 512, 512), 512)
        L[rows, cols] = s2 * dot3(Ih[rows, :], Il[rows, :], Th[cols, :], Tl[cols, :], 1, 1)

    def statistics(n):
        a, b = tile_at(n)
        cols = pl.ds(pl.multiple_of(b * 512, 512), 512)
        old = col_m[:, cols]
        top = old
        some = [pl.ds(pl.multiple_of(a * 256 + CHUNK * c, CHUNK), CHUNK) for c in range(256 // CHUNK)]
        for r in some:
            v = L[r, cols]
            vs = [v[:, 128 * j : 128 * j + 128] for j in range(4)]
            was = row_m[r, :]
            new = functools.reduce(jnp.maximum, vs, was)
            row_s[r, :] = row_s[r, :] * jnp.exp2(was - new) + sum(jnp.exp2(u - new) for u in vs)
            row_m[r, :] = new
            top = jnp.maximum(top, jnp.max(v.reshape(CHUNK // 8, 8, 512), axis=0))
        total = col_s[:, cols] * jnp.exp2(old - top)
        for r in some:
            v = L[r, cols].reshape(CHUNK // 8, 8, 512)
            total = total + jnp.sum(jnp.exp2(v - top[None]), axis=0)
        col_s[:, cols] = total
        col_m[:, cols] = top

    def tile(n, carry):
        for m, (qi, qt) in enumerate(TILES):

            @pl.when(n == m)
            def _():
                if m > 0:
                    for key in GATHER[m]:
                        gather_send(key)
                for p in range(2):
                    w.need(*keys_of("I", qi, p), *keys_of("T", qt, p), ("S", qt, p))
                split_arrived()

        a, b = tile_at(n)

        @pl.when(n > 0)
        def _():
            statistics(n - 1)
            logits(a, b)

        @pl.when(n == 0)
        def _():
            logits(a, b)

        return carry

    lax.fori_loop(0, len(TILES), tile, 0)
    statistics(len(TILES) - 1)

    def step_of(q):
        return q + q // 2 - 2 * (q // 3)

    def img_block(s):
        return ((x + step_of(s // 2)) % 4) * 2 + (y + s % 2) % 2

    def txt_block(s):
        return (((z + step_of(s // 4)) % 4) * 2 + (y + (s // 2) % 2) % 2) * 2 + (k + s % 2) % 2

    def on_diagonal(s):
        owner = (x * 2 + (k + s % 2) % 2) * 16 + ((z + step_of(s // 4)) % 4) * 4
        owner = owner + (y + ((s // 2) % 2) * (4 - even)) % 4
        bi, bt = owner // 8, owner % 8
        here = (bi // 4 == z) & ((bi % 4) // 2 == y // 2) & (bt % 2 == k)
        return here, step_of((bt // 2 + 4 - x) % 4) * 2 + (bi + y) % 2

    def sum_diagonal(s, carry):
        here, u = on_diagonal(s)

        @pl.when(here)
        def _():
            r = pl.ds(pl.multiple_of(u * ROWS, ROWS), ROWS)
            v = L[r, pl.ds(pl.multiple_of(s * ROWS, ROWS), ROWS)]
            lbuf[0] += jnp.sum((v * eye[...]).reshape(ROWS // 8, 8, 128), axis=0)

        return carry

    def fold_cols(s, carry):
        c = pl.ds(pl.multiple_of(s * ROWS, ROWS), ROWS)
        m8 = col_m[:, c]
        m1 = jnp.max(m8, axis=0, keepdims=True)
        at = pl.ds(txt_block(s), 1)
        cst[0, 0, at, :] = m1
        cst[0, 1, at, :] = jnp.sum(col_s[:, c] * jnp.exp2(m8 - m1), axis=0, keepdims=True)
        return carry

    def fold_rows(s, carry):
        r = pl.ds(pl.multiple_of(s * ROWS, ROWS), ROWS)
        mt, st = row_m[r, :].T, row_s[r, :].T
        m1 = jnp.max(mt, axis=0, keepdims=True)
        at = pl.ds(img_block(s), 1)
        rst[0, 0, at, :] = m1
        rst[0, 1, at, :] = jnp.sum(st * jnp.exp2(mt - m1), axis=0, keepdims=True)
        return carry

    lax.fori_loop(0, 16, fold_cols, 0)
    w.flush(like)
    assert not w.arrivals
    for n in range(7):
        w.open(("r", n), rst, 1 + n)
    for n in range(3):
        w.open(("c1", n), cst, 1 + n)
        w.open(("c2", n), cst, 5 + n)
    for n in range(3):
        w.send(cst.at[0], ("c1", n), col_peers[n])
    lax.fori_loop(0, 8, fold_rows, 0)
    for n in range(7):
        w.send(rst.at[0], ("r", n), row_peers[n])
    i_scale = 240.0 / jnp.maximum(jnp.max(span[0]), 1e-30)
    t_scale = 240.0 / jnp.maximum(jnp.max(span[1]), 1e-30)

    def to_eight(high, low, count, scale, high8, low8):
        def body(b, carry):
            r = pl.ds(pl.multiple_of(b * 64, 64), 64)
            high8[r, :] = (high[r, :].astype(F32) * scale).astype(F8)
            low8[r, :] = (low[r, :].astype(F32) * (256.0 * scale)).astype(F8)
            return carry

        lax.fori_loop(0, count // 64, body, 0)

    for n in range(3):
        w.wait(("c1", n))
    cst[4, 0], cst[4, 1] = merge([(cst[n, 0], cst[n, 1]) for n in range(4)])
    for n, d in enumerate((1, -1, 2)):
        w.send(cst.at[4], ("c2", n), zs[d])
    to_eight(Ih, Il, IMG, i_scale, I8h, I8l)
    to_eight(Th, Tl, TXT, t_scale, T8h, T8l)
    lbuf[0] = jnp.zeros((8, 128), F32)
    lax.fori_loop(0, 16, sum_diagonal, 0)
    for n in range(7):
        w.wait(("r", n))
    m, s = merge([(rst[n, 0], rst[n, 1]) for n in range(8)])
    row_lse = m + jnp.log2(s)
    rst[8, 0] = row_lse + 1.0

    def spread(s, carry):
        r = pl.ds(pl.multiple_of(s * ROWS, ROWS), ROWS)
        v = rst[8, 0, pl.ds(img_block(s), 1), :]
        row_m[r, :] = jnp.broadcast_to(v, (ROWS, 128)).T
        return carry

    lax.fori_loop(0, 8, spread, 0)
    for n in range(3):
        w.wait(("c2", n))
    m, s = merge([(cst[n, 0], cst[n, 1]) for n in range(4, 8)])
    col_lse = m + jnp.log2(s)
    w.flush(like)
    cst[8, 0] = col_lse + 1.0
    share = jnp.sum(row_lse) / 8 + jnp.sum(col_lse) / 16 - 2.0 * jnp.sum(lbuf[0])
    lbuf[0] = jnp.full((8, 128), LN2 * share, F32)
    for n in range(7):
        w.open(("l1", n), lbuf, 1 + n)
    for n in range(3):
        w.open(("l2", n), lbuf, 9 + n)
        w.open(("l3", n), lbuf, 13 + n)
    for n in range(7):
        w.send(lbuf.at[0], ("l1", n), row_peers[n])

    for name, land_a, land_b in (("I", ialand, ibland), ("T", taland, tbland)):
        for p in range(2):
            w.open((name + "A", "P", p), land_a, p)
            for n, d in enumerate((1, -1)):
                w.open((name + "A", "D", p, d), land_a, 2 + 2 * p + n)
        w.open((name + "A", "2"), land_a, 6)
        for q in range(4):
            w.open((name + "B", "Y", q), land_b, q)
        for n, d in enumerate((1, -1)):
            w.open((name + "B", "P", d), land_b, 4, pl.ds(H * n, H))
            w.open((name + "B", "D", d), land_b, 5 + n)
    for q in range(4):
        for p in range(2):
            w.open(("S", q, p), Ib, 2 * q + p)
    def add(dst, srcs, rows, out=None):
        step = 16 if rows % 16 == 0 else 8

        def body(b, carry):
            r = pl.ds(pl.multiple_of(b * step, step), step)
            v = dst[r, :]
            for src in srcs:
                v = v + src[r, :]
            (dst if out is None else out)[r, :] = v
            return carry

        lax.fori_loop(0, rows // step, body, 0)

    summed = set()

    def sums(name, q, p, at, rows):
        if name == "I":
            return L.at[pl.ds((2 * q + p) * ROWS + at, rows), pl.ds(0, E)]
        if (q, p) not in summed:
            summed.add((q, p))
            add(Tb.at[4 * q + 2 * p], [w.wait(("S", q, p))], ROWS)
        return Tb.at[4 * q + 2 * p, pl.ds(at, rows)]

    def back_send(key):
        if key[0] == "S":
            q, p = key[1:]
            w.send(Tb.at[4 * q + 2 * p + 1], key, sib)
            return
        name, kind = key[0][0], key[1]
        way, part = ring[name], key[0]
        if part == name:
            out = img_out if name == "I" else txt_out
            A, B = name + "A", name + "B"
            srcs = [w.wait((A, "D", 0, 1)), w.wait((A, "D", 0, -1)), w.wait((A, "2"))]
            add(sums(name, 0, 0, 0, CUT), srcs, CUT, out.at[lo])
            srcs = [w.wait((B, "Y", 0)), w.wait((B, "D", 1)), w.wait((B, "D", -1))]
            add(sums(name, 0, 0, CUT, REST), srcs, REST, out.at[hi])
        elif part[1] == "A":
            if kind == "P":
                w.send(sums(name, 3, key[2], 0, CUT), key, way[2 * key[2] - 1])
            elif kind == "D":
                p, d = key[2:]
                mine = sums(name, 2 if d == 1 else 1, p, 0, CUT)
                if p == (1 - d) // 2:
                    add(mine, [w.wait((part, "P", p))], CUT)
                w.send(mine, key, way[-d])
            else:
                mine = sums(name, 0, 1, 0, CUT)
                add(mine, [w.wait((part, "D", 1, 1)), w.wait((part, "D", 1, -1))], CUT)
                w.send(mine, key, across[name])
        elif kind == "Y":
            w.send(sums(name, key[2], 1, CUT, REST), key, across[name])
        elif kind == "P":
            d = key[2]
            if (name, "far") not in summed:
                summed.add((name, "far"))
                add(sums(name, 3, 0, CUT, REST), [w.wait((part, "Y", 3))], REST)
            w.send(sums(name, 3, 0, CUT if d == 1 else CUT + H, H), key, way[-d])
        else:
            d = key[2]
            q = 2 if d == 1 else 1
            mine = sums(name, q, 0, CUT, REST)
            add(mine, [w.wait((part, "Y", q))], REST)
            add(mine.at[pl.ds(0 if d == 1 else H, H)], [w.wait((part, "P", d))], H)
            w.send(mine, key, way[-d])

    def put_grad(g, r, c, width):
        first, size = r
        h = g.astype(BF16)
        rows = pl.ds(pl.multiple_of(first, ROWS), size)
        cols = pl.ds(pl.multiple_of(c, ROWS), width)
        below = pl.ds(pl.multiple_of(first + (c // IMG) * IMG, ROWS), size)
        Tl[below, pl.ds(pl.multiple_of(c % IMG, ROWS), width)] = h
        hf = h.astype(F32)
        P8h[rows, cols] = (hf * 256.0).astype(F8)
        P8l[rows, cols] = ((g - hf) * 65536.0).astype(F8)

    def soften(n, carry):
        p = pick(n, [m for kind, m in STEPS if kind == "t"])
        cols = pl.ds(pl.multiple_of(p * 256, 256), 256)
        cl = jnp.concatenate([cst[8, 0, pl.ds(txt_block(2 * p + j), 1), :] for j in range(2)], axis=1)

        def soft(b, inner):
            r = pl.ds(pl.multiple_of(b * ROWS, ROWS), ROWS)
            v = L[r, cols]
            rl = row_m[r, :]
            g = jnp.exp2(v - jnp.concatenate([rl, rl], axis=1)) + jnp.exp2(v - cl)
            put_grad(g, (b * ROWS, ROWS), p * 256, 256)
            return inner

        lax.fori_loop(0, IMG // ROWS, soft, 0)
        for j in range(2):
            s = 2 * p + j
            here, u = on_diagonal(s)

            @pl.when(here)
            def _():
                r = pl.ds(pl.multiple_of(u * ROWS, ROWS), ROWS)
                c = pl.ds(pl.multiple_of(s * ROWS, ROWS), ROWS)
                v = L[r, c]
                g = jnp.exp2(v - row_m[r, :]) + jnp.exp2(v - cl[:, 128 * j : 128 * j + 128]) - eye[...]
                put_grad(g, (u * ROWS, ROWS), s * ROWS, ROWS)

        return carry

    def loss_send(m):
        if m == 1:
            for n in range(7):
                w.wait(("l1", n))
            lbuf[8] = sum(lbuf[n] for n in range(8))
            for n in range(3):
                w.send(lbuf.at[8], ("l2", n), col_peers[n])
        if m == 3:
            for n in range(3):
                w.wait(("l2", n))
            lbuf[12] = sum(lbuf[n] for n in range(8, 12))
            for n, d in enumerate((1, -1, 2)):
                w.send(lbuf.at[12], ("l3", n), zs[d])

    def back_step(n, carry):
        is_text = pick(n, [int(kind == "t") for kind, _ in STEPS])
        arg = pick(n, [a for _, a in STEPS])
        lax.fori_loop(pick(n, SOFT[:-1]), pick(n, SOFT[1:]), soften, 0)

        @pl.when(is_text == 1)
        def _():
            cols = pl.ds(pl.multiple_of(arg * 256, 256), 256)
            below = pl.ds(pl.multiple_of((arg // 4) * IMG, IMG), IMG)
            high = dot(Tl[below, pl.ds(pl.multiple_of((arg % 4) * 256, 256), 256)], Ih[...], 0, 0)
            cross = dot(P8h[:, cols], I8l[...], 0, 0) + dot(P8l[:, cols], I8h[...], 0, 0)
            res = high + (1.0 / (65536.0 * i_scale)) * cross
            Tb[2 * arg] = res[:ROWS]
            Tb[2 * arg + 1] = res[ROWS:]

        @pl.when(is_text == 0)
        def _():
            r = pl.ds(pl.multiple_of(arg * ROWS, ROWS), ROWS)
            r2 = pl.ds(pl.multiple_of(IMG + arg * ROWS, ROWS), ROWS)
            high = dot(Tl[r, 0:IMG], Th[0:IMG, :], 1, 0) + dot(Tl[r2, 0:IMG], Th[IMG:TXT, :], 1, 0)
            cross = dot(P8h[r, :], T8l[...], 1, 0) + dot(P8l[r, :], T8h[...], 1, 0)
            L[r, 0:E] = high + (1.0 / (65536.0 * t_scale)) * cross

        for m in range(len(STEPS)):

            @pl.when(n == m)
            def _():
                for key in RETURN[m]:
                    back_send(key)
                loss_send(m)

        return carry

    lax.fori_loop(0, len(STEPS), back_step, 0)
    for n in range(3):
        w.wait(("l3", n))
    loss_ref[0] = jnp.sum(sum(lbuf[n] for n in range(12, 16))) / (1024 * 2.0 * 16384)
    w.flush(like)
    assert not w.arrivals


def on_device(image_emb, text_emb, logit_scale):
    vm = pltpu.VMEM
    loss, image_grad, text_grad = pl.pallas_call(
        kernel,
        out_shape=(
            jax.ShapeDtypeStruct((1,), F32),
            jax.ShapeDtypeStruct((ROWS, E), F32),
            jax.ShapeDtypeStruct((ROWS, E), F32),
        ),
        in_specs=[
            pl.BlockSpec(memory_space=pltpu.SMEM),
            pl.BlockSpec(memory_space=pl.ANY),
            pl.BlockSpec(memory_space=pl.ANY),
        ],
        out_specs=[pl.BlockSpec(memory_space=pltpu.SMEM)] + [pl.BlockSpec(memory_space=vm)] * 2,
        scratch_shapes=[
            vm((8, ROWS, E), F32),
            vm((16, ROWS, E), F32),
            vm((IMG, E), BF16),
            vm((IMG, E), BF16),
            vm((TXT, E), BF16),
            vm((TXT, E), BF16),
            vm((IMG, TXT), F32),
            vm((IMG, TXT), F8),
            vm((IMG, TXT), F8),
            vm((IMG, E), F8),
            vm((IMG, E), F8),
            vm((TXT, E), F8),
            vm((TXT, E), F8),
            vm((IMG, 128), F32),
            vm((IMG, 128), F32),
            vm((8, TXT), F32),
            vm((8, TXT), F32),
            vm((9, 2, 8, 128), F32),
            vm((9, 2, 16, 128), F32),
            vm((16, 8, 128), F32),
            vm((7, CUT, E), F32),
            vm((7, REST, E), F32),
            vm((7, CUT, E), F32),
            vm((7, REST, E), F32),
            vm((ROWS, ROWS), F32),
            vm((2, 8, E), F32),
            pltpu.SemaphoreType.DMA((56,)),
            pltpu.SemaphoreType.DMA((112,)),
            pltpu.SemaphoreType.DMA((2,)),
        ],
        compiler_params=pltpu.CompilerParams(
            collective_id=0, has_side_effects=True, vmem_limit_bytes=63 * 2**20
        ),
        name="contrastive",
    )(logit_scale.reshape(1), image_emb, text_emb)
    return loss.reshape(()), logit_scale * image_grad, logit_scale * text_grad


def solution(mesh):
    in_specs = (P(("img", "txt"), None), P(("txt", "img"), None), P())
    out_specs = (P(), P(("img", "txt"), None), P(("txt", "img"), None))
    return jax.shard_map(
        on_device, mesh=mesh, in_specs=in_specs, out_specs=out_specs, check_vma=False
    )
```
